32 devices in a mesh: cell: 8 (over y, x, core), spot: 4 (over z).
Axes of the slice: x: 2, y: 2, z: 4, core: 2. Of those that a mesh axis runs over, the one named last changes fastest.
Arguments:
- logits: float32 [11264, 8192], P('cell', 'spot'), may hold values from -10 to 10
- expression: float32 [11264, 2048], P('cell', 'spot'), may hold values from 0.05 to 20
- spatial: float32 [2048, 8192], P('cell', 'spot'), may hold values from 0.05 to 20
- cell_counts: int32 [11264], P('cell'), may hold values from 1 to 12
- spot_density: float32 [8192], P('spot'), may hold values from 0.5 to 8
- slide_id: int32 [8192], P('spot'), may hold values from 0 to 1
- padding: int32 [8192], P('spot'), may hold values 0 or 1
Outputs:
- losses: float32 [2], replicated
- grad_logits: float32 [11264, 8192], P('cell', 'spot')
- grad_expression: float32 [11264, 2048], P('cell', 'spot')
The draws below stay inside these ranges and needn't reach their ends.
All inputs are finite; a program needn't handle non-finite values. No bound on the sum of `padding` on one device may be relied on, other than what follows from the above.
Results may differ from the reference program's by a relative error of at most 0.0003.
Values sent between devices are 32-bit elements; how exact they have to be, the bound alone decides.
A program may use at most 128 MiB of HBM per device.

```python
import math
import jax
import jax.numpy as jnp
from jax import lax

G = 2048
NC = 11264
NS = 8192


def with_ends(entries, own_key, least, largest):
    place = [jax.random.randint(jax.random.fold_in(own_key, axis), (), 0, length) for axis, length in enumerate(entries.shape)]
    main_axis = entries.shape.index(max(entries.shape))
    neighbour = place[:main_axis] + [(place[main_axis] + 1) % entries.shape[main_axis]] + place[main_axis + 1:]
    return entries.at[tuple(place)].set(least).at[tuple(neighbour)].set(largest)


def block_scale(own_key, shape, pieces, smallest, top_value):
    gain, own = 1.0, jax.random.fold_in(own_key, 6)
    for position, parts in pieces:
        draws = jnp.exp(jax.random.uniform(jax.random.fold_in(own, position), (parts,), jnp.float32, smallest / len(pieces), top_value / len(pieces)))
        gain = gain * jnp.repeat(draws, shape[position] // parts).reshape([-1 if axis == position else 1 for axis in range(len(shape))])
    return gain


def centred(key, extent, deviation, limit, shards=(), dtype=jnp.bfloat16):
    entries = deviation * jax.random.normal(key, extent, jnp.float32)
    if shards:
        entries = entries * block_scale(key, extent, shards, -0.22, 0.18)
    return jnp.clip(entries, -limit, limit).astype(dtype)


def setup_inputs(seed: int = 0) -> dict:
    seeds = jax.random.split(jax.random.key(seed), 8)
    return {
        "logits": centred(seeds[0], (NC, NS), 2.0, 10.0, ((0, 8), (1, 4)), jnp.float32),
        "expression": jnp.clip(jnp.exp(math.log(20.0) - 5.9914645 * jax.random.uniform(seeds[1], (NC, G), jnp.float32) ** block_scale(seeds[1], (NC, G), ((0, 8), (1, 4)), -0.2, 0.2)), 0.05, 20.0),
        "spatial": jnp.clip(jnp.exp(math.log(20.0) - 5.9914645 * jax.random.uniform(seeds[2], (G, NS), jnp.float32) ** block_scale(seeds[2], (G, NS), ((0, 8), (1, 4)), -0.2, 0.2)), 0.05, 20.0),
        "cell_counts": with_ends(jax.random.randint(seeds[3], (NC,), 1, 13), jax.random.fold_in(seeds[3], 1), 1, 12).astype(jnp.int32),
        "spot_density": jnp.clip(jnp.exp(math.log(8.0) - 2.7725887 * jax.random.uniform(seeds[4], (NS,), jnp.float32) ** block_scale(seeds[4], (NS,), ((0, 4),), -0.2, 0.2)), 0.5, 8.0),
        "slide_id": with_ends(jax.random.randint(seeds[5], (NS,), 0, 2), jax.random.fold_in(seeds[5], 1), 0, 1).astype(jnp.int32),
        "padding": with_ends((jax.random.randint(seeds[6], (NS,), 0, 8) < 1).astype(jnp.int32), jax.random.fold_in(seeds[6], 1), 0, 1),
    }


epsilon = 1e-06
highest = lax.Precision.HIGHEST

@jax.custom_vjp
def low(v):
    return lax.optimization_barrier(v.astype(jnp.bfloat16)).astype(jnp.float32)

@jax.custom_vjp
def low_back(v):
    return v

def low_keep(v):
    return (low(v), None)

def low_pass(kept, grad):
    return (grad,)

def back_keep(v):
    return (v, None)

def back_low(kept, grad):
    return (low(grad),)
low.defvjp(low_keep, low_pass)
low_back.defvjp(back_keep, back_low)

def reference(logits, expression, spatial, cell_counts, spot_density, slide_id, padding):
    weights = cell_counts.astype(jnp.float32)
    valid = (1 - padding).astype(jnp.float32)
    slide_masks = jnp.stack([valid * (slide_id == 0).astype(jnp.float32), valid * (slide_id == 1).astype(jnp.float32)])
    cell_total, spot_total = logits.shape
    gene_total = expression.shape[1]
    block_width = math.gcd(spot_total, 512)
    block_count = spot_total // block_width

    def forward(logit_matrix, expr_matrix):
        stacked = logit_matrix.reshape(cell_total, block_count, block_width).transpose(1, 0, 2)

        def column_block(logit_block):
            column_peak = lax.optimization_barrier(jnp.max(logit_block, axis=0))
            exponent = jnp.exp(logit_block - column_peak)
            mapping = exponent / lax.optimization_barrier(jnp.sum(exponent, axis=0))
            predicted = lax.dot_general(expr_matrix, mapping, (((0,), (0,)), ((), ())), precision=highest)
            density_block = jnp.dot(weights, mapping, precision=highest)
            return (predicted, density_block)
        predicted_blocks, density_blocks = lax.map(jax.checkpoint(column_block), stacked)
        predicted = predicted_blocks.transpose(1, 0, 2).reshape(gene_total, spot_total)
        density = density_blocks.reshape(spot_total)
        spot_dot = lax.optimization_barrier(jnp.sum(predicted * spatial, axis=0))
        spot_aa = lax.optimization_barrier(jnp.sum(predicted * predicted, axis=0))
        spot_bb = lax.optimization_barrier(jnp.sum(spatial * spatial, axis=0))
        spot_cos = spot_dot / jnp.sqrt((spot_aa + epsilon) * (spot_bb + epsilon))
        masks_t = slide_masks.T
        gene_dot = jnp.dot(predicted * spatial, masks_t, precision=highest)
        gene_aa = jnp.dot(predicted * predicted, masks_t, precision=highest)
        gene_bb = jnp.dot(spatial * spatial, masks_t, precision=highest)
        gene_cos = gene_dot / jnp.sqrt((gene_aa + epsilon) * (gene_bb + epsilon))
        gene_mean = lax.optimization_barrier(jnp.mean(gene_cos, axis=0))
        live_spots = jnp.maximum(lax.optimization_barrier(jnp.sum(slide_masks, axis=1)), 1.0)
        spot_term = jnp.dot(slide_masks, spot_cos, precision=highest) / live_spots
        mass_target = jnp.dot(slide_masks, spot_density, precision=highest)
        mass_pred = jnp.dot(slide_masks, density, precision=highest)
        target_share = spot_density[None, :] / mass_target[:, None]
        pred_share = density[None, :] / mass_pred[:, None]
        divergence = lax.optimization_barrier(jnp.sum(slide_masks * target_share * (jnp.log(target_share) - jnp.log(pred_share)), axis=1))
        return -gene_mean - spot_term + divergence
    losses, pullback = jax.vjp(forward, logits, expression)
    grad_logits, grad_expression = pullback(jnp.ones_like(losses))
    return (losses, grad_logits, grad_expression)
```

```python
import functools

import jax
import jax.numpy as jnp
from jax import lax
from jax.experimental import pallas as pl
from jax.experimental.pallas import tpu as pltpu
from jax.sharding import PartitionSpec as P

epsilon = 1e-06
MESH = pl.DeviceIdType.MESH
F32, BF16 = jnp.float32, jnp.bfloat16
TN = (((0,), (0,)), ((), ()))
NN = (((1,), (0,)), ((), ()))
NT = (((1,), (1,)), ((), ()))


def dot(left, right, dims=NN):
    return lax.dot_general(left, right, dims, preferred_element_type=F32)


def split(v):
    high = v.astype(BF16)
    return high, (v - high.astype(F32)).astype(BF16)


def arrival(z, i, planes, per):
    near = jnp.minimum(z, planes - 1 - z)
    j = jnp.maximum(i - per, 0)
    pair = lax.rem(j, 2 * per)
    t = 1 + lax.div(j, 2 * per)
    both = jnp.where(lax.rem(pair, 2) == 0, z - t, z + t)
    late = jnp.maximum(j - 2 * near * per, 0)
    t = near + 1 + lax.div(late, per)
    one = jnp.where(z < planes - 1 - z, z + t, z - t)
    in_pairs = j < 2 * near * per
    shard = jnp.where(i < per, z, jnp.where(in_pairs, both, one))
    chunk = jnp.where(i < per, i, jnp.where(in_pairs, lax.div(pair, 2), lax.rem(late, per)))
    return shard, chunk


def greet(c, z, cells, planes):
    barrier = pltpu.get_barrier_semaphore()

    def in_plane(step, _):
        pl.semaphore_signal(barrier, inc=1, device_id=(lax.rem(c + step, cells), z), device_id_type=MESH)
        return 0

    def in_column(step, _):
        pl.semaphore_signal(barrier, inc=1, device_id=(c, lax.rem(z + step, planes)), device_id_type=MESH)
        return 0

    lax.fori_loop(1, cells, in_plane, 0)
    lax.fori_loop(1, planes, in_column, 0)
    pl.semaphore_wait(barrier, cells + planes - 2)


def share(src, dst, send, recv, me, count, device):
    def start(step, _):
        other = lax.rem(me + step, count)
        pltpu.make_async_remote_copy(
            src_ref=src, dst_ref=dst.at[me], send_sem=send.at[other], recv_sem=recv.at[me],
            device_id=device(other), device_id_type=MESH,
        ).start()
        return 0

    lax.fori_loop(1, count, start, 0)


def collect(src, dst, send, recv, me, count, device):
    def wait(step, total):
        other = lax.rem(me + step, count)
        copy = pltpu.make_async_remote_copy(
            src_ref=src, dst_ref=dst.at[other], send_sem=send.at[other], recv_sem=recv.at[other],
            device_id=device(other), device_id_type=MESH,
        )
        copy.wait_send()
        copy.wait_recv()
        return total + dst[other]

    return lax.fori_loop(1, count, wait, src[...])


def forward_kernel(
    cfg, logits, expr, spatial, counts, dens, slide, pad,
    gath, ehi_out, elo_out, gp_out, vec_out, loss_out,
    ehi, elo, lbuf, stage, amat, partial, corer, half, chipr, pred, spat,
    tots, totr, acc, spots, spotr, gcol, gst, gstr, vec,
    g_recv, up_send, down_send, l_sem, st_sem, core_send, core_recv, chip_send, chip_recv,
    spat_send, spat_recv, tot_send, tot_recv, spot_send, spot_recv, gst_send, gst_recv, out_sem,
):
    cells, planes, C, S, G, GK, r = (cfg[k] for k in ("cells", "planes", "C", "S", "G", "GK", "r"))
    chips, per, chunks = cells // 2, G // planes // GK, G // GK
    rows, tile = cfg["rows"], cfg["tile"]
    own_genes = G // cells
    c, z = lax.axis_index("cell"), lax.axis_index("spot")
    chip, core = lax.div(c, 2), lax.rem(c, 2)
    sibling = c + 1 - 2 * core
    in_plane = lambda other: (other, z)
    in_column = lambda other: (c, other)

    greet(c, z, cells, planes)

    def z_copy(src, g, to, send):
        return pltpu.make_async_remote_copy(
            src_ref=src, dst_ref=gath.at[g], send_sem=send.at[g], recv_sem=g_recv.at[g],
            device_id=(c, to), device_id_type=MESH,
        )

    up, down = jnp.minimum(z + 1, planes - 1), jnp.maximum(z - 1, 0)

    def send_own(k, _):
        g = z * per + k
        src = expr.at[:, pl.ds(pl.multiple_of(k * GK, 128), GK)]

        @pl.when(z < planes - 1)
        def _():
            z_copy(src, g, up, up_send).start()

        @pl.when(z > 0)
        def _():
            z_copy(src, g, down, down_send).start()

        pltpu.make_async_copy(src, gath.at[g], g_recv.at[g]).start()
        return 0

    lax.fori_loop(0, per, send_own, 0)

    blocks = own_genes // r

    def spat_copy(b):
        place = c * blocks + b
        g, owner = lax.div(place, cells), lax.rem(place, cells)
        src = spatial.at[pl.ds(pl.multiple_of(b * r, 8), r)]
        remote = pltpu.make_async_remote_copy(
            src_ref=src, dst_ref=spat.at[g], send_sem=spat_send.at[b], recv_sem=spat_recv.at[g],
            device_id=(owner, z), device_id_type=MESH,
        )
        local = pltpu.make_async_copy(src, spat.at[g], spat_recv.at[g])
        return owner, remote, local

    def send_spat(b, _):
        owner, remote, local = spat_copy(b)

        @pl.when(owner != c)
        def _():
            remote.start()

        @pl.when(owner == c)
        def _():
            local.start()

        return 0

    lax.fori_loop(0, blocks, send_spat, 0)

    def load(t):
        return pltpu.make_async_copy(
            logits.at[pl.ds(pl.multiple_of(t * rows, rows), rows)], lbuf.at[lax.rem(t, 2)], l_sem.at[lax.rem(t, 2)]
        )

    load(0).start()

    def exps(t, _):
        @pl.when(t + 1 < C // rows)
        def _():
            load(t + 1).start()

        load(t).wait()
        high, low = split(jnp.exp(lbuf[lax.rem(t, 2)]))
        place = pl.ds(pl.multiple_of(t * rows, rows), rows)
        ehi[place, :] = high
        elo[place, :] = low
        return 0

    lax.fori_loop(0, C // rows, exps, 0)
    keep = [pltpu.make_async_copy(ehi, ehi_out, out_sem.at[0]), pltpu.make_async_copy(elo, elo_out, out_sem.at[1])]
    for copy in keep:
        copy.start()

    row = lax.broadcasted_iota(jnp.int32, (16, C), 0)
    weight = jnp.broadcast_to(counts[...].astype(F32), (16, C))
    lhs = jnp.where(row == 0, 1.0, jnp.where(row == 1, weight, 0.0)).astype(BF16)

    def sums(t, _):
        place = pl.ds(pl.multiple_of(t * tile, tile), tile)
        both = dot(lhs, ehi[:, place]) + dot(lhs, elo[:, place])
        tots[:, place] = both[:8]
        return 0

    lax.fori_loop(0, S // tile, sums, 0)
    share(tots, totr, tot_send, tot_recv, c, cells, in_plane)

    valid = (1 - pad[...]).astype(F32)
    mask0 = valid * (slide[...] == 0).astype(F32)
    mask1 = valid * (slide[...] == 1).astype(F32)
    vec[4:5, :] = mask0
    vec[5:6, :] = mask1
    acc[...] = jnp.zeros_like(acc)
    gcol[...] = jnp.zeros_like(gcol)

    def core_copy(g, slot):
        return pltpu.make_async_remote_copy(
            src_ref=partial.at[slot, :, 1 - core], dst_ref=corer.at[g], send_sem=core_send.at[slot],
            recv_sem=core_recv.at[g], device_id=(sibling, z), device_id_type=MESH,
        )

    def chip_copy(g, slot, other):
        return pltpu.make_async_remote_copy(
            src_ref=half.at[slot, other], dst_ref=chipr.at[g, chip], send_sem=chip_send.at[slot, other],
            recv_sem=chip_recv.at[g, chip], device_id=(2 * other + core, z), device_id_type=MESH,
        )

    def chip_wait(g, slot, other):
        return pltpu.make_async_remote_copy(
            src_ref=half.at[slot, chip], dst_ref=chipr.at[g, other], send_sem=chip_send.at[slot, other],
            recv_sem=chip_recv.at[g, other], device_id=(2 * other + core, z), device_id_type=MESH,
        )

    def product(i):
        d, k = arrival(z, i, planes, per)
        g, slot = d * per + k, lax.rem(i, 2)
        z_copy(gath.at[g], g, down, down_send).wait_recv()

        @pl.when((d < z) & (z < planes - 1))
        def _():
            z_copy(gath.at[g], g, up, up_send).start()

        @pl.when((d > z) & (z > 0))
        def _():
            z_copy(gath.at[g], g, down, down_send).start()

        pull = pltpu.make_async_copy(gath.at[g], stage, st_sem)
        pull.start()
        pull.wait()

        @pl.when(i >= 2)
        def _():
            core_copy(g, slot).wait_send()

        def turn(t, _):
            place = pl.ds(pl.multiple_of(t * 128, 128), 128)
            high, low = split(stage[place, :].T)
            amat[:GK, place] = high
            amat[GK:, place] = low
            return 0

        lax.fori_loop(0, C // 128, turn, 0)

        def multiply(t, _):
            place = pl.ds(pl.multiple_of(t * tile, tile), tile)
            both = dot(amat[...], ehi[:, place])
            total = both[:GK] + both[GK:] + dot(amat[:GK, :], elo[:, place])
            partial[slot, :, :, :, place] = total.reshape(chips, 2, r, tile)
            return 0

        lax.fori_loop(0, S // tile, multiply, 0)
        core_copy(g, slot).start()

    def to_chips(i):
        d, k = arrival(z, i, planes, per)
        g, slot = d * per + k, lax.rem(i, 2)
        core_copy(g, slot).wait_recv()

        @pl.when(i >= 2)
        def _():
            def drain(step, _):
                chip_copy(g, slot, lax.rem(chip + step, chips)).wait_send()
                return 0

            lax.fori_loop(1, chips, drain, 0)

        def add(other, _):
            half[slot, other] = partial[slot, other, core] + corer[g, other]

            @pl.when(other != chip)
            def _():
                chip_copy(g, slot, other).start()

            return 0

        lax.fori_loop(0, chips, add, 0)

    def finish(i):
        d, k = arrival(z, i, planes, per)
        g, slot = d * per + k, lax.rem(i, 2)
        pltpu.make_async_copy(spat.at[g], spat.at[g], spat_recv.at[g]).wait()

        def add(step, total):
            other = lax.rem(chip + step, chips)
            chip_wait(g, slot, other).wait_recv()
            return total + chipr[g, other]

        p = lax.fori_loop(1, chips, add, half[slot, chip]) * vec[0:1, :]
        s = spat[g]
        pred[g] = p
        ps, pp, ss = p * s, p * p, s * s
        acc[0] += ps
        acc[1] += pp
        acc[2] += ss
        lane = lax.broadcasted_iota(jnp.int32, (r, 128), 1)
        cols = jnp.zeros((r, 128), F32)
        for n, v in enumerate((ps, pp, ss)):
            for m in range(2):
                one = jnp.sum(v * vec[4 + m : 5 + m, :], axis=1, keepdims=True)
                cols = jnp.where(lane == 2 * n + m, one, cols)
        gcol[pl.ds(pl.multiple_of(g * r, 8), r), :] = cols

    def step(i, _):
        @pl.when(i < chunks)
        def _():
            product(i)

        @pl.when(i == 1)
        def _():
            total = collect(tots, totr, tot_send, tot_recv, c, cells, in_plane)
            vec[0:1, :] = 1.0 / total[0:1, :]
            vec[1:2, :] = total[1:2, :] / total[0:1, :]

        @pl.when((i >= 1) & (i <= chunks))
        def _():
            to_chips(i - 1)

        @pl.when(i >= 2)
        def _():
            finish(i - 2)

        return 0

    lax.fori_loop(0, chunks + 2, step, 0)

    spots[...] = jnp.zeros_like(spots)
    for n in range(3):
        spots[n : n + 1, :] = jnp.sum(acc[n], axis=0, keepdims=True)
    share(spots, spotr, spot_send, spot_recv, c, cells, in_plane)
    gst[...] = jnp.zeros_like(gst)
    gst[0:8, :] = gcol[...].T[0:8, :]
    density = vec[1:2, :]
    target = dens[...]
    lane = lax.broadcasted_iota(jnp.int32, (1, gst.shape[1]), 1)
    logs = target * jnp.log(target), target * jnp.log(density)
    for n, v in enumerate((jnp.ones_like(target), target, density, *logs)):
        line = jnp.zeros((1, gst.shape[1]), F32)
        for m in range(2):
            one = jnp.sum(v * vec[4 + m : 5 + m, :], axis=1, keepdims=True)
            line = jnp.where(lane == m, one, line)
        gst[8 + n : 9 + n, :] = line
    share(gst, gstr, gst_send, gst_recv, z, planes, in_column)

    genes = collect(gst, gstr, gst_send, gst_recv, z, planes, in_column)
    dot_g, aa_g, bb_g = ([genes[2 * n + m : 2 * n + m + 1, :] for m in range(2)] for n in range(3))
    slides = [[genes[8 + n : 9 + n, m : m + 1] for m in range(2)] for n in range(5)]
    lines, cos_sums, own_losses = [], [], []
    for m in range(2):
        norm = jnp.sqrt((aa_g[m] + epsilon) * (bb_g[m] + epsilon))
        cos = dot_g[m] / norm
        lines += [-1.0 / (norm * G), cos / ((aa_g[m] + epsilon) * G)]
        cos_sums.append(jnp.sum(cos, axis=1, keepdims=True))
    lines.append(jnp.zeros((124, gst.shape[1]), F32))
    gcol[...] = jnp.concatenate(lines, axis=0).T
    live = [jnp.maximum(v, 1.0) for v in slides[0]]
    mass_target, mass_pred = slides[1], slides[2]
    divergence = [
        (slides[3][m] - slides[4][m]) / mass_target[m] - jnp.log(mass_target[m]) + jnp.log(mass_pred[m])
        for m in range(2)
    ]
    mask0, mask1 = vec[4:5, :], vec[5:6, :]
    grad_density = (
        mask0 / mass_pred[0] + mask1 / mass_pred[1]
        - dens[...] * (mask0 / mass_target[0] + mask1 / mass_target[1]) / vec[1:2, :]
    )
    spot_weight = mask0 / live[0] + mask1 / live[1]

    spot = collect(spots, spotr, spot_send, spot_recv, c, cells, in_plane)
    norm = jnp.sqrt((spot[1:2, :] + epsilon) * (spot[2:3, :] + epsilon))
    spot_cos = spot[0:1, :] / norm
    inverse = vec[0:1, :]
    vec[2:3, :] = -spot_weight / norm
    vec[3:4, :] = spot_weight * spot_cos / (spot[1:2, :] + epsilon)
    vec[6:7, :] = grad_density * inverse
    vec[7:8, :] = vec[1:2, :] * grad_density * inverse
    acc[0] = jnp.zeros((r, S), F32)

    def gradient(g, _):
        columns = gcol[pl.ds(pl.multiple_of(g * r, 8), r), :]
        by_spatial = vec[4:5, :] * columns[:, 0:1] + vec[5:6, :] * columns[:, 2:3] + vec[2:3, :]
        by_pred = vec[4:5, :] * columns[:, 1:2] + vec[5:6, :] * columns[:, 3:4] + vec[3:4, :]
        p = pred[g]
        value = (spat[g] * by_spatial + p * by_pred) * vec[0:1, :]
        acc[0] += p * value
        pred[g] = value
        return 0

    lax.fori_loop(0, chunks, gradient, 0)
    copy = pltpu.make_async_copy(pred, gp_out, out_sem.at[2])
    copy.start()
    vec_out[...] = jnp.zeros_like(vec_out)
    vec_out[0:1, :] = jnp.sum(acc[0], axis=0, keepdims=True)
    vec_out[8:9, :] = vec[6:7, :]
    vec_out[9:10, :] = vec[7:8, :]
    lane = lax.broadcasted_iota(jnp.int32, (1, 128), 1)
    spot_sums = [jnp.sum(vec[4 + m : 5 + m, :] * spot_cos, axis=1, keepdims=True) for m in range(2)]
    loss_out[...] = jnp.zeros_like(loss_out)
    for n, v in enumerate((cos_sums, spot_sums, live, divergence)):
        loss_out[n : n + 1, :] = jnp.where(lane == 0, v[0], jnp.where(lane == 1, v[1], 0.0))

    copy.wait()
    for copy in keep:
        copy.wait()

    def drain_z(g, _):
        d = lax.div(g, per)

        @pl.when((d <= z) & (z < planes - 1))
        def _():
            z_copy(gath.at[g], g, up, up_send).wait_send()

        @pl.when((d >= z) & (z > 0))
        def _():
            z_copy(gath.at[g], g, down, down_send).wait_send()

        return 0

    lax.fori_loop(0, chunks, drain_z, 0)

    def drain_spat(b, _):
        owner, remote, _ = spat_copy(b)

        @pl.when(owner != c)
        def _():
            remote.wait_send()

        return 0

    lax.fori_loop(0, blocks, drain_spat, 0)
    for slot in range(2):
        core_copy(0, slot).wait_send()

        def drain(step, _):
            chip_copy(0, slot, lax.rem(chip + step, chips)).wait_send()
            return 0

        lax.fori_loop(1, chips, drain, 0)


ANY = pl.BlockSpec(memory_space=pl.ANY)
VMEM = pl.BlockSpec(memory_space=pltpu.VMEM)


def forward(cfg, logits, expression, spatial, counts, dens, slide, pad):
    cells, planes, C, S, G, GK, r = (cfg[k] for k in ("cells", "planes", "C", "S", "G", "GK", "r"))
    chips, per, chunks = cells // 2, G // planes // GK, G // GK
    rows = cfg["rows"]
    wide = max(G // cells, 128)
    blocks = G // cells // r
    sem = pltpu.SemaphoreType.DMA
    scratch = [
        pltpu.VMEM((C, S), BF16), pltpu.VMEM((C, S), BF16), pltpu.VMEM((2, rows, S), F32),
        pltpu.VMEM((C, GK), F32), pltpu.VMEM((2 * GK, C), BF16),
        pltpu.VMEM((2, chips, 2, r, S), F32), pltpu.VMEM((chunks, chips, r, S), F32),
        pltpu.VMEM((2, chips, r, S), F32), pltpu.VMEM((chunks, chips, r, S), F32),
        pltpu.VMEM((chunks, r, S), F32), pltpu.VMEM((chunks, r, S), F32),
        pltpu.VMEM((8, S), F32), pltpu.VMEM((cells, 8, S), F32), pltpu.VMEM((3, r, S), F32),
        pltpu.VMEM((8, S), F32), pltpu.VMEM((cells, 8, S), F32), pltpu.VMEM((wide, 128), F32),
        pltpu.VMEM((16, wide), F32), pltpu.VMEM((planes, 16, wide), F32), pltpu.VMEM((8, S), F32),
        sem((chunks,)), sem((chunks,)), sem((chunks,)), sem((2,)), sem,
        sem((2,)), sem((chunks,)), sem((2, chips)), sem((chunks, chips)),
        sem((blocks,)), sem((chunks,)), sem((cells,)), sem((cells,)), sem((cells,)), sem((cells,)),
        sem((planes,)), sem((planes,)), sem((3,)),
    ]
    flops = 6 * C * S * G
    return pl.pallas_call(
        functools.partial(forward_kernel, cfg),
        out_shape=(
            jax.ShapeDtypeStruct((chunks, C, GK), F32),
            jax.ShapeDtypeStruct((C, S), BF16),
            jax.ShapeDtypeStruct((C, S), BF16),
            jax.ShapeDtypeStruct((chunks, r, S), F32),
            jax.ShapeDtypeStruct((16, S), F32),
            jax.ShapeDtypeStruct((8, 128), F32),
        ),
        in_specs=[ANY, ANY, ANY, VMEM, VMEM, VMEM, VMEM],
        out_specs=(ANY, ANY, ANY, ANY, VMEM, VMEM),
        scratch_shapes=scratch,
        compiler_params=pltpu.CompilerParams(
            collective_id=0, has_side_effects=True, vmem_limit_bytes=56 * 2**20
        ),
        cost_estimate=pl.CostEstimate(flops=flops, bytes_accessed=8 * C * S, transcendentals=C * S),
        name="forward",
    )(logits, expression, spatial, counts, dens, slide, pad)


def local(cells, planes, logits, expression, spatial, cell_counts, spot_density, slide_id, padding):
    C, S = logits.shape
    G = expression.shape[1] * planes
    GK = max(128, 8 * cells)
    cfg = dict(cells=cells, planes=planes, C=C, S=S, G=G, GK=GK, r=GK // cells, rows=128, tile=512)
    gath, ehi, elo, gp, vec, loss = forward(
        cfg, logits, expression, spatial, cell_counts[None, :], spot_density[None, :],
        slide_id[None, :], padding[None, :],
    )
    high = lax.Precision.HIGH
    full = lax.all_gather(gp, "cell", axis=1).reshape(G, S)
    gathered = gath.transpose(1, 0, 2).reshape(C, G)
    exponent = ehi.astype(F32) + elo.astype(F32)
    column = lax.psum(vec[0], "cell") + vec[9]
    cos_sum = lax.psum(loss[0, :2], "cell")
    spot_sum = lax.psum(loss[1, :2], "spot")
    losses = -cos_sum / G - spot_sum / loss[2, :2] + loss[3, :2]
    grad_map = jnp.dot(gathered, full, precision=high) + cell_counts.astype(F32)[:, None] * vec[8][None, :]
    grad_logits = exponent * (grad_map - column)
    partial_grad = lax.dot_general(exponent, full, NT, precision=high, preferred_element_type=F32)
    grad_expression = lax.psum_scatter(partial_grad, "spot", scatter_dimension=1, tiled=True)
    return (losses, grad_logits, grad_expression)


def solution(mesh):
    cells, planes = mesh.shape["cell"], mesh.shape["spot"]
    in_specs = (
        P("cell", "spot"), P("cell", "spot"), P("cell", "spot"), P("cell"), P("spot"), P("spot"), P("spot"),
    )
    out_specs = (P(), P("cell", "spot"), P("cell", "spot"))
    return jax.shard_map(
        functools.partial(local, cells, planes), mesh=mesh, in_specs=in_specs, out_specs=out_specs, check_vma=False
    )
```

```python
import functools

import jax
import jax.numpy as jnp
from jax import lax
from jax.experimental import pallas as pl
from jax.experimental.pallas import tpu as pltpu
from jax.sharding import PartitionSpec as P

epsilon = 1e-06
MESH = pl.DeviceIdType.MESH
F32, BF16 = jnp.float32, jnp.bfloat16
TN = (((0,), (0,)), ((), ()))
NN = (((1,), (0,)), ((), ()))
NT = (((1,), (1,)), ((), ()))


def dot(left, right, dims=NN):
    return lax.dot_general(left, right, dims, preferred_element_type=F32)


def split(v):
    high = v.astype(BF16)
    return high, (v - high.astype(F32)).astype(BF16)


def arrival(z, i, planes, per):
    near = jnp.minimum(z, planes - 1 - z)
    j = jnp.maximum(i - per, 0)
    pair = lax.rem(j, 2 * per)
    t = 1 + lax.div(j, 2 * per)
    both = jnp.where(lax.rem(pair, 2) == 0, z - t, z + t)
    late = jnp.maximum(j - 2 * near * per, 0)
    t = near + 1 + lax.div(late, per)
    one = jnp.where(z < planes - 1 - z, z + t, z - t)
    in_pairs = j < 2 * near * per
    shard = jnp.where(i < per, z, jnp.where(in_pairs, both, one))
    chunk = jnp.where(i < per, i, jnp.where(in_pairs, lax.div(pair, 2), lax.rem(late, per)))
    return shard, chunk


def greet(c, z, cells, planes):
    barrier = pltpu.get_barrier_semaphore()

    def in_plane(step, _):
        pl.semaphore_signal(barrier, inc=1, device_id=(lax.rem(c + step, cells), z), device_id_type=MESH)
        return 0

    def in_column(step, _):
        pl.semaphore_signal(barrier, inc=1, device_id=(c, lax.rem(z + step, planes)), device_id_type=MESH)
        return 0

    lax.fori_loop(1, cells, in_plane, 0)
    lax.fori_loop(1, planes, in_column, 0)
    pl.semaphore_wait(barrier, cells + planes - 2)


def share(src, dst, send, recv, me, count, device):
    def start(step, _):
        other = lax.rem(me + step, count)
        pltpu.make_async_remote_copy(
            src_ref=src, dst_ref=dst.at[me], send_sem=send.at[other], recv_sem=recv.at[me],
            device_id=device(other), device_id_type=MESH,
        ).start()
        return 0

    lax.fori_loop(1, count, start, 0)


def collect(src, dst, send, recv, me, count, device):
    def wait(step, total):
        other = lax.rem(me + step, count)
        copy = pltpu.make_async_remote_copy(
            src_ref=src, dst_ref=dst.at[other], send_sem=send.at[other], recv_sem=recv.at[other],
            device_id=device(other), device_id_type=MESH,
        )
        copy.wait_send()
        copy.wait_recv()
        return total + dst[other]

    return lax.fori_loop(1, count, wait, src[...])


def forward_kernel(
    cfg, logits, expr, spatial, counts, dens, slide, pad,
    gath, ehi_out, elo_out, gp_out, vec_out, loss_out,
    ehi, elo, lbuf, stage, amat, partial, corer, half, chipr, pred, spat,
    tots, totr, acc, spots, spotr, gcol, gst, gstr, vec,
    g_recv, up_send, down_send, l_sem, st_sem, core_send, core_recv, chip_send, chip_recv,
    spat_send, spat_recv, tot_send, tot_recv, spot_send, spot_recv, gst_send, gst_recv, out_sem,
):
    cells, planes, C, S, G, GK, r = (cfg[k] for k in ("cells", "planes", "C", "S", "G", "GK", "r"))
    chips, per, chunks = cells // 2, G // planes // GK, G // GK
    rows, tile = cfg["rows"], cfg["tile"]
    own_genes = G // cells
    c, z = lax.axis_index("cell"), lax.axis_index("spot")
    chip, core = lax.div(c, 2), lax.rem(c, 2)
    sibling = c + 1 - 2 * core
    in_plane = lambda other: (other, z)
    in_column = lambda other: (c, other)

    greet(c, z, cells, planes)

    def z_copy(src, g, to, send):
        return pltpu.make_async_remote_copy(
            src_ref=src, dst_ref=gath.at[g], send_sem=send.at[g], recv_sem=g_recv.at[g],
            device_id=(c, to), device_id_type=MESH,
        )

    up, down = jnp.minimum(z + 1, planes - 1), jnp.maximum(z - 1, 0)

    def send_own(k, _):
        g = z * per + k
        src = expr.at[:, pl.ds(pl.multiple_of(k * GK, 128), GK)]

        @pl.when(z < planes - 1)
        def _():
            z_copy(src, g, up, up_send).start()

        @pl.when(z > 0)
        def _():
            z_copy(src, g, down, down_send).start()

        pltpu.make_async_copy(src, gath.at[g], g_recv.at[g]).start()
        return 0

    lax.fori_loop(0, per, send_own, 0)

    blocks = own_genes // r

    def spat_copy(b):
        place = c * blocks + b
        g, owner = lax.div(place, cells), lax.rem(place, cells)
        src = spatial.at[pl.ds(pl.multiple_of(b * r, 8), r)]
        remote = pltpu.make_async_remote_copy(
            src_ref=src, dst_ref=spat.at[g], send_sem=spat_send.at[b], recv_sem=spat_recv.at[g],
            device_id=(owner, z), device_id_type=MESH,
        )
        local = pltpu.make_async_copy(src, spat.at[g], spat_recv.at[g])
        return owner, remote, local

    def send_spat(b, _):
        owner, remote, local = spat_copy(b)

        @pl.when(owner != c)
        def _():
            remote.start()

        @pl.when(owner == c)
        def _():
            local.start()

        return 0

    lax.fori_loop(0, blocks, send_spat, 0)

    def load(t):
        return pltpu.make_async_copy(
            logits.at[pl.ds(pl.multiple_of(t * rows, rows), rows)], lbuf.at[lax.rem(t, 2)], l_sem.at[lax.rem(t, 2)]
        )

    load(0).start()

    def exps(t, _):
        @pl.when(t + 1 < C // rows)
        def _():
            load(t + 1).start()

        load(t).wait()
        high, low = split(jnp.exp(lbuf[lax.rem(t, 2)]))
        place = pl.ds(pl.multiple_of(t * rows, rows), rows)
        ehi[place, :] = high
        elo[place, :] = low
        return 0

    lax.fori_loop(0, C // rows, exps, 0)
    keep = [pltpu.make_async_copy(ehi, ehi_out, out_sem.at[0]), pltpu.make_async_copy(elo, elo_out, out_sem.at[1])]
    for copy in keep:
        copy.start()

    row = lax.broadcasted_iota(jnp.int32, (16, C), 0)
    weight = jnp.broadcast_to(counts[...].astype(F32), (16, C))
    lhs = jnp.where(row == 0, 1.0, jnp.where(row == 1, weight, 0.0)).astype(BF16)

    def sums(t, _):
        place = pl.ds(pl.multiple_of(t * tile, tile), tile)
        both = dot(lhs, ehi[:, place]) + dot(lhs, elo[:, place])
        tots[:, place] = both[:8]
        return 0

    lax.fori_loop(0, S // tile, sums, 0)
    share(tots, totr, tot_send, tot_recv, c, cells, in_plane)

    valid = (1 - pad[...]).astype(F32)
    mask0 = valid * (slide[...] == 0).astype(F32)
    mask1 = valid * (slide[...] == 1).astype(F32)
    vec[4:5, :] = mask0
    vec[5:6, :] = mask1
    acc[...] = jnp.zeros_like(acc)
    gcol[...] = jnp.zeros_like(gcol)

    def core_copy(g, slot):
        return pltpu.make_async_remote_copy(
            src_ref=partial.at[slot, :, 1 - core], dst_ref=corer.at[g], send_sem=core_send.at[slot],
            recv_sem=core_recv.at[g], device_id=(sibling, z), device_id_type=MESH,
        )

    def chip_copy(g, slot, other):
        return pltpu.make_async_remote_copy(
            src_ref=half.at[slot, other], dst_ref=chipr.at[g, chip], send_sem=chip_send.at[slot, other],
            recv_sem=chip_recv.at[g, chip], device_id=(2 * other + core, z), device_id_type=MESH,
        )

    def chip_wait(g, slot, other):
        return pltpu.make_async_remote_copy(
            src_ref=half.at[slot, chip], dst_ref=chipr.at[g, other], send_sem=chip_send.at[slot, other],
            recv_sem=chip_recv.at[g, other], device_id=(2 * other + core, z), device_id_type=MESH,
        )

    def product(i):
        d, k = arrival(z, i, planes, per)
        g, slot = d * per + k, lax.rem(i, 2)
        z_copy(gath.at[g], g, down, down_send).wait_recv()

        @pl.when((d < z) & (z < planes - 1))
        def _():
            z_copy(gath.at[g], g, up, up_send).start()

        @pl.when((d > z) & (z > 0))
        def _():
            z_copy(gath.at[g], g, down, down_send).start()

        pull = pltpu.make_async_copy(gath.at[g], stage, st_sem)
        pull.start()
        pull.wait()

        @pl.when(i >= 2)
        def _():
            core_copy(g, slot).wait_send()

        def turn(t, _):
            place = pl.ds(pl.multiple_of(t * 128, 128), 128)
            high, low = split(stage[place, :].T)
            amat[:GK, place] = high
            amat[GK:, place] = low
            return 0

        lax.fori_loop(0, C // 128, turn, 0)

        def multiply(t, _):
            place = pl.ds(pl.multiple_of(t * tile, tile), tile)
            both = dot(amat[...], ehi[:, place])
            total = both[:GK] + both[GK:] + dot(amat[:GK, :], elo[:, place])
            partial[slot, :, :, :, place] = total.reshape(chips, 2, r, tile)
            return 0

        lax.fori_loop(0, S // tile, multiply, 0)
        core_copy(g, slot).start()

    def to_chips(i):
        d, k = arrival(z, i, planes, per)
        g, slot = d * per + k, lax.rem(i, 2)
        core_copy(g, slot).wait_recv()

        @pl.when(i >= 2)
        def _():
            def drain(step, _):
                chip_copy(g, slot, lax.rem(chip + step, chips)).wait_send()
                return 0

            lax.fori_loop(1, chips, drain, 0)

        def add(other, _):
            half[slot, other] = partial[slot, other, core] + corer[g, other]

            @pl.when(other != chip)
            def _():
                chip_copy(g, slot, other).start()

            return 0

        lax.fori_loop(0, chips, add, 0)

    def finish(i):
        d, k = arrival(z, i, planes, per)
        g, slot = d * per + k, lax.rem(i, 2)
        pltpu.make_async_copy(spat.at[g], spat.at[g], spat_recv.at[g]).wait()

        def add(step, total):
            other = lax.rem(chip + step, chips)
            chip_wait(g, slot, other).wait_recv()
            return total + chipr[g, other]

        p = lax.fori_loop(1, chips, add, half[slot, chip]) * vec[0:1, :]
        s = spat[g]
        pred[g] = p
        ps, pp, ss = p * s, p * p, s * s
        acc[0] += ps
        acc[1] += pp
        acc[2] += ss
        lane = lax.broadcasted_iota(jnp.int32, (r, 128), 1)
        cols = jnp.zeros((r, 128), F32)
        for n, v in enumerate((ps, pp, ss)):
            for m in range(2):
                one = jnp.sum(v * vec[4 + m : 5 + m, :], axis=1, keepdims=True)
                cols = jnp.where(lane == 2 * n + m, one, cols)
        gcol[pl.ds(pl.multiple_of(g * r, 8), r), :] = cols

    def step(i, _):
        @pl.when(i < chunks)
        def _():
            product(i)

        @pl.when(i == 1)
        def _():
            total = collect(tots, totr, tot_send, tot_recv, c, cells, in_plane)
            vec[0:1, :] = 1.0 / total[0:1, :]
            vec[1:2, :] = total[1:2, :] / total[0:1, :]

        @pl.when((i >= 1) & (i <= chunks))
        def _():
            to_chips(i - 1)

        @pl.when(i >= 2)
        def _():
            finish(i - 2)

        return 0

    lax.fori_loop(0, chunks + 2, step, 0)

    spots[...] = jnp.zeros_like(spots)
    for n in range(3):
        spots[n : n + 1, :] = jnp.sum(acc[n], axis=0, keepdims=True)
    share(spots, spotr, spot_send, spot_recv, c, cells, in_plane)
    gst[...] = jnp.zeros_like(gst)
    gst[0:8, :] = gcol[...].T[0:8, :]
    density = vec[1:2, :]
    target = dens[...]
    lane = lax.broadcasted_iota(jnp.int32, (1, gst.shape[1]), 1)
    logs = target * jnp.log(target), target * jnp.log(density)
    for n, v in enumerate((jnp.ones_like(target), target, density, *logs)):
        line = jnp.zeros((1, gst.shape[1]), F32)
        for m in range(2):
            one = jnp.sum(v * vec[4 + m : 5 + m, :], axis=1, keepdims=True)
            line = jnp.where(lane == m, one, line)
        gst[8 + n : 9 + n, :] = line
    share(gst, gstr, gst_send, gst_recv, z, planes, in_column)

    genes = collect(gst, gstr, gst_send, gst_recv, z, planes, in_column)
    dot_g, aa_g, bb_g = ([genes[2 * n + m : 2 * n + m + 1, :] for m in range(2)] for n in range(3))
    slides = [[genes[8 + n : 9 + n, m : m + 1] for m in range(2)] for n in range(5)]
    lines, cos_sums, own_losses = [], [], []
    for m in range(2):
        norm = jnp.sqrt((aa_g[m] + epsilon) * (bb_g[m] + epsilon))
        cos = dot_g[m] / norm
        lines += [-1.0 / (norm * G), cos / ((aa_g[m] + epsilon) * G)]
        cos_sums.append(jnp.sum(cos, axis=1, keepdims=True))
    lines.append(jnp.zeros((124, gst.shape[1]), F32))
    gcol[...] = jnp.concatenate(lines, axis=0).T
    live = [jnp.maximum(v, 1.0) for v in slides[0]]
    mass_target, mass_pred = slides[1], slides[2]
    divergence = [
        (slides[3][m] - slides[4][m]) / mass_target[m] - jnp.log(mass_target[m]) + jnp.log(mass_pred[m])
        for m in range(2)
    ]
    mask0, mask1 = vec[4:5, :], vec[5:6, :]
    grad_density = (
        mask0 / mass_pred[0] + mask1 / mass_pred[1]
        - dens[...] * (mask0 / mass_target[0] + mask1 / mass_target[1]) / vec[1:2, :]
    )
    spot_weight = mask0 / live[0] + mask1 / live[1]

    spot = collect(spots, spotr, spot_send, spot_recv, c, cells, in_plane)
    norm = jnp.sqrt((spot[1:2, :] + epsilon) * (spot[2:3, :] + epsilon))
    spot_cos = spot[0:1, :] / norm
    inverse = vec[0:1, :]
    vec[2:3, :] = -spot_weight / norm
    vec[3:4, :] = spot_weight * spot_cos / (spot[1:2, :] + epsilon)
    vec[6:7, :] = grad_density * inverse
    vec[7:8, :] = vec[1:2, :] * grad_density * inverse
    acc[0] = jnp.zeros((r, S), F32)

    def gradient(g, _):
        columns = gcol[pl.ds(pl.multiple_of(g * r, 8), r), :]
        by_spatial = vec[4:5, :] * columns[:, 0:1] + vec[5:6, :] * columns[:, 2:3] + vec[2:3, :]
        by_pred = vec[4:5, :] * columns[:, 1:2] + vec[5:6, :] * columns[:, 3:4] + vec[3:4, :]
        p = pred[g]
        value = (spat[g] * by_spatial + p * by_pred) * vec[0:1, :]
        acc[0] += p * value
        pred[g] = value
        return 0

    lax.fori_loop(0, chunks, gradient, 0)
    copy = pltpu.make_async_copy(pred, gp_out, out_sem.at[2])
    copy.start()
    vec_out[...] = jnp.zeros_like(vec_out)
    vec_out[0:1, :] = jnp.sum(acc[0], axis=0, keepdims=True)
    vec_out[8:9, :] = vec[6:7, :]
    vec_out[9:10, :] = vec[7:8, :]
    lane = lax.broadcasted_iota(jnp.int32, (1, 128), 1)
    vec_out[1:2, 0:128] = jnp.where(lane == 0, cos_sums[0], jnp.where(lane == 1, cos_sums[1], 0.0))
    spot_sums = [jnp.sum(vec[4 + m : 5 + m, :] * spot_cos, axis=1, keepdims=True) for m in range(2)]
    loss_out[...] = jnp.zeros_like(loss_out)
    for n, v in enumerate((spot_sums, live, divergence)):
        loss_out[n : n + 1, :] = jnp.where(lane == 0, v[0], jnp.where(lane == 1, v[1], 0.0))

    copy.wait()
    for copy in keep:
        copy.wait()

    def drain_z(g, _):
        d = lax.div(g, per)

        @pl.when((d <= z) & (z < planes - 1))
        def _():
            z_copy(gath.at[g], g, up, up_send).wait_send()

        @pl.when((d >= z) & (z > 0))
        def _():
            z_copy(gath.at[g], g, down, down_send).wait_send()

        return 0

    lax.fori_loop(0, chunks, drain_z, 0)

    def drain_spat(b, _):
        owner, remote, _ = spat_copy(b)

        @pl.when(owner != c)
        def _():
            remote.wait_send()

        return 0

    lax.fori_loop(0, blocks, drain_spat, 0)
    for slot in range(2):
        core_copy(0, slot).wait_send()

        def drain(step, _):
            chip_copy(0, slot, lax.rem(chip + step, chips)).wait_send()
            return 0

        lax.fori_loop(1, chips, drain, 0)


ANY = pl.BlockSpec(memory_space=pl.ANY)
VMEM = pl.BlockSpec(memory_space=pltpu.VMEM)


def forward(cfg, logits, expression, spatial, counts, dens, slide, pad):
    cells, planes, C, S, G, GK, r = (cfg[k] for k in ("cells", "planes", "C", "S", "G", "GK", "r"))
    chips, per, chunks = cells // 2, G // planes // GK, G // GK
    rows = cfg["rows"]
    wide = max(G // cells, 128)
    blocks = G // cells // r
    sem = pltpu.SemaphoreType.DMA
    scratch = [
        pltpu.VMEM((C, S), BF16), pltpu.VMEM((C, S), BF16), pltpu.VMEM((2, rows, S), F32),
        pltpu.VMEM((C, GK), F32), pltpu.VMEM((2 * GK, C), BF16),
        pltpu.VMEM((2, chips, 2, r, S), F32), pltpu.VMEM((chunks, chips, r, S), F32),
        pltpu.VMEM((2, chips, r, S), F32), pltpu.VMEM((chunks, chips, r, S), F32),
        pltpu.VMEM((chunks, r, S), F32), pltpu.VMEM((chunks, r, S), F32),
        pltpu.VMEM((8, S), F32), pltpu.VMEM((cells, 8, S), F32), pltpu.VMEM((3, r, S), F32),
        pltpu.VMEM((8, S), F32), pltpu.VMEM((cells, 8, S), F32), pltpu.VMEM((wide, 128), F32),
        pltpu.VMEM((16, wide), F32), pltpu.VMEM((planes, 16, wide), F32), pltpu.VMEM((8, S), F32),
        sem((chunks,)), sem((chunks,)), sem((chunks,)), sem((2,)), sem,
        sem((2,)), sem((chunks,)), sem((2, chips)), sem((chunks, chips)),
        sem((blocks,)), sem((chunks,)), sem((cells,)), sem((cells,)), sem((cells,)), sem((cells,)),
        sem((planes,)), sem((planes,)), sem((3,)),
    ]
    flops = 6 * C * S * G
    return pl.pallas_call(
        functools.partial(forward_kernel, cfg),
        out_shape=(
            jax.ShapeDtypeStruct((chunks, C, GK), F32),
            jax.ShapeDtypeStruct((C, S), BF16),
            jax.ShapeDtypeStruct((C, S), BF16),
            jax.ShapeDtypeStruct((chunks, r, S), F32),
            jax.ShapeDtypeStruct((16, S), F32),
            jax.ShapeDtypeStruct((8, 128), F32),
        ),
        in_specs=[ANY, ANY, ANY, VMEM, VMEM, VMEM, VMEM],
        out_specs=(ANY, ANY, ANY, ANY, VMEM, VMEM),
        scratch_shapes=scratch,
        compiler_params=pltpu.CompilerParams(
            collective_id=0, has_side_effects=True, vmem_limit_bytes=56 * 2**20
        ),
        cost_estimate=pl.CostEstimate(flops=flops, bytes_accessed=8 * C * S, transcendentals=C * S),
        name="forward",
    )(logits, expression, spatial, counts, dens, slide, pad)


def backward_kernel(
    cfg, gp, gath, ehi, elo, vec, loss, weight,
    grad_logits, grad_expr, losses, gpland, below, above,
    e2, x2, gph, gpl, gstage, xstage, zst, zsend, outst, cols, vecr, lossr,
    e_sem, own_sem, gp_recv, own_send, fwd_send, gs_sem, xs_sem, b_recv, a_recv, zs_sem, zst_sem, out_sem,
    vec_send, vec_recv, loss_send, loss_recv,
):
    cells, planes, C, S, G, GK, r = (cfg[k] for k in ("cells", "planes", "C", "S", "G", "GK", "r"))
    chips, per, chunks = cells // 2, G // planes // GK, G // GK
    parts, tile, slots = cfg["parts"], cfg["tile"], cfg["slots"]
    rows, tiles = C // parts, S // tile
    c, z = lax.axis_index("cell"), lax.axis_index("spot")
    chip, core = lax.div(c, 2), lax.rem(c, 2)
    sibling = c + 1 - 2 * core
    in_plane = lambda other: (other, z)
    in_column = lambda other: (c, other)
    at_end = (z == 0) | (z == planes - 1)

    def order(i):
        d, k = arrival(z, chunks - 1 - i, planes, per)
        return d, k, d * per + k

    def e_copy(t, _=None):
        place = pl.ds(pl.multiple_of(t * rows, 16), rows)
        return (
            pltpu.make_async_copy(ehi.at[place], e2.at[t, pl.ds(0, rows)], e_sem.at[0, t]),
            pltpu.make_async_copy(elo.at[place], e2.at[t, pl.ds(rows, rows)], e_sem.at[1, t]),
        )

    greet(c, z, cells, planes)

    def own_copy(g, other):
        to = jnp.where(other == chip, sibling, 2 * other + core)
        return pltpu.make_async_remote_copy(
            src_ref=gp.at[g], dst_ref=gpland.at[g, c], send_sem=own_send.at[g, other], recv_sem=gp_recv.at[g, c],
            device_id=(to, z), device_id_type=MESH,
        )

    def forward_copy(g, other):
        source = 2 * other + core
        return pltpu.make_async_remote_copy(
            src_ref=gpland.at[g, source], dst_ref=gpland.at[g, source], send_sem=fwd_send.at[g, other],
            recv_sem=gp_recv.at[g, source], device_id=(sibling, z), device_id_type=MESH,
        )

    def landed(g, source):
        pltpu.make_async_copy(gpland.at[g, source], gpland.at[g, source], gp_recv.at[g, source]).wait()

    def send_own(i):
        _, _, g = order(i)

        def start(step, _):
            own_copy(g, lax.rem(chip + step, chips)).start()
            return 0

        lax.fori_loop(1, chips + 1, start, 0)
        pltpu.make_async_copy(gp.at[g], gpland.at[g, c], own_sem.at[g]).start()

    send_own(0)
    send_own(1)
    for t in range(parts):
        for copy in e_copy(t):
            copy.start()
    mine = vec.at[pl.ds(0, 8)]
    share(mine, vecr, vec_send, vec_recv, c, cells, in_plane)
    share(loss, lossr, loss_send, loss_recv, z, planes, in_column)
    for t in range(parts):
        for copy in e_copy(t):
            copy.wait()

    def gather(i):
        _, _, g = order(i)

        @pl.when(i + 2 < chunks)
        def _():
            send_own(i + 2)

        x_copy = pltpu.make_async_copy(gath.at[g], xstage, xs_sem)
        x_copy.start()

        def pass_on(step, _):
            other = lax.rem(chip + step, chips)
            landed(g, 2 * other + core)
            forward_copy(g, other).start()
            return 0

        lax.fori_loop(1, chips, pass_on, 0)

        def take(other, _):
            landed(g, 2 * other + 1 - core)
            return 0

        lax.fori_loop(0, chips, take, 0)
        pltpu.make_async_copy(gp.at[g], gpland.at[g, c], own_sem.at[g]).wait()
        g_copy = pltpu.make_async_copy(gpland.at[g], gstage, gs_sem)
        g_copy.start()
        x_copy.wait()
        columns = pl.ds(pl.multiple_of(g * GK, 128), GK)

        def split_x(t, _):
            high, low = split(xstage[pl.ds(pl.multiple_of(t * rows, 16), rows), :])
            x2[t, pl.ds(0, rows), columns] = high
            x2[t, pl.ds(rows, rows), columns] = low
            return 0

        lax.fori_loop(0, parts, split_x, 0)
        g_copy.wait()

        def split_g(t, _):
            place = pl.ds(pl.multiple_of(t * 128, 128), 128)
            high, low = split(gstage[:, :, place].reshape(GK, 128))
            lines = pl.ds(pl.multiple_of(g * GK, 128), GK)
            gph[lines, place] = high
            gpl[lines, place] = low
            return 0

        lax.fori_loop(0, S // 128, split_g, 0)

    def up_copy(g, slot):
        return pltpu.make_async_remote_copy(
            src_ref=zsend.at[slot], dst_ref=below.at[g], send_sem=zs_sem.at[slot], recv_sem=b_recv.at[g],
            device_id=(c, jnp.minimum(z + 1, planes - 1)), device_id_type=MESH,
        )

    def down_copy(g, slot):
        return pltpu.make_async_remote_copy(
            src_ref=zsend.at[slot], dst_ref=above.at[g], send_sem=zs_sem.at[slot], recv_sem=a_recv.at[g],
            device_id=(c, jnp.maximum(z - 1, 0)), device_id_type=MESH,
        )

    def sent(slot):
        pltpu.make_async_copy(zsend.at[slot], zsend.at[slot], zs_sem.at[slot]).wait()

    def expression_part(i):
        d, k, g = order(i)
        slot = lax.rem(i, 3)

        @pl.when(i >= 3)
        def _():
            sent(slot)

        lines = pl.ds(pl.multiple_of(g * GK, 128), GK)

        def multiply(t, _):
            both = dot(e2[t], gph[lines, :], NT)
            total = both[:rows] + both[rows:] + dot(e2[t, pl.ds(0, rows)], gpl[lines, :], NT)
            zsend[slot, pl.ds(pl.multiple_of(t * rows, 16), rows), :] = total
            return 0

        lax.fori_loop(0, parts, multiply, 0)

        def take(source, recv):
            pltpu.make_async_copy(source.at[g], source.at[g], recv.at[g]).wait()
            copy = pltpu.make_async_copy(source.at[g], zst, zst_sem)
            copy.start()
            copy.wait()

            def add(t, _):
                place = pl.ds(pl.multiple_of(t * rows, 16), rows)
                zsend[slot, place, :] += zst[place, :]
                return 0

            lax.fori_loop(0, parts, add, 0)

        @pl.when((d >= z) & (z > 0))
        def _():
            take(below, b_recv)

        @pl.when((d <= z) & (z < planes - 1))
        def _():
            take(above, a_recv)

        @pl.when(d > z)
        def _():
            up_copy(g, slot).start()

        @pl.when(d < z)
        def _():
            down_copy(g, slot).start()

        @pl.when(d == z)
        def _():
            place = pl.ds(pl.multiple_of(k * GK, 128), GK)
            pltpu.make_async_copy(zsend.at[slot], grad_expr.at[:, place], zs_sem.at[slot]).start()

    def out_copy(j, slot):
        t, n = lax.div(j, tiles), lax.rem(j, tiles)
        return pltpu.make_async_copy(
            outst.at[slot],
            grad_logits.at[pl.ds(pl.multiple_of(t * rows, 8), rows), pl.ds(pl.multiple_of(n * tile, 128), tile)],
            out_sem.at[slot],
        )

    def logits_part(j):
        t, n = lax.div(j, tiles), lax.rem(j, tiles)
        slot = lax.rem(j, 2)
        place = pl.ds(pl.multiple_of(n * tile, 128), tile)

        @pl.when(j >= 2)
        def _():
            out_copy(j - 2, slot).wait()

        both = dot(x2[t], gph[:, place])
        total = both[:rows] + both[rows:] + dot(x2[t, pl.ds(0, rows)], gpl[:, place])
        scale = weight[pl.ds(pl.multiple_of(t * rows, 8), rows), :]
        total = total + (scale * cols[0:1, place] - cols[1:2, place])
        exponent = e2[t, pl.ds(0, rows), place].astype(F32) + e2[t, pl.ds(rows, rows), place].astype(F32)
        outst[slot] = exponent * total
        out_copy(j, slot).start()

    def step(t, _):
        @pl.when(t < chunks)
        def _():
            gather(t)

        @pl.when(t == chunks)
        def _():
            total = collect(mine, vecr, vec_send, vec_recv, c, cells, in_plane)
            spot_sum = collect(loss, lossr, loss_send, loss_recv, z, planes, in_column)
            cols[0:1, :] = vec[8:9, :]
            cols[1:2, :] = total[0:1, :] + vec[9:10, :]
            losses[...] = jnp.zeros_like(losses)
            losses[0:1, :] = loss[2:3, :] - total[1:2, 0:128] / G - spot_sum[0:1, :] / loss[1:2, :]

        late = t - jnp.where(at_end, 0, cfg["late"])
        i = lax.div(3 * jnp.maximum(late, 0) + 7, 8)

        @pl.when((late >= 0) & (lax.div(8 * i, 3) == late) & (i < chunks))
        def _():
            expression_part(i)

        @pl.when((t >= chunks) & (t < chunks + parts * tiles))
        def _():
            logits_part(t - chunks)

        return 0

    lax.fori_loop(0, slots, step, 0)

    for slot in range(3):
        sent(slot)
    for j in range(parts * tiles - 2, parts * tiles):
        out_copy(j, j % 2).wait()

    def drain(g, _):
        def one(step, _):
            other = lax.rem(chip + step, chips)
            own_copy(g, other).wait_send()

            @pl.when(step < chips)
            def _():
                forward_copy(g, other).wait_send()

            return 0

        lax.fori_loop(1, chips + 1, one, 0)
        return 0

    lax.fori_loop(0, chunks, drain, 0)


def backward(cfg, gp, gath, ehi, elo, vec, loss, weight):
    cells, planes, C, S, G, GK, r = (cfg[k] for k in ("cells", "planes", "C", "S", "G", "GK", "r"))
    chips, per, chunks = cells // 2, G // planes // GK, G // GK
    parts, tile = cfg["parts"], cfg["tile"]
    rows = C // parts
    sem = pltpu.SemaphoreType.DMA
    scratch = [
        pltpu.VMEM((parts, 2 * rows, S), BF16), pltpu.VMEM((parts, 2 * rows, G), BF16),
        pltpu.VMEM((G, S), BF16), pltpu.VMEM((G, S), BF16),
        pltpu.VMEM((cells, r, S), F32), pltpu.VMEM((C, GK), F32), pltpu.VMEM((C, GK), F32),
        pltpu.VMEM((3, C, GK), F32), pltpu.VMEM((2, rows, tile), F32),
        pltpu.VMEM((8, S), F32), pltpu.VMEM((cells, 8, S), F32), pltpu.VMEM((planes, 8, 128), F32),
        sem((2, parts)), sem((chunks,)), sem((chunks, cells)), sem((chunks, chips)), sem((chunks, chips)),
        sem, sem, sem((chunks,)), sem((chunks,)), sem((3,)), sem, sem((2,)),
        sem((cells,)), sem((cells,)), sem((planes,)), sem((planes,)),
    ]
    return pl.pallas_call(
        functools.partial(backward_kernel, cfg),
        out_shape=(
            jax.ShapeDtypeStruct((C, S), F32),
            jax.ShapeDtypeStruct((C, G // planes), F32),
            jax.ShapeDtypeStruct((8, 128), F32),
            jax.ShapeDtypeStruct((chunks, cells, r, S), F32),
            jax.ShapeDtypeStruct((chunks, C, GK), F32),
            jax.ShapeDtypeStruct((chunks, C, GK), F32),
        ),
        in_specs=[ANY, ANY, ANY, ANY, VMEM, VMEM, VMEM],
        out_specs=(ANY, ANY, VMEM, ANY, ANY, ANY),
        scratch_shapes=scratch,
        compiler_params=pltpu.CompilerParams(
            collective_id=1, has_side_effects=True, vmem_limit_bytes=60 * 2**20
        ),
        cost_estimate=pl.CostEstimate(flops=12 * C * S * G, bytes_accessed=16 * C * S, transcendentals=0),
        name="backward",
    )(gp, gath, ehi, elo, vec, loss, weight)


def local(cells, planes, logits, expression, spatial, cell_counts, spot_density, slide_id, padding):
    C, S = logits.shape
    G = expression.shape[1] * planes
    GK = max(128, 8 * cells)
    chunks, parts, tile, late = G // GK, 4, 512, 5
    slots = max(chunks + parts * (S // tile), late + 8 * (chunks - 1) // 3 + 1)
    cfg = dict(
        cells=cells, planes=planes, C=C, S=S, G=G, GK=GK, r=GK // cells, rows=128, tile=tile, parts=parts,
        late=late, slots=slots,
    )
    gath, ehi, elo, gp, vec, loss = forward(
        cfg, logits, expression, spatial, cell_counts[None, :], spot_density[None, :],
        slide_id[None, :], padding[None, :],
    )
    grad_logits, grad_expression, losses, *_ = backward(
        cfg, gp, gath, ehi, elo, vec, loss, cell_counts.astype(F32)[:, None]
    )
    return (losses[0, :2], grad_logits, grad_expression)


def solution(mesh):
    cells, planes = mesh.shape["cell"], mesh.shape["spot"]
    in_specs = (
        P("cell", "spot"), P("cell", "spot"), P("cell", "spot"), P("cell"), P("spot"), P("spot"), P("spot"),
    )
    out_specs = (P(), P("cell", "spot"), P("cell", "spot"))
    return jax.shard_map(
        functools.partial(local, cells, planes), mesh=mesh, in_specs=in_specs, out_specs=out_specs, check_vma=False
    )
```

```python
import functools

import jax
import jax.numpy as jnp
from jax import lax
from jax.experimental import pallas as pl
from jax.experimental.pallas import tpu as pltpu
from jax.sharding import PartitionSpec as P

epsilon = 1e-06
MESH = pl.DeviceIdType.MESH
F32, BF16 = jnp.float32, jnp.bfloat16
TN = (((0,), (0,)), ((), ()))
NN = (((1,), (0,)), ((), ()))
NT = (((1,), (1,)), ((), ()))


def dot(left, right, dims=NN):
    return lax.dot_general(left, right, dims, preferred_element_type=F32)


def split(v):
    high = v.astype(BF16)
    return high, (v - high.astype(F32)).astype(BF16)


def arrival(z, i, planes, per):
    near = jnp.minimum(z, planes - 1 - z)
    j = jnp.maximum(i - per, 0)
    pair = lax.rem(j, 2 * per)
    t = 1 + lax.div(j, 2 * per)
    both = jnp.where(lax.rem(pair, 2) == 0, z - t, z + t)
    late = jnp.maximum(j - 2 * near * per, 0)
    t = near + 1 + lax.div(late, per)
    one = jnp.where(z < planes - 1 - z, z + t, z - t)
    in_pairs = j < 2 * near * per
    shard = jnp.where(i < per, z, jnp.where(in_pairs, both, one))
    chunk = jnp.where(i < per, i, jnp.where(in_pairs, lax.div(pair, 2), lax.rem(late, per)))
    return shard, chunk


def greet(c, z, cells, planes):
    barrier = pltpu.get_barrier_semaphore()

    def in_plane(step, _):
        pl.semaphore_signal(barrier, inc=1, device_id=(lax.rem(c + step, cells), z), device_id_type=MESH)
        return 0

    def in_column(step, _):
        pl.semaphore_signal(barrier, inc=1, device_id=(c, lax.rem(z + step, planes)), device_id_type=MESH)
        return 0

    lax.fori_loop(1, cells, in_plane, 0)
    lax.fori_loop(1, planes, in_column, 0)
    pl.semaphore_wait(barrier, cells + planes - 2)


def share(src, dst, send, recv, me, count, device):
    def start(step, _):
        other = lax.rem(me + step, count)
        pltpu.make_async_remote_copy(
            src_ref=src, dst_ref=dst.at[me], send_sem=send.at[other], recv_sem=recv.at[me],
            device_id=device(other), device_id_type=MESH,
        ).start()
        return 0

    lax.fori_loop(1, count, start, 0)


def collect(src, dst, send, recv, me, count, device):
    def wait(step, total):
        other = lax.rem(me + step, count)
        copy = pltpu.make_async_remote_copy(
            src_ref=src, dst_ref=dst.at[other], send_sem=send.at[other], recv_sem=recv.at[other],
            device_id=device(other), device_id_type=MESH,
        )
        copy.wait_send()
        copy.wait_recv()
        return total + dst[other]

    return lax.fori_loop(1, count, wait, src[...])


def forward_kernel(
    cfg, logits, expr, spatial, counts, dens, slide, pad,
    gath, ehi_out, elo_out, gp_out, vec_out, loss_out,
    ehi, elo, lbuf, stage, amat, partial, corer, half, chipr, pred, spat,
    tots, totr, acc, spots, spotr, gcol, gst, gstr, vec,
    g_recv, up_send, down_send, l_sem, st_sem, put_sem, core_send, core_recv, chip_send, chip_recv,
    spat_send, spat_recv, tot_send, tot_recv, spot_send, spot_recv, gst_send, gst_recv, out_sem,
):
    cells, planes, C, S, G, GK, r = (cfg[k] for k in ("cells", "planes", "C", "S", "G", "GK", "r"))
    chips, per, chunks = cells // 2, G // planes // GK, G // GK
    rows, tile = cfg["rows"], cfg["tile"]
    own_genes = G // cells
    c, z = lax.axis_index("cell"), lax.axis_index("spot")
    chip, core = lax.div(c, 2), lax.rem(c, 2)
    sibling = c + 1 - 2 * core
    in_plane = lambda other: (other, z)
    in_column = lambda other: (c, other)

    greet(c, z, cells, planes)

    def z_copy(src, g, to, send):
        return pltpu.make_async_remote_copy(
            src_ref=src, dst_ref=gath.at[g], send_sem=send.at[g], recv_sem=g_recv.at[g],
            device_id=(c, to), device_id_type=MESH,
        )

    up, down = jnp.minimum(z + 1, planes - 1), jnp.maximum(z - 1, 0)

    def send_own(k, _):
        g = z * per + k
        src = expr.at[:, pl.ds(pl.multiple_of(k * GK, 128), GK)]

        @pl.when(z < planes - 1)
        def _():
            z_copy(src, g, up, up_send).start()

        @pl.when(z > 0)
        def _():
            z_copy(src, g, down, down_send).start()

        return 0

    lax.fori_loop(0, per, send_own, 0)

    blocks = own_genes // r

    def spat_copy(b):
        place = c * blocks + b
        g, owner = lax.div(place, cells), lax.rem(place, cells)
        src = spatial.at[pl.ds(pl.multiple_of(b * r, 8), r)]
        remote = pltpu.make_async_remote_copy(
            src_ref=src, dst_ref=spat.at[g], send_sem=spat_send.at[b], recv_sem=spat_recv.at[g],
            device_id=(owner, z), device_id_type=MESH,
        )
        local = pltpu.make_async_copy(src, spat.at[g], spat_recv.at[g])
        return owner, remote, local

    def send_spat(b, _):
        owner, remote, local = spat_copy(b)

        @pl.when(owner != c)
        def _():
            remote.start()

        @pl.when(owner == c)
        def _():
            local.start()

        return 0

    lax.fori_loop(0, blocks, send_spat, 0)

    def load(t):
        return pltpu.make_async_copy(
            logits.at[pl.ds(pl.multiple_of(t * rows, rows), rows)], lbuf.at[lax.rem(t, 2)], l_sem.at[lax.rem(t, 2)]
        )

    load(0).start()

    def exps(t, _):
        @pl.when(t + 1 < C // rows)
        def _():
            load(t + 1).start()

        load(t).wait()
        high, low = split(jnp.exp(lbuf[lax.rem(t, 2)]))
        place = pl.ds(pl.multiple_of(t * rows, rows), rows)
        ehi[place, :] = high
        elo[place, :] = low
        return 0

    lax.fori_loop(0, C // rows, exps, 0)
    keep = [pltpu.make_async_copy(ehi, ehi_out, out_sem.at[0]), pltpu.make_async_copy(elo, elo_out, out_sem.at[1])]
    for copy in keep:
        copy.start()

    row = lax.broadcasted_iota(jnp.int32, (16, C), 0)
    weight = jnp.broadcast_to(counts[...].astype(F32), (16, C))
    lhs = jnp.where(row == 0, 1.0, jnp.where(row == 1, weight, 0.0)).astype(BF16)

    def sums(t, _):
        place = pl.ds(pl.multiple_of(t * tile, tile), tile)
        both = dot(lhs, ehi[:, place]) + dot(lhs, elo[:, place])
        tots[:, place] = both[:8]
        return 0

    lax.fori_loop(0, S // tile, sums, 0)
    share(tots, totr, tot_send, tot_recv, c, cells, in_plane)

    valid = (1 - pad[...]).astype(F32)
    mask0 = valid * (slide[...] == 0).astype(F32)
    mask1 = valid * (slide[...] == 1).astype(F32)
    vec[4:5, :] = mask0
    vec[5:6, :] = mask1
    acc[...] = jnp.zeros_like(acc)
    gcol[...] = jnp.zeros_like(gcol)

    def core_copy(g, slot):
        return pltpu.make_async_remote_copy(
            src_ref=partial.at[slot, :, 1 - core], dst_ref=corer.at[g], send_sem=core_send.at[slot],
            recv_sem=core_recv.at[g], device_id=(sibling, z), device_id_type=MESH,
        )

    def chip_copy(g, slot, other):
        return pltpu.make_async_remote_copy(
            src_ref=half.at[slot, other], dst_ref=chipr.at[g, chip], send_sem=chip_send.at[slot, other],
            recv_sem=chip_recv.at[g, chip], device_id=(2 * other + core, z), device_id_type=MESH,
        )

    def chip_wait(g, slot, other):
        return pltpu.make_async_remote_copy(
            src_ref=half.at[slot, chip], dst_ref=chipr.at[g, other], send_sem=chip_send.at[slot, other],
            recv_sem=chip_recv.at[g, other], device_id=(2 * other + core, z), device_id_type=MESH,
        )

    def product(i):
        d, k = arrival(z, i, planes, per)
        g, slot = d * per + k, lax.rem(i, 2)
        own = pltpu.make_async_copy(expr.at[:, pl.ds(pl.multiple_of(k * GK, 128), GK)], stage, st_sem)
        pull = pltpu.make_async_copy(gath.at[g], stage, st_sem)
        put = pltpu.make_async_copy(stage, gath.at[g], put_sem)

        @pl.when(d == z)
        def _():
            own.start()

        @pl.when(d != z)
        def _():
            z_copy(gath.at[g], g, down, down_send).wait_recv()

        @pl.when((d < z) & (z < planes - 1))
        def _():
            z_copy(gath.at[g], g, up, up_send).start()

        @pl.when((d > z) & (z > 0))
        def _():
            z_copy(gath.at[g], g, down, down_send).start()

        @pl.when(d != z)
        def _():
            pull.start()

        pull.wait()

        @pl.when(d == z)
        def _():
            put.start()

        @pl.when(i >= 2)
        def _():
            core_copy(g, slot).wait_send()

        def turn(t, _):
            place = pl.ds(pl.multiple_of(t * 128, 128), 128)
            high, low = split(stage[place, :].T)
            amat[:GK, place] = high
            amat[GK:, place] = low
            return 0

        lax.fori_loop(0, C // 128, turn, 0)

        def multiply(t, _):
            place = pl.ds(pl.multiple_of(t * tile, tile), tile)
            both = dot(amat[...], ehi[:, place])
            total = both[:GK] + both[GK:] + dot(amat[:GK, :], elo[:, place])
            partial[slot, :, :, :, place] = total.reshape(chips, 2, r, tile)
            return 0

        lax.fori_loop(0, S // tile, multiply, 0)
        core_copy(g, slot).start()

        @pl.when(d == z)
        def _():
            put.wait()

    def to_chips(i):
        d, k = arrival(z, i, planes, per)
        g, slot = d * per + k, lax.rem(i, 2)
        core_copy(g, slot).wait_recv()

        @pl.when(i >= 2)
        def _():
            def drain(step, _):
                chip_copy(g, slot, lax.rem(chip + step, chips)).wait_send()
                return 0

            lax.fori_loop(1, chips, drain, 0)

        def add(other, _):
            half[slot, other] = partial[slot, other, core] + corer[g, other]

            @pl.when(other != chip)
            def _():
                chip_copy(g, slot, other).start()

            return 0

        lax.fori_loop(0, chips, add, 0)

    def finish(i):
        d, k = arrival(z, i, planes, per)
        g, slot = d * per + k, lax.rem(i, 2)
        pltpu.make_async_copy(spat.at[g], spat.at[g], spat_recv.at[g]).wait()

        def add(step, total):
            other = lax.rem(chip + step, chips)
            chip_wait(g, slot, other).wait_recv()
            return total + chipr[g, other]

        p = lax.fori_loop(1, chips, add, half[slot, chip]) * vec[0:1, :]
        s = spat[g]
        pred[g] = p
        ps, pp, ss = p * s, p * p, s * s
        acc[0] += ps
        acc[1] += pp
        acc[2] += ss
        lane = lax.broadcasted_iota(jnp.int32, (r, 128), 1)
        cols = jnp.zeros((r, 128), F32)
        for n, v in enumerate((ps, pp, ss)):
            for m in range(2):
                one = jnp.sum(v * vec[4 + m : 5 + m, :], axis=1, keepdims=True)
                cols = jnp.where(lane == 2 * n + m, one, cols)
        gcol[pl.ds(pl.multiple_of(g * r, 8), r), :] = cols

    def step(i, _):
        @pl.when(i < chunks)
        def _():
            product(i)

        @pl.when(i == 1)
        def _():
            total = collect(tots, totr, tot_send, tot_recv, c, cells, in_plane)
            vec[0:1, :] = 1.0 / total[0:1, :]
            vec[1:2, :] = total[1:2, :] / total[0:1, :]

        @pl.when((i >= 1) & (i <= chunks))
        def _():
            to_chips(i - 1)

        @pl.when(i >= 2)
        def _():
            finish(i - 2)

        return 0

    lax.fori_loop(0, chunks + 2, step, 0)

    spots[...] = jnp.zeros_like(spots)
    for n in range(3):
        spots[n : n + 1, :] = jnp.sum(acc[n], axis=0, keepdims=True)
    share(spots, spotr, spot_send, spot_recv, c, cells, in_plane)
    gst[...] = jnp.zeros_like(gst)
    gst[0:8, :] = gcol[...].T[0:8, :]
    density = vec[1:2, :]
    target = dens[...]
    lane = lax.broadcasted_iota(jnp.int32, (1, gst.shape[1]), 1)
    logs = target * jnp.log(target), target * jnp.log(density)
    for n, v in enumerate((jnp.ones_like(target), target, density, *logs)):
        line = jnp.zeros((1, gst.shape[1]), F32)
        for m in range(2):
            one = jnp.sum(v * vec[4 + m : 5 + m, :], axis=1, keepdims=True)
            line = jnp.where(lane == m, one, line)
        gst[8 + n : 9 + n, :] = line
    share(gst, gstr, gst_send, gst_recv, z, planes, in_column)

    genes = collect(gst, gstr, gst_send, gst_recv, z, planes, in_column)
    dot_g, aa_g, bb_g = ([genes[2 * n + m : 2 * n + m + 1, :] for m in range(2)] for n in range(3))
    slides = [[genes[8 + n : 9 + n, m : m + 1] for m in range(2)] for n in range(5)]
    lines, cos_sums, own_losses = [], [], []
    for m in range(2):
        norm = jnp.sqrt((aa_g[m] + epsilon) * (bb_g[m] + epsilon))
        cos = dot_g[m] / norm
        lines += [-1.0 / (norm * G), cos / ((aa_g[m] + epsilon) * G)]
        cos_sums.append(jnp.sum(cos, axis=1, keepdims=True))
    lines.append(jnp.zeros((124, gst.shape[1]), F32))
    gcol[...] = jnp.concatenate(lines, axis=0).T
    live = [jnp.maximum(v, 1.0) for v in slides[0]]
    mass_target, mass_pred = slides[1], slides[2]
    divergence = [
        (slides[3][m] - slides[4][m]) / mass_target[m] - jnp.log(mass_target[m]) + jnp.log(mass_pred[m])
        for m in range(2)
    ]
    mask0, mask1 = vec[4:5, :], vec[5:6, :]
    grad_density = (
        mask0 / mass_pred[0] + mask1 / mass_pred[1]
        - dens[...] * (mask0 / mass_target[0] + mask1 / mass_target[1]) / vec[1:2, :]
    )
    spot_weight = mask0 / live[0] + mask1 / live[1]

    spot = collect(spots, spotr, spot_send, spot_recv, c, cells, in_plane)
    norm = jnp.sqrt((spot[1:2, :] + epsilon) * (spot[2:3, :] + epsilon))
    spot_cos = spot[0:1, :] / norm
    inverse = vec[0:1, :]
    vec[2:3, :] = -spot_weight / norm
    vec[3:4, :] = spot_weight * spot_cos / (spot[1:2, :] + epsilon)
    vec[6:7, :] = grad_density * inverse
    vec[7:8, :] = vec[1:2, :] * grad_density * inverse
    acc[0] = jnp.zeros((r, S), F32)

    def gradient(g, _):
        columns = gcol[pl.ds(pl.multiple_of(g * r, 8), r), :]
        by_spatial = vec[4:5, :] * columns[:, 0:1] + vec[5:6, :] * columns[:, 2:3] + vec[2:3, :]
        by_pred = vec[4:5, :] * columns[:, 1:2] + vec[5:6, :] * columns[:, 3:4] + vec[3:4, :]
        p = pred[g]
        value = (spat[g] * by_spatial + p * by_pred) * vec[0:1, :]
        acc[0] += p * value
        pred[g] = value
        return 0

    lax.fori_loop(0, chunks, gradient, 0)
    copy = pltpu.make_async_copy(pred, gp_out, out_sem.at[2])
    copy.start()
    vec_out[...] = jnp.zeros_like(vec_out)
    vec_out[0:1, :] = jnp.sum(acc[0], axis=0, keepdims=True)
    vec_out[8:9, :] = vec[6:7, :]
    vec_out[9:10, :] = vec[7:8, :]
    lane = lax.broadcasted_iota(jnp.int32, (1, 128), 1)
    vec_out[1:2, 0:128] = jnp.where(lane == 0, cos_sums[0], jnp.where(lane == 1, cos_sums[1], 0.0))
    spot_sums = [jnp.sum(vec[4 + m : 5 + m, :] * spot_cos, axis=1, keepdims=True) for m in range(2)]
    loss_out[...] = jnp.zeros_like(loss_out)
    for n, v in enumerate((spot_sums, live, divergence)):
        loss_out[n : n + 1, :] = jnp.where(lane == 0, v[0], jnp.where(lane == 1, v[1], 0.0))

    copy.wait()
    for copy in keep:
        copy.wait()

    def drain_z(g, _):
        d = lax.div(g, per)

        @pl.when((d <= z) & (z < planes - 1))
        def _():
            z_copy(gath.at[g], g, up, up_send).wait_send()

        @pl.when((d >= z) & (z > 0))
        def _():
            z_copy(gath.at[g], g, down, down_send).wait_send()

        return 0

    lax.fori_loop(0, chunks, drain_z, 0)

    def drain_spat(b, _):
        owner, remote, _ = spat_copy(b)

        @pl.when(owner != c)
        def _():
            remote.wait_send()

        return 0

    lax.fori_loop(0, blocks, drain_spat, 0)
    for slot in range(2):
        core_copy(0, slot).wait_send()

        def drain(step, _):
            chip_copy(0, slot, lax.rem(chip + step, chips)).wait_send()
            return 0

        lax.fori_loop(1, chips, drain, 0)


ANY = pl.BlockSpec(memory_space=pl.ANY)
VMEM = pl.BlockSpec(memory_space=pltpu.VMEM)


def forward(cfg, logits, expression, spatial, counts, dens, slide, pad):
    cells, planes, C, S, G, GK, r = (cfg[k] for k in ("cells", "planes", "C", "S", "G", "GK", "r"))
    chips, per, chunks = cells // 2, G // planes // GK, G // GK
    rows = cfg["rows"]
    wide = max(G // cells, 128)
    blocks = G // cells // r
    sem = pltpu.SemaphoreType.DMA
    scratch = [
        pltpu.VMEM((C, S), BF16), pltpu.VMEM((C, S), BF16), pltpu.VMEM((2, rows, S), F32),
        pltpu.VMEM((C, GK), F32), pltpu.VMEM((2 * GK, C), BF16),
        pltpu.VMEM((2, chips, 2, r, S), F32), pltpu.VMEM((chunks, chips, r, S), F32),
        pltpu.VMEM((2, chips, r, S), F32), pltpu.VMEM((chunks, chips, r, S), F32),
        pltpu.VMEM((chunks, r, S), F32), pltpu.VMEM((chunks, r, S), F32),
        pltpu.VMEM((8, S), F32), pltpu.VMEM((cells, 8, S), F32), pltpu.VMEM((3, r, S), F32),
        pltpu.VMEM((8, S), F32), pltpu.VMEM((cells, 8, S), F32), pltpu.VMEM((wide, 128), F32),
        pltpu.VMEM((16, wide), F32), pltpu.VMEM((planes, 16, wide), F32), pltpu.VMEM((8, S), F32),
        sem((chunks,)), sem((chunks,)), sem((chunks,)), sem((2,)), sem, sem,
        sem((2,)), sem((chunks,)), sem((2, chips)), sem((chunks, chips)),
        sem((blocks,)), sem((chunks,)), sem((cells,)), sem((cells,)), sem((cells,)), sem((cells,)),
        sem((planes,)), sem((planes,)), sem((3,)),
    ]
    flops = 6 * C * S * G
    return pl.pallas_call(
        functools.partial(forward_kernel, cfg),
        out_shape=(
            jax.ShapeDtypeStruct((chunks, C, GK), F32),
            jax.ShapeDtypeStruct((C, S), BF16),
            jax.ShapeDtypeStruct((C, S), BF16),
            jax.ShapeDtypeStruct((chunks, r, S), F32),
            jax.ShapeDtypeStruct((16, S), F32),
            jax.ShapeDtypeStruct((8, 128), F32),
        ),
        in_specs=[ANY, ANY, ANY, VMEM, VMEM, VMEM, VMEM],
        out_specs=(ANY, ANY, ANY, ANY, VMEM, VMEM),
        scratch_shapes=scratch,
        compiler_params=pltpu.CompilerParams(
            collective_id=0, has_side_effects=True, vmem_limit_bytes=56 * 2**20
        ),
        cost_estimate=pl.CostEstimate(flops=flops, bytes_accessed=8 * C * S, transcendentals=C * S),
        name="forward",
    )(logits, expression, spatial, counts, dens, slide, pad)


def backward_kernel(
    cfg, gp, gath, ehi, elo, vec, loss, weight,
    grad_logits, grad_expr, losses, gpland, below, above,
    e2, x2, gph, gpl, gstage, xstage, zst, zsend, outst, cols, vecr, lossr,
    e_sem, gp_recv, own_send, fwd_send, gs_sem, xs_sem, b_recv, a_recv, zs_sem, zst_sem, out_sem,
    vec_send, vec_recv, loss_send, loss_recv,
):
    cells, planes, C, S, G, GK, r = (cfg[k] for k in ("cells", "planes", "C", "S", "G", "GK", "r"))
    chips, per, chunks = cells // 2, G // planes // GK, G // GK
    parts, tile, slots = cfg["parts"], cfg["tile"], cfg["slots"]
    rows, tiles = C // parts, S // tile
    c, z = lax.axis_index("cell"), lax.axis_index("spot")
    chip, core = lax.div(c, 2), lax.rem(c, 2)
    sibling = c + 1 - 2 * core
    in_plane = lambda other: (other, z)
    in_column = lambda other: (c, other)
    at_end = (z == 0) | (z == planes - 1)

    def order(i):
        d, k = arrival(z, chunks - 1 - i, planes, per)
        return d, k, d * per + k

    def e_copy(t, _=None):
        place = pl.ds(pl.multiple_of(t * rows, 16), rows)
        return (
            pltpu.make_async_copy(ehi.at[place], e2.at[t, pl.ds(0, rows)], e_sem.at[0, t]),
            pltpu.make_async_copy(elo.at[place], e2.at[t, pl.ds(rows, rows)], e_sem.at[1, t]),
        )

    greet(c, z, cells, planes)

    def own_copy(g, other):
        to = jnp.where(other == chip, sibling, 2 * other + core)
        return pltpu.make_async_remote_copy(
            src_ref=gp.at[g], dst_ref=gpland.at[g, c], send_sem=own_send.at[g, other], recv_sem=gp_recv.at[g, c],
            device_id=(to, z), device_id_type=MESH,
        )

    def forward_copy(g, other):
        source = 2 * other + core
        return pltpu.make_async_remote_copy(
            src_ref=gpland.at[g, source], dst_ref=gpland.at[g, source], send_sem=fwd_send.at[g, other],
            recv_sem=gp_recv.at[g, source], device_id=(sibling, z), device_id_type=MESH,
        )

    def landed(g, source):
        pltpu.make_async_copy(gpland.at[g, source], gpland.at[g, source], gp_recv.at[g, source]).wait()

    def send_own(i):
        _, _, g = order(i)

        def start(step, _):
            own_copy(g, lax.rem(chip + step, chips)).start()
            return 0

        lax.fori_loop(1, chips + 1, start, 0)

    send_own(0)
    send_own(1)
    for t in range(parts):
        for copy in e_copy(t):
            copy.start()
    mine = vec.at[pl.ds(0, 8)]
    share(mine, vecr, vec_send, vec_recv, c, cells, in_plane)
    share(loss, lossr, loss_send, loss_recv, z, planes, in_column)
    for t in range(parts):
        for copy in e_copy(t):
            copy.wait()

    def gather(i):
        _, _, g = order(i)

        @pl.when(i + 2 < chunks)
        def _():
            send_own(i + 2)

        x_copy = pltpu.make_async_copy(gath.at[g], xstage, xs_sem)
        x_copy.start()
        pltpu.make_async_copy(gp.at[g], gstage.at[c], gs_sem).start()

        def pass_on(step, _):
            other = lax.rem(chip + step, chips)
            landed(g, 2 * other + core)
            forward_copy(g, other).start()
            pltpu.make_async_copy(gpland.at[g, 2 * other + core], gstage.at[2 * other + core], gs_sem).start()
            return 0

        lax.fori_loop(1, chips, pass_on, 0)

        def take(other, _):
            landed(g, 2 * other + 1 - core)
            pltpu.make_async_copy(gpland.at[g, 2 * other + 1 - core], gstage.at[2 * other + 1 - core], gs_sem).start()
            return 0

        lax.fori_loop(0, chips, take, 0)
        x_copy.wait()
        columns = pl.ds(pl.multiple_of(g * GK, 128), GK)

        def split_x(t, _):
            high, low = split(xstage[pl.ds(pl.multiple_of(t * rows, 16), rows), :])
            x2[t, pl.ds(0, rows), columns] = high
            x2[t, pl.ds(rows, rows), columns] = low
            return 0

        lax.fori_loop(0, parts, split_x, 0)
        pltpu.make_async_copy(gstage, gstage, gs_sem).wait()

        def split_g(t, _):
            place = pl.ds(pl.multiple_of(t * 128, 128), 128)
            high, low = split(gstage[:, :, place].reshape(GK, 128))
            lines = pl.ds(pl.multiple_of(g * GK, 128), GK)
            gph[lines, place] = high
            gpl[lines, place] = low
            return 0

        lax.fori_loop(0, S // 128, split_g, 0)

    def up_copy(g, slot):
        return pltpu.make_async_remote_copy(
            src_ref=zsend.at[slot], dst_ref=below.at[g], send_sem=zs_sem.at[slot], recv_sem=b_recv.at[g],
            device_id=(c, jnp.minimum(z + 1, planes - 1)), device_id_type=MESH,
        )

    def down_copy(g, slot):
        return pltpu.make_async_remote_copy(
            src_ref=zsend.at[slot], dst_ref=above.at[g], send_sem=zs_sem.at[slot], recv_sem=a_recv.at[g],
            device_id=(c, jnp.maximum(z - 1, 0)), device_id_type=MESH,
        )

    def sent(slot):
        pltpu.make_async_copy(zsend.at[slot], zsend.at[slot], zs_sem.at[slot]).wait()

    def expression_part(i):
        d, k, g = order(i)
        slot = lax.rem(i, 3)

        @pl.when(i >= 3)
        def _():
            sent(slot)

        lines = pl.ds(pl.multiple_of(g * GK, 128), GK)

        def multiply(t, _):
            both = dot(e2[t], gph[lines, :], NT)
            total = both[:rows] + both[rows:] + dot(e2[t, pl.ds(0, rows)], gpl[lines, :], NT)
            zsend[slot, pl.ds(pl.multiple_of(t * rows, 16), rows), :] = total
            return 0

        lax.fori_loop(0, parts, multiply, 0)

        def take(source, recv):
            pltpu.make_async_copy(source.at[g], source.at[g], recv.at[g]).wait()
            copy = pltpu.make_async_copy(source.at[g], zst, zst_sem)
            copy.start()
            copy.wait()

            def add(t, _):
                place = pl.ds(pl.multiple_of(t * rows, 16), rows)
                zsend[slot, place, :] += zst[place, :]
                return 0

            lax.fori_loop(0, parts, add, 0)

        @pl.when((d >= z) & (z > 0))
        def _():
            take(below, b_recv)

        @pl.when((d <= z) & (z < planes - 1))
        def _():
            take(above, a_recv)

        @pl.when(d > z)
        def _():
            up_copy(g, slot).start()

        @pl.when(d < z)
        def _():
            down_copy(g, slot).start()

        @pl.when(d == z)
        def _():
            place = pl.ds(pl.multiple_of(k * GK, 128), GK)
            pltpu.make_async_copy(zsend.at[slot], grad_expr.at[:, place], zs_sem.at[slot]).start()

    def out_copy(j, slot):
        t, n = lax.div(j, tiles), lax.rem(j, tiles)
        return pltpu.make_async_copy(
            outst.at[slot],
            grad_logits.at[pl.ds(pl.multiple_of(t * rows, 8), rows), pl.ds(pl.multiple_of(n * tile, 128), tile)],
            out_sem.at[slot],
        )

    def logits_part(j):
        t, n = lax.div(j, tiles), lax.rem(j, tiles)
        slot = lax.rem(j, 2)
        place = pl.ds(pl.multiple_of(n * tile, 128), tile)

        @pl.when(j >= 2)
        def _():
            out_copy(j - 2, slot).wait()

        both = dot(x2[t], gph[:, place])
        total = both[:rows] + both[rows:] + dot(x2[t, pl.ds(0, rows)], gpl[:, place])
        scale = weight[pl.ds(pl.multiple_of(t * rows, 8), rows), :]
        total = total + (scale * cols[0:1, place] - cols[1:2, place])
        exponent = e2[t, pl.ds(0, rows), place].astype(F32) + e2[t, pl.ds(rows, rows), place].astype(F32)
        outst[slot] = exponent * total
        out_copy(j, slot).start()

    def step(t, _):
        @pl.when(t < chunks)
        def _():
            gather(t)

        @pl.when(t == chunks)
        def _():
            total = collect(mine, vecr, vec_send, vec_recv, c, cells, in_plane)
            spot_sum = collect(loss, lossr, loss_send, loss_recv, z, planes, in_column)
            cols[0:1, :] = vec[8:9, :]
            cols[1:2, :] = total[0:1, :] + vec[9:10, :]
            losses[...] = jnp.zeros_like(losses)
            losses[0:1, :] = loss[2:3, :] - total[1:2, 0:128] / G - spot_sum[0:1, :] / loss[1:2, :]

        late = t - jnp.where(at_end, 0, cfg["late"])
        i = lax.div(3 * jnp.maximum(late, 0) + 7, 8)

        @pl.when((late >= 0) & (lax.div(8 * i, 3) == late) & (i < chunks))
        def _():
            expression_part(i)

        @pl.when((t >= chunks) & (t < chunks + parts * tiles))
        def _():
            logits_part(t - chunks)

        return 0

    lax.fori_loop(0, slots, step, 0)

    for slot in range(3):
        sent(slot)
    for j in range(parts * tiles - 2, parts * tiles):
        out_copy(j, j % 2).wait()

    def drain(g, _):
        def one(step, _):
            other = lax.rem(chip + step, chips)
            own_copy(g, other).wait_send()

            @pl.when(step < chips)
            def _():
                forward_copy(g, other).wait_send()

            return 0

        lax.fori_loop(1, chips + 1, one, 0)
        return 0

    lax.fori_loop(0, chunks, drain, 0)


def backward(cfg, gp, gath, ehi, elo, vec, loss, weight):
    cells, planes, C, S, G, GK, r = (cfg[k] for k in ("cells", "planes", "C", "S", "G", "GK", "r"))
    chips, per, chunks = cells // 2, G // planes // GK, G // GK
    parts, tile = cfg["parts"], cfg["tile"]
    rows = C // parts
    sem = pltpu.SemaphoreType.DMA
    scratch = [
        pltpu.VMEM((parts, 2 * rows, S), BF16), pltpu.VMEM((parts, 2 * rows, G), BF16),
        pltpu.VMEM((G, S), BF16), pltpu.VMEM((G, S), BF16),
        pltpu.VMEM((cells, r, S), F32), pltpu.VMEM((C, GK), F32), pltpu.VMEM((C, GK), F32),
        pltpu.VMEM((3, C, GK), F32), pltpu.VMEM((2, rows, tile), F32),
        pltpu.VMEM((8, S), F32), pltpu.VMEM((cells, 8, S), F32), pltpu.VMEM((planes, 8, 128), F32),
        sem((2, parts)), sem((chunks, cells)), sem((chunks, chips)), sem((chunks, chips)),
        sem, sem, sem((chunks,)), sem((chunks,)), sem((3,)), sem, sem((2,)),
        sem((cells,)), sem((cells,)), sem((planes,)), sem((planes,)),
    ]
    return pl.pallas_call(
        functools.partial(backward_kernel, cfg),
        out_shape=(
            jax.ShapeDtypeStruct((C, S), F32),
            jax.ShapeDtypeStruct((C, G // planes), F32),
            jax.ShapeDtypeStruct((8, 128), F32),
            jax.ShapeDtypeStruct((chunks, cells, r, S), F32),
            jax.ShapeDtypeStruct((chunks, C, GK), F32),
            jax.ShapeDtypeStruct((chunks, C, GK), F32),
        ),
        in_specs=[ANY, ANY, ANY, ANY, VMEM, VMEM, VMEM],
        out_specs=(ANY, ANY, VMEM, ANY, ANY, ANY),
        scratch_shapes=scratch,
        compiler_params=pltpu.CompilerParams(
            collective_id=1, has_side_effects=True, vmem_limit_bytes=60 * 2**20
        ),
        cost_estimate=pl.CostEstimate(flops=12 * C * S * G, bytes_accessed=16 * C * S, transcendentals=0),
        name="backward",
    )(gp, gath, ehi, elo, vec, loss, weight)


def local(cells, planes, logits, expression, spatial, cell_counts, spot_density, slide_id, padding):
    C, S = logits.shape
    G = expression.shape[1] * planes
    GK = max(128, 8 * cells)
    chunks, parts, tile, late = G // GK, 4, 512, 5
    slots = max(chunks + parts * (S // tile), late + 8 * (chunks - 1) // 3 + 1)
    cfg = dict(
        cells=cells, planes=planes, C=C, S=S, G=G, GK=GK, r=GK // cells, rows=128, tile=tile, parts=parts,
        late=late, slots=slots,
    )
    gath, ehi, elo, gp, vec, loss = forward(
        cfg, logits, expression, spatial, cell_counts[None, :], spot_density[None, :],
        slide_id[None, :], padding[None, :],
    )
    grad_logits, grad_expression, losses, *_ = backward(
        cfg, gp, gath, ehi, elo, vec, loss, cell_counts.astype(F32)[:, None]
    )
    return (losses[0, :2], grad_logits, grad_expression)


def solution(mesh):
    cells, planes = mesh.shape["cell"], mesh.shape["spot"]
    in_specs = (
        P("cell", "spot"), P("cell", "spot"), P("cell", "spot"), P("cell"), P("spot"), P("spot"), P("spot"),
    )
    out_specs = (P(), P("cell", "spot"), P("cell", "spot"))
    return jax.shard_map(
        functools.partial(local, cells, planes), mesh=mesh, in_specs=in_specs, out_specs=out_specs, check_vma=False
    )
```

```python
import functools

import jax
import jax.numpy as jnp
from jax import lax
from jax.experimental import pallas as pl
from jax.experimental.pallas import tpu as pltpu
from jax.sharding import PartitionSpec as P

epsilon = 1e-06
MESH = pl.DeviceIdType.MESH
F32, BF16 = jnp.float32, jnp.bfloat16
TN = (((0,), (0,)), ((), ()))
NN = (((1,), (0,)), ((), ()))
NT = (((1,), (1,)), ((), ()))


def dot(left, right, dims=NN):
    return lax.dot_general(left, right, dims, preferred_element_type=F32)


def split(v):
    high = v.astype(BF16)
    return high, (v - high.astype(F32)).astype(BF16)


def arrival(z, i, planes, per):
    near = jnp.minimum(z, planes - 1 - z)
    j = jnp.maximum(i - per, 0)
    pair = lax.rem(j, 2 * per)
    t = 1 + lax.div(j, 2 * per)
    both = jnp.where(lax.rem(pair, 2) == 0, z - t, z + t)
    late = jnp.maximum(j - 2 * near * per, 0)
    t = near + 1 + lax.div(late, per)
    one = jnp.where(z < planes - 1 - z, z + t, z - t)
    in_pairs = j < 2 * near * per
    shard = jnp.where(i < per, z, jnp.where(in_pairs, both, one))
    chunk = jnp.where(i < per, i, jnp.where(in_pairs, lax.div(pair, 2), lax.rem(late, per)))
    return shard, chunk


def greet(c, z, cells, planes):
    barrier = pltpu.get_barrier_semaphore()

    def in_plane(step, _):
        pl.semaphore_signal(barrier, inc=1, device_id=(lax.rem(c + step, cells), z), device_id_type=MESH)
        return 0

    def in_column(step, _):
        pl.semaphore_signal(barrier, inc=1, device_id=(c, lax.rem(z + step, planes)), device_id_type=MESH)
        return 0

    lax.fori_loop(1, cells, in_plane, 0)
    lax.fori_loop(1, planes, in_column, 0)
    pl.semaphore_wait(barrier, cells + planes - 2)


def share(src, dst, send, recv, me, count, device):
    def start(step, _):
        other = lax.rem(me + step, count)
        pltpu.make_async_remote_copy(
            src_ref=src, dst_ref=dst.at[me], send_sem=send.at[other], recv_sem=recv.at[me],
            device_id=device(other), device_id_type=MESH,
        ).start()
        return 0

    lax.fori_loop(1, count, start, 0)


def collect(src, dst, send, recv, me, count, device):
    def wait(step, total):
        other = lax.rem(me + step, count)
        copy = pltpu.make_async_remote_copy(
            src_ref=src, dst_ref=dst.at[other], send_sem=send.at[other], recv_sem=recv.at[other],
            device_id=device(other), device_id_type=MESH,
        )
        copy.wait_send()
        copy.wait_recv()
        return total + dst[other]

    return lax.fori_loop(1, count, wait, src[...])


def forward_kernel(
    cfg, logits, expr, spatial, counts, dens, slide, pad,
    gath, ehi_out, elo_out, x_out, far_logits, gp_out, vec_out, loss_out,
    ehi, elo, lbuf, stage, xparts, amat, partial, corer, half, chipr, pred, spat,
    tots, totr, acc, spots, spotr, gcol, gst, gstr, vec,
    g_recv, up_send, down_send, l_sem, st_sem, put_sem, core_send, core_recv, chip_send, chip_recv,
    far_send, far_recv, spat_send, spat_recv, tot_send, tot_recv, spot_send, spot_recv, gst_send, gst_recv, out_sem,
):
    cells, planes, C, S, G, GK, r = (cfg[k] for k in ("cells", "planes", "C", "S", "G", "GK", "r"))
    chips, per, chunks = cells // 2, G // planes // GK, G // GK
    rows, tile, parts, helped = cfg["rows"], cfg["tile"], cfg["parts"], cfg["helped"]
    part, pieces = C // parts, cfg["pieces"]
    own_genes = G // cells
    c, z = lax.axis_index("cell"), lax.axis_index("spot")
    chip, core = lax.div(c, 2), lax.rem(c, 2)
    sibling = c + 1 - 2 * core
    in_plane = lambda other: (other, z)
    in_column = lambda other: (c, other)

    greet(c, z, cells, planes)

    def z_copy(src, g, to, send):
        return pltpu.make_async_remote_copy(
            src_ref=src, dst_ref=gath.at[g], send_sem=send.at[g], recv_sem=g_recv.at[g],
            device_id=(c, to), device_id_type=MESH,
        )

    up, down = jnp.minimum(z + 1, planes - 1), jnp.maximum(z - 1, 0)

    def send_own(k, _):
        g = z * per + k
        src = expr.at[:, pl.ds(pl.multiple_of(k * GK, 128), GK)]

        @pl.when(z < planes - 1)
        def _():
            z_copy(src, g, up, up_send).start()

        @pl.when(z > 0)
        def _():
            z_copy(src, g, down, down_send).start()

        return 0

    lax.fori_loop(0, per, send_own, 0)

    at_end = (z == 0) | (z == planes - 1)
    helper = ((z == 1) | (z == planes - 2)) & helped
    beside = jnp.where(z == 0, 1, jnp.where(z == planes - 1, planes - 2, jnp.where(z == 1, 0, planes - 1)))
    piece = C // 2 // pieces

    def far_copy(n):
        return pltpu.make_async_remote_copy(
            src_ref=logits.at[pl.ds(pl.multiple_of(C // 2 + n * piece, 8), piece)],
            dst_ref=far_logits.at[pl.ds(pl.multiple_of(n * piece, 8), piece)],
            send_sem=far_send.at[n], recv_sem=far_recv.at[n], device_id=(c, beside), device_id_type=MESH,
        )

    blocks = own_genes // r

    def spat_copy(b):
        place = c * blocks + b
        g, owner = lax.div(place, cells), lax.rem(place, cells)
        src = spatial.at[pl.ds(pl.multiple_of(b * r, 8), r)]
        remote = pltpu.make_async_remote_copy(
            src_ref=src, dst_ref=spat.at[g], send_sem=spat_send.at[b], recv_sem=spat_recv.at[g],
            device_id=(owner, z), device_id_type=MESH,
        )
        local = pltpu.make_async_copy(src, spat.at[g], spat_recv.at[g])
        return owner, remote, local

    def send_spat(b, _):
        owner, remote, local = spat_copy(b)

        @pl.when(owner != c)
        def _():
            remote.start()

        @pl.when(owner == c)
        def _():
            local.start()

        return 0

    lax.fori_loop(0, blocks, send_spat, 0)

    def load(t):
        return pltpu.make_async_copy(
            logits.at[pl.ds(pl.multiple_of(t * rows, rows), rows)], lbuf.at[lax.rem(t, 2)], l_sem.at[lax.rem(t, 2)]
        )

    load(0).start()

    def exps(t, _):
        @pl.when(t + 1 < C // rows)
        def _():
            load(t + 1).start()

        load(t).wait()
        high, low = split(jnp.exp(lbuf[lax.rem(t, 2)]))
        place = pl.ds(pl.multiple_of(t * rows, rows), rows)
        ehi[place, :] = high
        elo[place, :] = low
        return 0

    lax.fori_loop(0, C // rows, exps, 0)
    keep = [pltpu.make_async_copy(ehi, ehi_out, out_sem.at[0]), pltpu.make_async_copy(elo, elo_out, out_sem.at[1])]
    for copy in keep:
        copy.start()

    row = lax.broadcasted_iota(jnp.int32, (16, C), 0)
    weight = jnp.broadcast_to(counts[...].astype(F32), (16, C))
    lhs = jnp.where(row == 0, 1.0, jnp.where(row == 1, weight, 0.0)).astype(BF16)

    def sums(t, _):
        place = pl.ds(pl.multiple_of(t * tile, tile), tile)
        both = dot(lhs, ehi[:, place]) + dot(lhs, elo[:, place])
        tots[:, place] = both[:8]
        return 0

    lax.fori_loop(0, S // tile, sums, 0)
    share(tots, totr, tot_send, tot_recv, c, cells, in_plane)

    valid = (1 - pad[...]).astype(F32)
    mask0 = valid * (slide[...] == 0).astype(F32)
    mask1 = valid * (slide[...] == 1).astype(F32)
    vec[4:5, :] = mask0
    vec[5:6, :] = mask1
    acc[...] = jnp.zeros_like(acc)
    gcol[...] = jnp.zeros_like(gcol)

    def core_copy(g, slot):
        return pltpu.make_async_remote_copy(
            src_ref=partial.at[slot, :, 1 - core], dst_ref=corer.at[g], send_sem=core_send.at[slot],
            recv_sem=core_recv.at[g], device_id=(sibling, z), device_id_type=MESH,
        )

    def chip_copy(g, slot, other):
        return pltpu.make_async_remote_copy(
            src_ref=half.at[slot, other], dst_ref=chipr.at[g, chip], send_sem=chip_send.at[slot, other],
            recv_sem=chip_recv.at[g, chip], device_id=(2 * other + core, z), device_id_type=MESH,
        )

    def chip_wait(g, slot, other):
        return pltpu.make_async_remote_copy(
            src_ref=half.at[slot, chip], dst_ref=chipr.at[g, other], send_sem=chip_send.at[slot, other],
            recv_sem=chip_recv.at[g, other], device_id=(2 * other + core, z), device_id_type=MESH,
        )

    def product(i):
        d, k = arrival(z, i, planes, per)
        g, slot = d * per + k, lax.rem(i, 2)
        own = pltpu.make_async_copy(expr.at[:, pl.ds(pl.multiple_of(k * GK, 128), GK)], stage, st_sem)
        pull = pltpu.make_async_copy(gath.at[g], stage, st_sem)

        @pl.when(d == z)
        def _():
            own.start()

        @pl.when(d != z)
        def _():
            z_copy(gath.at[g], g, down, down_send).wait_recv()

        @pl.when((d < z) & (z < planes - 1))
        def _():
            z_copy(gath.at[g], g, up, up_send).start()

        @pl.when((d > z) & (z > 0))
        def _():
            z_copy(gath.at[g], g, down, down_send).start()

        @pl.when(d != z)
        def _():
            pull.start()

        pull.wait()
        columns = pl.ds(pl.multiple_of(g * GK, 128), GK)

        @pl.when(i >= 1)
        def _():
            pltpu.make_async_copy(xparts, x_out.at[:, :, columns], put_sem).wait()

        def keep_parts(t, _):
            high, low = split(stage[pl.ds(pl.multiple_of(t * part, 16), part), :])
            xparts[t, pl.ds(0, part), :] = high
            xparts[t, pl.ds(part, part), :] = low
            return 0

        lax.fori_loop(0, parts, keep_parts, 0)
        pltpu.make_async_copy(xparts, x_out.at[:, :, columns], put_sem).start()

        @pl.when(i >= 2)
        def _():
            core_copy(g, slot).wait_send()

        def turn(t, _):
            place = pl.ds(pl.multiple_of(t * 128, 128), 128)
            high, low = split(stage[place, :].T)
            amat[:GK, place] = high
            amat[GK:, place] = low
            return 0

        lax.fori_loop(0, C // 128, turn, 0)

        def multiply(t, _):
            place = pl.ds(pl.multiple_of(t * tile, tile), tile)
            both = dot(amat[...], ehi[:, place])
            total = both[:GK] + both[GK:] + dot(amat[:GK, :], elo[:, place])
            partial[slot, :, :, :, place] = total.reshape(chips, 2, r, tile)
            return 0

        lax.fori_loop(0, S // tile, multiply, 0)
        core_copy(g, slot).start()

    def to_chips(i):
        d, k = arrival(z, i, planes, per)
        g, slot = d * per + k, lax.rem(i, 2)
        core_copy(g, slot).wait_recv()

        @pl.when(i >= 2)
        def _():
            def drain(step, _):
                chip_copy(g, slot, lax.rem(chip + step, chips)).wait_send()
                return 0

            lax.fori_loop(1, chips, drain, 0)

        def add(other, _):
            half[slot, other] = partial[slot, other, core] + corer[g, other]

            @pl.when(other != chip)
            def _():
                chip_copy(g, slot, other).start()

            return 0

        lax.fori_loop(0, chips, add, 0)

    def finish(i):
        d, k = arrival(z, i, planes, per)
        g, slot = d * per + k, lax.rem(i, 2)
        pltpu.make_async_copy(spat.at[g], spat.at[g], spat_recv.at[g]).wait()

        def add(step, total):
            other = lax.rem(chip + step, chips)
            chip_wait(g, slot, other).wait_recv()
            return total + chipr[g, other]

        p = lax.fori_loop(1, chips, add, half[slot, chip]) * vec[0:1, :]
        s = spat[g]
        pred[g] = p
        ps, pp, ss = p * s, p * p, s * s
        acc[0] += ps
        acc[1] += pp
        acc[2] += ss
        lane = lax.broadcasted_iota(jnp.int32, (r, 128), 1)
        cols = jnp.zeros((r, 128), F32)
        for n, v in enumerate((ps, pp, ss)):
            for m in range(2):
                one = jnp.sum(v * vec[4 + m : 5 + m, :], axis=1, keepdims=True)
                cols = jnp.where(lane == 2 * n + m, one, cols)
        gcol[pl.ds(pl.multiple_of(g * r, 8), r), :] = cols

    def step(i, _):
        @pl.when((i >= per) & (i < per + pieces) & at_end & helped)
        def _():
            far_copy(i - per).start()

        @pl.when(i < chunks)
        def _():
            product(i)

        @pl.when(i == 1)
        def _():
            total = collect(tots, totr, tot_send, tot_recv, c, cells, in_plane)
            vec[0:1, :] = 1.0 / total[0:1, :]
            vec[1:2, :] = total[1:2, :] / total[0:1, :]

        @pl.when((i >= 1) & (i <= chunks))
        def _():
            to_chips(i - 1)

        @pl.when(i >= 2)
        def _():
            finish(i - 2)

        return 0

    lax.fori_loop(0, chunks + 2, step, 0)

    spots[...] = jnp.zeros_like(spots)
    for n in range(3):
        spots[n : n + 1, :] = jnp.sum(acc[n], axis=0, keepdims=True)
    share(spots, spotr, spot_send, spot_recv, c, cells, in_plane)
    gst[...] = jnp.zeros_like(gst)
    gst[0:8, :] = gcol[...].T[0:8, :]
    density = vec[1:2, :]
    target = dens[...]
    lane = lax.broadcasted_iota(jnp.int32, (1, gst.shape[1]), 1)
    logs = target * jnp.log(target), target * jnp.log(density)
    for n, v in enumerate((jnp.ones_like(target), target, density, *logs)):
        line = jnp.zeros((1, gst.shape[1]), F32)
        for m in range(2):
            one = jnp.sum(v * vec[4 + m : 5 + m, :], axis=1, keepdims=True)
            line = jnp.where(lane == m, one, line)
        gst[8 + n : 9 + n, :] = line
    share(gst, gstr, gst_send, gst_recv, z, planes, in_column)

    genes = collect(gst, gstr, gst_send, gst_recv, z, planes, in_column)
    dot_g, aa_g, bb_g = ([genes[2 * n + m : 2 * n + m + 1, :] for m in range(2)] for n in range(3))
    slides = [[genes[8 + n : 9 + n, m : m + 1] for m in range(2)] for n in range(5)]
    lines, cos_sums, own_losses = [], [], []
    for m in range(2):
        norm = jnp.sqrt((aa_g[m] + epsilon) * (bb_g[m] + epsilon))
        cos = dot_g[m] / norm
        lines += [-1.0 / (norm * G), cos / ((aa_g[m] + epsilon) * G)]
        cos_sums.append(jnp.sum(cos, axis=1, keepdims=True))
    lines.append(jnp.zeros((124, gst.shape[1]), F32))
    gcol[...] = jnp.concatenate(lines, axis=0).T
    live = [jnp.maximum(v, 1.0) for v in slides[0]]
    mass_target, mass_pred = slides[1], slides[2]
    divergence = [
        (slides[3][m] - slides[4][m]) / mass_target[m] - jnp.log(mass_target[m]) + jnp.log(mass_pred[m])
        for m in range(2)
    ]
    mask0, mask1 = vec[4:5, :], vec[5:6, :]
    grad_density = (
        mask0 / mass_pred[0] + mask1 / mass_pred[1]
        - dens[...] * (mask0 / mass_target[0] + mask1 / mass_target[1]) / vec[1:2, :]
    )
    spot_weight = mask0 / live[0] + mask1 / live[1]

    spot = collect(spots, spotr, spot_send, spot_recv, c, cells, in_plane)
    norm = jnp.sqrt((spot[1:2, :] + epsilon) * (spot[2:3, :] + epsilon))
    spot_cos = spot[0:1, :] / norm
    inverse = vec[0:1, :]
    vec[2:3, :] = -spot_weight / norm
    vec[3:4, :] = spot_weight * spot_cos / (spot[1:2, :] + epsilon)
    vec[6:7, :] = grad_density * inverse
    vec[7:8, :] = vec[1:2, :] * grad_density * inverse
    acc[0] = jnp.zeros((r, S), F32)

    def gradient(g, _):
        columns = gcol[pl.ds(pl.multiple_of(g * r, 8), r), :]
        by_spatial = vec[4:5, :] * columns[:, 0:1] + vec[5:6, :] * columns[:, 2:3] + vec[2:3, :]
        by_pred = vec[4:5, :] * columns[:, 1:2] + vec[5:6, :] * columns[:, 3:4] + vec[3:4, :]
        p = pred[g]
        value = (spat[g] * by_spatial + p * by_pred) * vec[0:1, :]
        acc[0] += p * value
        pred[g] = value
        return 0

    lax.fori_loop(0, chunks, gradient, 0)
    copy = pltpu.make_async_copy(pred, gp_out.at[:, chip, core], out_sem.at[2])
    copy.start()
    vec_out[...] = jnp.zeros_like(vec_out)
    vec_out[0:1, :] = jnp.sum(acc[0], axis=0, keepdims=True)
    vec_out[8:9, :] = vec[6:7, :]
    vec_out[9:10, :] = vec[7:8, :]
    lane = lax.broadcasted_iota(jnp.int32, (1, 128), 1)
    vec_out[1:2, 0:128] = jnp.where(lane == 0, cos_sums[0], jnp.where(lane == 1, cos_sums[1], 0.0))
    spot_sums = [jnp.sum(vec[4 + m : 5 + m, :] * spot_cos, axis=1, keepdims=True) for m in range(2)]
    loss_out[...] = jnp.zeros_like(loss_out)
    for n, v in enumerate((spot_sums, live, divergence)):
        loss_out[n : n + 1, :] = jnp.where(lane == 0, v[0], jnp.where(lane == 1, v[1], 0.0))

    copy.wait()
    for copy in keep:
        copy.wait()
    pltpu.make_async_copy(xparts, x_out.at[:, :, pl.ds(0, GK)], put_sem).wait()

    def drain_far(n, _):
        @pl.when(at_end & helped)
        def _():
            far_copy(n).wait_send()

        @pl.when(helper)
        def _():
            far_copy(n).wait_recv()

        return 0

    lax.fori_loop(0, pieces, drain_far, 0)

    def drain_z(g, _):
        d = lax.div(g, per)

        @pl.when((d <= z) & (z < planes - 1))
        def _():
            z_copy(gath.at[g], g, up, up_send).wait_send()

        @pl.when((d >= z) & (z > 0))
        def _():
            z_copy(gath.at[g], g, down, down_send).wait_send()

        return 0

    lax.fori_loop(0, chunks, drain_z, 0)

    def drain_spat(b, _):
        owner, remote, _ = spat_copy(b)

        @pl.when(owner != c)
        def _():
            remote.wait_send()

        return 0

    lax.fori_loop(0, blocks, drain_spat, 0)
    for slot in range(2):
        core_copy(0, slot).wait_send()

        def drain(step, _):
            chip_copy(0, slot, lax.rem(chip + step, chips)).wait_send()
            return 0

        lax.fori_loop(1, chips, drain, 0)


ANY = pl.BlockSpec(memory_space=pl.ANY)
VMEM = pl.BlockSpec(memory_space=pltpu.VMEM)


def forward(cfg, logits, expression, spatial, counts, dens, slide, pad):
    cells, planes, C, S, G, GK, r = (cfg[k] for k in ("cells", "planes", "C", "S", "G", "GK", "r"))
    chips, per, chunks = cells // 2, G // planes // GK, G // GK
    rows = cfg["rows"]
    wide = max(G // cells, 128)
    blocks = G // cells // r
    sem = pltpu.SemaphoreType.DMA
    scratch = [
        pltpu.VMEM((C, S), BF16), pltpu.VMEM((C, S), BF16), pltpu.VMEM((2, rows, S), F32),
        pltpu.VMEM((C, GK), F32), pltpu.VMEM((cfg["parts"], 2 * C // cfg["parts"], GK), BF16), pltpu.VMEM((2 * GK, C), BF16),
        pltpu.VMEM((2, chips, 2, r, S), F32), pltpu.VMEM((chunks, chips, r, S), F32),
        pltpu.VMEM((2, chips, r, S), F32), pltpu.VMEM((chunks, chips, r, S), F32),
        pltpu.VMEM((chunks, r, S), F32), pltpu.VMEM((chunks, r, S), F32),
        pltpu.VMEM((8, S), F32), pltpu.VMEM((cells, 8, S), F32), pltpu.VMEM((3, r, S), F32),
        pltpu.VMEM((8, S), F32), pltpu.VMEM((cells, 8, S), F32), pltpu.VMEM((wide, 128), F32),
        pltpu.VMEM((16, wide), F32), pltpu.VMEM((planes, 16, wide), F32), pltpu.VMEM((8, S), F32),
        sem((chunks,)), sem((chunks,)), sem((chunks,)), sem((2,)), sem, sem,
        sem((2,)), sem((chunks,)), sem((2, chips)), sem((chunks, chips)),
        sem((cfg["pieces"],)), sem((cfg["pieces"],)),
        sem((blocks,)), sem((chunks,)), sem((cells,)), sem((cells,)), sem((cells,)), sem((cells,)),
        sem((planes,)), sem((planes,)), sem((3,)),
    ]
    flops = 6 * C * S * G
    return pl.pallas_call(
        functools.partial(forward_kernel, cfg),
        out_shape=(
            jax.ShapeDtypeStruct((chunks, C, GK), F32),
            jax.ShapeDtypeStruct((C, S), BF16),
            jax.ShapeDtypeStruct((C, S), BF16),
            jax.ShapeDtypeStruct((cfg["parts"], 2 * C // cfg["parts"], G), BF16),
            jax.ShapeDtypeStruct((C // 2, S), F32),
            jax.ShapeDtypeStruct((chunks, chips, 2, r, S), F32),
            jax.ShapeDtypeStruct((16, S), F32),
            jax.ShapeDtypeStruct((8, 128), F32),
        ),
        in_specs=[ANY, ANY, ANY, VMEM, VMEM, VMEM, VMEM],
        out_specs=(ANY, ANY, ANY, ANY, ANY, ANY, VMEM, VMEM),
        scratch_shapes=scratch,
        compiler_params=pltpu.CompilerParams(
            collective_id=0, has_side_effects=True, vmem_limit_bytes=56 * 2**20
        ),
        cost_estimate=pl.CostEstimate(flops=flops, bytes_accessed=8 * C * S, transcendentals=C * S),
        name="forward",
    )(logits, expression, spatial, counts, dens, slide, pad)


def backward_kernel(
    cfg, ehi, elo, xparts, far_logits, vec, loss, counts, _gp, _gath,
    grad_logits, grad_expr, losses, land, far_land, zland, zlast,
    e2, x2, e3, gph, gpl, far_g, gstage, fstage, lbuf, zst, zsend, outst, inst, cols, vecr, lossr, weight,
    e_sem, x_sem, l_sem, g_recv, g_pair, g_sent, f_recv, f_pair, f_sent, row_recv, row_sent, gs_sem, fs_sem,
    z_recv, zs_sem, zst_sem, out_sem, in_sem, vec_send, vec_recv, loss_send, loss_recv,
):
    cells, planes, C, S, G, GK, r = (cfg[k] for k in ("cells", "planes", "C", "S", "G", "GK", "r"))
    chips, per, chunks = cells // 2, G // planes // GK, G // GK
    parts, tile, slots, group, zslots = (cfg[k] for k in ("parts", "tile", "slots", "group", "zslots"))
    ahead = cfg["ahead"]
    handed = cfg["handed"]
    count, groups = parts * (S // tile), chunks // group
    cuts = (0, chunks // 2, chunks)
    last = len(cuts) - 2
    helped, across = cfg["helped"], cfg["across"]
    rows, tiles, halves = C // parts, S // tile, parts // 2
    piece = cfg["piece"]
    pieces = C // 2 // piece
    down_chips = chips // across
    c, z = lax.axis_index("cell"), lax.axis_index("spot")
    chip, core = lax.div(c, 2), lax.rem(c, 2)
    chip_row, chip_col = lax.div(chip, across), lax.rem(chip, across)
    sibling = c + 1 - 2 * core
    in_plane = lambda other: (other, z)
    in_column = lambda other: (c, other)
    at_end = ((z == 0) | (z == planes - 1)) & helped
    helper = ((z == 1) | (z == planes - 2)) & helped
    beside = jnp.where(z == 0, 1, jnp.where(z == planes - 1, planes - 2, jnp.where(z == 1, 0, planes - 1)))

    def order(i):
        d, k = arrival(z, chunks - 1 - i, planes, per)
        return d, k, d * per + k

    greet(c, z, cells, planes)

    def spread(land, recv, pair, sent, buffer, ready):
        def copy(ref, source, g, other):
            return pltpu.make_async_remote_copy(
                src_ref=ref, dst_ref=ref, send_sem=sent.at[g, 0], recv_sem=recv.at[g, source],
                device_id=(2 * other + core, z), device_id_type=MESH,
            )

        def along_row(n):
            return chip_row * across + lax.rem(chip_col + n, across)

        def along_col(n):
            return lax.rem(chip_row + n, down_chips) * across + chip_col

        def each(count, body):
            def one(n, _):
                body(n)
                return 0

            lax.fori_loop(1, count, one, 0)

        def send(g):
            own = land.at[g, chip, core]
            each(across, lambda n: copy(own, chip, g, along_row(n)).start())
            each(down_chips, lambda n: copy(own, chip, g, along_col(n)).start())

        def landed(g, source):
            ref = land.at[g, source, core]
            pltpu.make_async_copy(ref, ref, recv.at[g, source]).wait()

        def first_hop(g):
            def from_row(n):
                source = along_row(n)
                landed(g, source)
                half = land.at[g, source, core, :, pl.ds(0, S // 2)]
                each(down_chips, lambda m: copy(half, source, g, along_col(m)).start())

            def from_col(n):
                source = along_col(n)
                landed(g, source)
                half = land.at[g, source, core, :, pl.ds(S // 2, S // 2)]
                each(across, lambda m: copy(half, source, g, along_row(m)).start())

            each(across, from_row)
            each(down_chips, from_col)

        def to_sibling(g):
            ref = land.at[g, :, core]
            return pltpu.make_async_remote_copy(
                src_ref=ref, dst_ref=ref, send_sem=sent.at[g, 1], recv_sem=pair.at[g],
                device_id=(sibling, z), device_id_type=MESH,
            )

        def second_hop(g):
            def from_rest(n):
                other = lax.rem(chip_row + 1 + lax.div(n - 1, across - 1), down_chips) * across
                landed(g, other + lax.rem(chip_col + 1 + lax.rem(n - 1, across - 1), across))

            each((across - 1) * (down_chips - 1) + 1, from_rest)
            to_sibling(g).start()

        def stage(g, slot):
            ref = land.at[g, :, 1 - core]
            pltpu.make_async_copy(ref, ref, pair.at[g]).wait()
            pltpu.make_async_copy(land.at[g], buffer.at[slot], ready.at[slot]).start()

        def take(slot, high_ref, low_ref, first):
            pltpu.make_async_copy(buffer.at[slot], buffer.at[slot], ready.at[slot]).wait()

            def split_tile(t, _):
                place = pl.ds(pl.multiple_of(t * 128, 128), 128)
                high, low = split(buffer[slot, :, :, :, place].reshape(GK, 128))
                lines = pl.ds(pl.multiple_of(first, 128), GK)
                high_ref[lines, place] = high
                low_ref[lines, place] = low
                return 0

            lax.fori_loop(0, S // 128, split_tile, 0)

        def drain(g):
            direct = land.at[g, pl.ds(0, chips - 1), 0]
            pltpu.make_async_copy(direct, direct, sent.at[g, 0]).wait()
            to_sibling(g).wait_send()

        return send, first_hop, second_hop, stage, take, drain

    send_own, first_own, second_own, stage_own, take_own, drain_own = spread(
        land, g_recv, g_pair, g_sent, gstage, gs_sem
    )
    send_far, first_far, second_far, stage_far, take_far, drain_far = spread(
        far_land, f_recv, f_pair, f_sent, fstage, fs_sem
    )

    def rank(d, k):
        end = jnp.where(at_end, z, beside)
        return (planes - 1 - jnp.abs(d - end)) * per + per - 1 - k

    def row_copy(n, g):
        return pltpu.make_async_remote_copy(
            src_ref=land.at[g, chip, core], dst_ref=far_land.at[n, chip, core],
            send_sem=row_sent.at[n], recv_sem=row_recv.at[n],
            device_id=(c, beside), device_id_type=MESH,
        )

    def announce(i):
        _, _, g = order(i)
        send_own(g)

        @pl.when(at_end & (i < handed))
        def _():
            row_copy(i, g).start()

    announce(0)
    announce(1)

    def e_copy(t):
        place = pl.ds(pl.multiple_of(t * rows, 16), rows)
        return (
            pltpu.make_async_copy(ehi.at[place], e2.at[t, pl.ds(0, rows)], e_sem.at[0, t]),
            pltpu.make_async_copy(elo.at[place], e2.at[t, pl.ds(rows, rows)], e_sem.at[1, t]),
        )

    for t in range(parts):
        for copy in e_copy(t):
            copy.start()
    def load_x(i, _):
        from_place = pl.ds(pl.multiple_of(order(i)[2] * GK, 128), GK)
        to_place = pl.ds(pl.multiple_of(i * GK, 128), GK)
        pltpu.make_async_copy(xparts.at[:, :, from_place], x2.at[:, :, to_place], x_sem).start()
        return 0

    mine = vec.at[pl.ds(0, 8)]
    share(mine, vecr, vec_send, vec_recv, c, cells, in_plane)
    share(loss, lossr, loss_send, loss_recv, z, planes, in_column)

    def far_exponentials():
        def load(n):
            return pltpu.make_async_copy(
                far_logits.at[pl.ds(pl.multiple_of(n * piece, 8), piece)], lbuf.at[lax.rem(n, 2)], l_sem.at[lax.rem(n, 2)]
            )

        for n in range(2):
            load(n).start()

        def exps(n, _):
            load(n).wait()
            high, low = split(jnp.exp(lbuf[lax.rem(n, 2)]))
            t, place = lax.div(n * piece, rows), lax.rem(n * piece, rows)
            e3[t, pl.ds(pl.multiple_of(place, 16), piece), :] = high
            e3[t, pl.ds(pl.multiple_of(rows + place, 16), piece), :] = low

            @pl.when(n + 2 < pieces)
            def _():
                load(n + 2).start()

            return 0

        lax.fori_loop(0, pieces, exps, 0)

    def far_step(n, what):
        @pl.when(helper & (n < handed))
        def _():
            what(n)

    def ask_far(n):
        row_copy(n, 0).wait_recv()
        send_far(n)

    def z_copy(land, index, number, slot, n, h, to):
        place = pl.ds(h * (C // 2), C // 2)
        return pltpu.make_async_remote_copy(
            src_ref=zsend.at[slot, n, h], dst_ref=land.at[index, place], send_sem=zs_sem.at[slot, n, h],
            recv_sem=z_recv.at[number, h], device_id=(c, to), device_id_type=MESH,
        )

    def sent(slot, n, h):
        pltpu.make_async_copy(zsend.at[slot, n, h], zsend.at[slot, n, h], zs_sem.at[slot, n, h]).wait()

    def had(p, h):
        return True if h == 0 else jnp.logical_not(at_end) | (p * group >= handed)

    def multiply_group(p):
        slot = lax.rem(p, zslots)
        lines = pl.ds(pl.multiple_of(p * group * GK, 128), group * GK)

        def half(h):
            @pl.when((p >= zslots) & had(p - zslots, h))
            def _():
                for n in range(group):
                    sent(slot, n, h)

            def multiply(t, _):
                both = dot(e2[h * halves + t], gph[lines, :], NT)
                total = both[:rows] + both[rows:] + dot(e2[h * halves + t, pl.ds(0, rows)], gpl[lines, :], NT)
                for n in range(group):
                    zsend[slot, n, h, pl.ds(pl.multiple_of(t * rows, 16), rows), :] = total[:, n * GK : (n + 1) * GK]
                return 0

            lax.fori_loop(0, halves, multiply, 0)

        half(0)

        @pl.when(had(p, 1))
        def _():
            half(1)

    def finish_group(p):
        slot = lax.rem(p, zslots)
        members = [order(p * group + n) for n in range(group)]

        def first(h):
            for n, (d, k, g) in enumerate(members):
                fetch_half(n, h, d, k, g)

        def second(h):
            for n, (d, k, g) in enumerate(members):
                finish_half(slot, n, h, d, k, g)

        first(0)

        @pl.when(had(p, 1))
        def _():
            first(1)

        second(0)

        @pl.when(had(p, 1))
        def _():
            for n, (d, k, g) in enumerate(members):

                @pl.when(helper & (rank(d, k) < handed))
                def _():
                    take_far(n, far_g.at[0], far_g.at[1], 0)

                    def more(t, _):
                        right = jnp.concatenate([far_g[0], far_g[1]], axis=0)
                        both = dot(e3[t, pl.ds(0, rows)], right, NT)
                        total = both[:, :GK] + both[:, GK:] + dot(e3[t, pl.ds(rows, rows)], far_g[0], NT)
                        zsend[slot, n, 1, pl.ds(pl.multiple_of(t * rows, 16), rows), :] += total
                        return 0

                    lax.fori_loop(0, halves, more, 0)

            second(1)

    def fetch(land, index, number, n, h):
        place = land.at[index, pl.ds(h * (C // 2), C // 2)]
        pltpu.make_async_copy(place, place, z_recv.at[number, h]).wait()
        copy = pltpu.make_async_copy(place, zst.at[n, h], zst_sem.at[n, h])
        copy.start()
        return copy

    def from_behind(h, d, k):
        comes = ((d >= z) & (z > 0)) | ((d < z) & (z < planes - 1))
        if h == 0:
            return comes
        from_end = ((z == 1) & (d >= z)) | ((z == planes - 2) & (d < z))
        return comes & jnp.logical_not(helper & from_end & (rank(d, k) < handed))

    def from_front(h, d, k):
        comes = (d == z) & (z < planes - 1)
        if h == 0:
            return comes
        return comes & jnp.logical_not(helper & (z == planes - 2) & (rank(d, k) < handed))

    def fetch_half(n, h, d, k, g):
        @pl.when(from_behind(h, d, k))
        def _():
            fetch(zland, g, g, n, h)

    def finish_half(slot, n, h, d, k, g):
        def add():
            pltpu.make_async_copy(zst.at[n, h], zst.at[n, h], zst_sem.at[n, h]).wait()

            def one(t, _):
                place = pl.ds(pl.multiple_of(t * rows, 16), rows)
                zsend[slot, n, h, place, :] += zst[n, h, place, :]
                return 0

            lax.fori_loop(0, halves, one, 0)

        @pl.when(from_behind(h, d, k))
        def _():
            add()

        @pl.when(from_front(h, d, k))
        def _():
            fetch(zlast, k, chunks + k, n, h)
            add()

        @pl.when(d > z)
        def _():
            z_copy(zland, g, g, slot, n, h, jnp.minimum(z + 1, planes - 1)).start()

        @pl.when(d < z - 1)
        def _():
            z_copy(zland, g, g, slot, n, h, jnp.maximum(z - 1, 0)).start()

        @pl.when(d == z - 1)
        def _():
            z_copy(zlast, k, chunks + k, slot, n, h, jnp.maximum(z - 1, 0)).start()

        @pl.when(d == z)
        def _():
            place = pl.ds(h * (C // 2), C // 2), pl.ds(pl.multiple_of(k * GK, 128), GK)
            pltpu.make_async_copy(zsend.at[slot, n, h], grad_expr.at[place], zs_sem.at[slot, n, h]).start()

    def tile_of(j):
        t, n = lax.div(j, tiles), lax.rem(j, tiles)
        return grad_logits.at[pl.ds(pl.multiple_of(t * rows, 8), rows), pl.ds(pl.multiple_of(n * tile, 128), tile)]

    def out_copy(j):
        return pltpu.make_async_copy(outst.at[lax.rem(j, 2)], tile_of(j), out_sem.at[lax.rem(j, 2)])

    def in_copy(j):
        return pltpu.make_async_copy(tile_of(j), inst.at[lax.rem(j, 2)], in_sem.at[lax.rem(j, 2)])

    def map_part(j, first, last):
        t, place = lax.div(j, tiles), pl.ds(pl.multiple_of(lax.rem(j, tiles) * tile, 128), tile)
        genes = pl.ds(first * GK, (last - first) * GK)
        both = dot(x2[t, :, genes], gph[genes, place])
        return both[:rows] + both[rows:] + dot(x2[t, pl.ds(0, rows), genes], gpl[genes, place])

    def stored_part(j, stage):
        slot = lax.rem(j, 2)

        @pl.when(j >= 2)
        def _():
            out_copy(j - 2).wait()

        if stage > 0:

            @pl.when(j + 1 < count)
            def _():
                in_copy(j + 1).start()

        total = map_part(j, cuts[stage], cuts[stage + 1])
        if stage == last:
            t, place = lax.div(j, tiles), pl.ds(pl.multiple_of(lax.rem(j, tiles) * tile, 128), tile)
            scale = weight[pl.ds(pl.multiple_of(t * rows, 8), rows), 0:1]
            total = total + (scale * cols[0:1, place] - cols[1:2, place])
        if stage > 0:
            in_copy(j).wait()
            total = total + inst[slot]
        if stage == last:
            exponent = e2[t, pl.ds(0, rows), place].astype(F32) + e2[t, pl.ds(rows, rows), place].astype(F32)
            total = exponent * total
        outst[slot] = total
        out_copy(j).start()

    ends = [0] + [group - 1 + 2 * group * p for p in range(1, groups)]
    finishes = [4 + group + 2 * group * p for p in range(groups)]
    makes = [max((p + 1) * group - 1, finishes[p - zslots] + 5 if p >= zslots else 0) for p in range(groups)]
    makes = finishes

    def at(t, of_ends, of_others):
        p = jnp.int32(-1)
        for n in range(groups):
            p = jnp.where(t == jnp.where(at_end, of_ends[n], of_others[n]), n, p)
        return p

    def step(t, _):
        def hops(firsts, seconds):
            for i in firsts:
                first_own(order(i)[2])
            for i in seconds:
                second_own(order(i)[2])

        @pl.when(t == 0)
        def _():
            hops((0, 1), ())
            for i in range(2, ahead + 1):
                announce(i)
            hops((), (0, 1))
            stage_own(order(0)[2], 0)
            stage_own(order(1)[2], 1)

        @pl.when(t == 1)
        def _():
            hops((2, 3), (2,))

        @pl.when(t == 2)
        def _():
            hops((4, 5), (3, 4))

        @pl.when((t >= 3) & (t + 3 < chunks))
        def _():
            first_own(order(t + 3)[2])

        @pl.when((t >= 3) & (t + 2 < chunks))
        def _():
            second_own(order(t + 2)[2])

        @pl.when((t >= 1) & (t + 1 < chunks))
        def _():
            stage_own(order(t + 1)[2], lax.rem(t + 1, 2))

        @pl.when((t >= 1) & (t + ahead < chunks))
        def _():
            announce(t + ahead)

        @pl.when(lax.rem(t, 2) == 0)
        def _():
            far_step(lax.div(t, 2), ask_far)

            @pl.when(t >= 2)
            def _():
                far_step(lax.div(t - 2, 2), first_far)

        @pl.when((t >= 3) & (lax.rem(t, 2) == 1))
        def _():
            far_step(lax.div(t - 3, 2), second_far)

        soon = at(t + 1, [-1] * groups, finishes)

        @pl.when(helper & (soon >= 0))
        def _():
            for n in range(group):
                d, k, _ = order(soon * group + n)
                far_step(rank(d, k), lambda m, n=n: stage_far(m, n))

        @pl.when((t < chunks) & (t != 1))
        def _():
            take_own(lax.rem(t, 2), gph, gpl, t * GK)

        @pl.when(t == 0)
        def _():
            take_own(1, gph, gpl, GK)
            for n in range(parts):
                for copy in e_copy(n):
                    copy.wait()
            lax.fori_loop(0, chunks, load_x, 0)

        p = at(t, ends, makes)

        @pl.when(p >= 0)
        def _():
            multiply_group(p)

        q = at(t, ends, finishes)

        @pl.when(q >= 0)
        def _():
            finish_group(q)

        @pl.when((t == 2) & helper)
        def _():
            far_exponentials()

        @pl.when(t == cuts[1])
        def _():
            pltpu.make_async_copy(xparts, x2, x_sem).wait()
            total = collect(mine, vecr, vec_send, vec_recv, c, cells, in_plane)
            spot_sum = collect(loss, lossr, loss_send, loss_recv, z, planes, in_column)
            weight[...] = jnp.broadcast_to(counts[...].astype(F32), (128, C)).T
            cols[0:1, :] = vec[8:9, :]
            cols[1:2, :] = total[0:1, :] + vec[9:10, :]
            losses[...] = jnp.zeros_like(losses)
            losses[0:1, :] = loss[2:3, :] - total[1:2, 0:128] / G - spot_sum[0:1, :] / loss[1:2, :]

        for stage in range(last + 1):
            begin = cuts[stage + 1]
            steps = cuts[stage + 2] - begin if stage < last else count
            each = -(-count // steps)

            @pl.when((t >= begin) & (t < begin + steps))
            def _():
                if stage > 0:

                    @pl.when(t == begin)
                    def _():
                        for j in range(count - 2, count):
                            out_copy(j).wait()
                        in_copy(0).start()

                def one(j, _):
                    stored_part(j, stage)
                    return 0

                lax.fori_loop(
                    jnp.minimum((t - begin) * each, count), jnp.minimum((t - begin + 1) * each, count), one, 0
                )

        return 0

    lax.fori_loop(0, slots, step, 0)

    for p in range(groups - zslots, groups):
        for h in range(2):

            @pl.when(had(p, h))
            def _():
                for n in range(group):
                    sent(p % zslots, n, h)

    for j in range(count - 2, count):
        out_copy(j).wait()

    def drain(g, _):
        n = rank(lax.div(g, per), lax.rem(g, per))
        drain_own(g)

        @pl.when(helper & (n < handed))
        def _():
            drain_far(n)

        @pl.when(at_end & (n < handed))
        def _():
            row_copy(n, g).wait_send()

        return 0

    lax.fori_loop(0, chunks, drain, 0)


def backward(cfg, ehi, elo, xparts, far_logits, vec, loss, counts, gp, spent):
    cells, planes, C, S, G, GK, r = (cfg[k] for k in ("cells", "planes", "C", "S", "G", "GK", "r"))
    chips, per, chunks = cells // 2, G // planes // GK, G // GK
    parts, tile, group, zslots = cfg["parts"], cfg["tile"], cfg["group"], cfg["zslots"]
    rows, handed = C // parts, cfg["handed"]
    sem = pltpu.SemaphoreType.DMA
    scratch = [
        pltpu.VMEM((parts, 2 * rows, S), BF16), pltpu.VMEM((parts, 2 * rows, G), BF16),
        pltpu.VMEM((parts // 2, 2 * rows, S), BF16),
        pltpu.VMEM((G, S), BF16), pltpu.VMEM((G, S), BF16), pltpu.VMEM((2, GK, S), BF16),
        pltpu.VMEM((2, chips, 2, r, S), F32), pltpu.VMEM((group, chips, 2, r, S), F32),
        pltpu.VMEM((2, cfg["piece"], S), F32), pltpu.VMEM((group, 2, C // 2, GK), F32),
        pltpu.VMEM((zslots, group, 2, C // 2, GK), F32), pltpu.VMEM((2, rows, tile), F32), pltpu.VMEM((2, rows, tile), F32),
        pltpu.VMEM((8, S), F32), pltpu.VMEM((cells, 8, S), F32), pltpu.VMEM((planes, 8, 128), F32), pltpu.VMEM((C, 128), F32),
        sem((2, parts)), sem, sem((2,)), sem((chunks, chips)), sem((chunks,)), sem((chunks, 2)),
        sem((handed, chips)), sem((handed,)), sem((handed, 2)),
        sem((handed,)), sem((handed,)), sem((2,)), sem((group,)),
        sem((chunks + per, 2)), sem((zslots, group, 2)), sem((group, 2)), sem((2,)), sem((2,)),
        sem((cells,)), sem((cells,)), sem((planes,)), sem((planes,)),
    ]
    return pl.pallas_call(
        functools.partial(backward_kernel, cfg),
        out_shape=(
            jax.ShapeDtypeStruct((C, S), F32),
            jax.ShapeDtypeStruct((C, G // planes), F32),
            jax.ShapeDtypeStruct((8, 128), F32),
            jax.ShapeDtypeStruct((chunks, chips, 2, r, S), F32),
            jax.ShapeDtypeStruct((cfg["handed"], chips, 2, r, S), F32),
            jax.ShapeDtypeStruct((chunks, C, GK), F32),
            jax.ShapeDtypeStruct((per, C, GK), F32),
        ),
        in_specs=[ANY, ANY, ANY, ANY, VMEM, VMEM, VMEM, ANY, ANY],
        out_specs=(ANY, ANY, VMEM, ANY, ANY, ANY, ANY),
        input_output_aliases={7: 3, 8: 5},
        scratch_shapes=scratch,
        compiler_params=pltpu.CompilerParams(
            collective_id=1, has_side_effects=True, vmem_limit_bytes=61 * 2**20
        ),
        cost_estimate=pl.CostEstimate(flops=12 * C * S * G, bytes_accessed=16 * C * S, transcendentals=0),
        name="backward",
    )(ehi, elo, xparts, far_logits, vec, loss, counts, gp, spent)


def local(cells, planes, logits, expression, spatial, cell_counts, spot_density, slide_id, padding):
    C, S = logits.shape
    G = expression.shape[1] * planes
    GK = max(128, 8 * cells)
    chunks, parts, group = G // GK, 4, 256 // GK
    tile = 256 * group
    across = 1
    while across * across < cells // 2:
        across *= 2
    cfg = dict(
        cells=cells, planes=planes, C=C, S=S, G=G, GK=GK, r=GK // cells, rows=128, tile=tile, parts=parts,
        group=group, zslots=1 + group, slots=max(chunks + parts * (S // tile), 5 + group + 2 * (chunks - group)), pieces=8, ahead=5, handed=chunks // 4,
        across=across, helped=planes >= 4, piece=max(n for n in range(16, 65, 16) if C // parts % n == 0),
    )
    counts = cell_counts[None, :]
    gath, ehi, elo, xparts, far_logits, gp, vec, loss = forward(
        cfg, logits, expression, spatial, counts, spot_density[None, :],
        slide_id[None, :], padding[None, :],
    )
    grad_logits, grad_expression, losses, *_ = backward(
        cfg, ehi, elo, xparts, far_logits, vec, loss, counts, gp, gath
    )
    return (losses[0, :2], grad_logits, grad_expression)


def solution(mesh):
    cells, planes = mesh.shape["cell"], mesh.shape["spot"]
    in_specs = (
        P("cell", "spot"), P("cell", "spot"), P("cell", "spot"), P("cell"), P("spot"), P("spot"), P("spot"),
    )
    out_specs = (P(), P("cell", "spot"), P("cell", "spot"))
    return jax.shard_map(
        functools.partial(local, cells, planes), mesh=mesh, in_specs=in_specs, out_specs=out_specs, check_vma=False
    )
```

```python
import functools

import jax
import jax.numpy as jnp
from jax import lax
from jax.experimental import pallas as pl
from jax.experimental.pallas import tpu as pltpu
from jax.sharding import PartitionSpec as P

epsilon = 1e-06
MESH = pl.DeviceIdType.MESH
F32, BF16 = jnp.float32, jnp.bfloat16
TN = (((0,), (0,)), ((), ()))
NN = (((1,), (0,)), ((), ()))
NT = (((1,), (1,)), ((), ()))


def dot(left, right, dims=NN):
    return lax.dot_general(left, right, dims, preferred_element_type=F32)


def split(v):
    high = v.astype(BF16)
    return high, (v - high.astype(F32)).astype(BF16)


def arrival(z, i, planes, per):
    near = jnp.minimum(z, planes - 1 - z)
    j = jnp.maximum(i - per, 0)
    pair = lax.rem(j, 2 * per)
    t = 1 + lax.div(j, 2 * per)
    both = jnp.where(lax.rem(pair, 2) == 0, z - t, z + t)
    late = jnp.maximum(j - 2 * near * per, 0)
    t = near + 1 + lax.div(late, per)
    one = jnp.where(z < planes - 1 - z, z + t, z - t)
    in_pairs = j < 2 * near * per
    shard = jnp.where(i < per, z, jnp.where(in_pairs, both, one))
    chunk = jnp.where(i < per, i, jnp.where(in_pairs, lax.div(pair, 2), lax.rem(late, per)))
    return shard, chunk


def greet(c, z, cells, planes):
    barrier = pltpu.get_barrier_semaphore()

    def in_plane(step, _):
        pl.semaphore_signal(barrier, inc=1, device_id=(lax.rem(c + step, cells), z), device_id_type=MESH)
        return 0

    def in_column(step, _):
        pl.semaphore_signal(barrier, inc=1, device_id=(c, lax.rem(z + step, planes)), device_id_type=MESH)
        return 0

    lax.fori_loop(1, cells, in_plane, 0)
    lax.fori_loop(1, planes, in_column, 0)
    pl.semaphore_wait(barrier, cells + planes - 2)


def share(src, dst, send, recv, me, count, device):
    def start(step, _):
        other = lax.rem(me + step, count)
        pltpu.make_async_remote_copy(
            src_ref=src, dst_ref=dst.at[me], send_sem=send.at[other], recv_sem=recv.at[me],
            device_id=device(other), device_id_type=MESH,
        ).start()
        return 0

    lax.fori_loop(1, count, start, 0)


def collect(src, dst, send, recv, me, count, device):
    def wait(step, total):
        other = lax.rem(me + step, count)
        copy = pltpu.make_async_remote_copy(
            src_ref=src, dst_ref=dst.at[other], send_sem=send.at[other], recv_sem=recv.at[other],
            device_id=device(other), device_id_type=MESH,
        )
        copy.wait_send()
        copy.wait_recv()
        return total + dst[other]

    return lax.fori_loop(1, count, wait, src[...])


def forward_kernel(
    cfg, logits, expr, spatial, counts, dens, slide, pad,
    gath, ehi_out, elo_out, x_out, far_logits, gp_out, vec_out, loss_out,
    ehi, elo, lbuf, stage, xparts, amat, partial, corer, half, chipr, pred, spat,
    tots, totr, acc, spots, spotr, gcol, gst, gstr, vec,
    g_recv, up_send, down_send, l_sem, st_sem, put_sem, core_send, core_recv, chip_send, chip_recv,
    far_send, far_recv, spat_send, spat_recv, tot_send, tot_recv, spot_send, spot_recv, gst_send, gst_recv, out_sem,
):
    cells, planes, C, S, G, GK, r = (cfg[k] for k in ("cells", "planes", "C", "S", "G", "GK", "r"))
    chips, per, chunks = cells // 2, G // planes // GK, G // GK
    rows, tile, parts, helped = cfg["rows"], cfg["tile"], cfg["parts"], cfg["helped"]
    part, pieces = C // parts, cfg["pieces"]
    own_genes = G // cells
    c, z = lax.axis_index("cell"), lax.axis_index("spot")
    chip, core = lax.div(c, 2), lax.rem(c, 2)
    sibling = c + 1 - 2 * core
    in_plane = lambda other: (other, z)
    in_column = lambda other: (c, other)

    greet(c, z, cells, planes)

    def z_copy(src, g, to, send):
        return pltpu.make_async_remote_copy(
            src_ref=src, dst_ref=gath.at[g], send_sem=send.at[g], recv_sem=g_recv.at[g],
            device_id=(c, to), device_id_type=MESH,
        )

    up, down = jnp.minimum(z + 1, planes - 1), jnp.maximum(z - 1, 0)

    def send_own(k, _):
        g = z * per + k
        src = expr.at[:, pl.ds(pl.multiple_of(k * GK, 128), GK)]

        @pl.when(z < planes - 1)
        def _():
            z_copy(src, g, up, up_send).start()

        @pl.when(z > 0)
        def _():
            z_copy(src, g, down, down_send).start()

        return 0

    lax.fori_loop(0, per, send_own, 0)

    at_end = (z == 0) | (z == planes - 1)
    helper = ((z == 1) | (z == planes - 2)) & helped
    beside = jnp.where(z == 0, 1, jnp.where(z == planes - 1, planes - 2, jnp.where(z == 1, 0, planes - 1)))
    piece = C // 2 // pieces

    def far_copy(n):
        return pltpu.make_async_remote_copy(
            src_ref=logits.at[pl.ds(pl.multiple_of(C // 2 + n * piece, 8), piece)],
            dst_ref=far_logits.at[pl.ds(pl.multiple_of(n * piece, 8), piece)],
            send_sem=far_send.at[n], recv_sem=far_recv.at[n], device_id=(c, beside), device_id_type=MESH,
        )

    blocks = own_genes // r

    def spat_copy(b):
        place = c * blocks + b
        g, owner = lax.div(place, cells), lax.rem(place, cells)
        src = spatial.at[pl.ds(pl.multiple_of(b * r, 8), r)]
        remote = pltpu.make_async_remote_copy(
            src_ref=src, dst_ref=spat.at[g], send_sem=spat_send.at[b], recv_sem=spat_recv.at[g],
            device_id=(owner, z), device_id_type=MESH,
        )
        local = pltpu.make_async_copy(src, spat.at[g], spat_recv.at[g])
        return owner, remote, local

    def send_spat(b, _):
        owner, remote, local = spat_copy(b)

        @pl.when(owner != c)
        def _():
            remote.start()

        @pl.when(owner == c)
        def _():
            local.start()

        return 0

    lax.fori_loop(0, blocks, send_spat, 0)

    def load(t):
        return pltpu.make_async_copy(
            logits.at[pl.ds(pl.multiple_of(t * rows, rows), rows)], lbuf.at[lax.rem(t, 2)], l_sem.at[lax.rem(t, 2)]
        )

    load(0).start()

    def exps(t, _):
        @pl.when(t + 1 < C // rows)
        def _():
            load(t + 1).start()

        load(t).wait()
        high, low = split(jnp.exp(lbuf[lax.rem(t, 2)]))
        place = pl.ds(pl.multiple_of(t * rows, rows), rows)
        ehi[place, :] = high
        elo[place, :] = low
        return 0

    lax.fori_loop(0, C // rows, exps, 0)
    keep = [pltpu.make_async_copy(ehi, ehi_out, out_sem.at[0]), pltpu.make_async_copy(elo, elo_out, out_sem.at[1])]
    for copy in keep:
        copy.start()

    row = lax.broadcasted_iota(jnp.int32, (16, C), 0)
    weight = jnp.broadcast_to(counts[...].astype(F32)[None, :], (16, C))
    lhs = jnp.where(row == 0, 1.0, jnp.where(row == 1, weight, 0.0)).astype(BF16)

    def sums(t, _):
        place = pl.ds(pl.multiple_of(t * tile, tile), tile)
        both = dot(lhs, ehi[:, place]) + dot(lhs, elo[:, place])
        tots[:, place] = both[:8]
        return 0

    lax.fori_loop(0, S // tile, sums, 0)
    share(tots, totr, tot_send, tot_recv, c, cells, in_plane)

    valid = (1 - pad[...]).astype(F32)
    mask0 = valid * (slide[...] == 0).astype(F32)
    mask1 = valid * (slide[...] == 1).astype(F32)
    vec[4:5, :] = mask0
    vec[5:6, :] = mask1
    acc[...] = jnp.zeros_like(acc)
    gcol[...] = jnp.zeros_like(gcol)

    def core_copy(g, slot):
        return pltpu.make_async_remote_copy(
            src_ref=partial.at[slot, :, 1 - core], dst_ref=corer.at[g], send_sem=core_send.at[slot],
            recv_sem=core_recv.at[g], device_id=(sibling, z), device_id_type=MESH,
        )

    def chip_copy(g, slot, other):
        return pltpu.make_async_remote_copy(
            src_ref=half.at[slot, other], dst_ref=chipr.at[g, chip], send_sem=chip_send.at[slot, other],
            recv_sem=chip_recv.at[g, chip], device_id=(2 * other + core, z), device_id_type=MESH,
        )

    def chip_wait(g, slot, other):
        return pltpu.make_async_remote_copy(
            src_ref=half.at[slot, chip], dst_ref=chipr.at[g, other], send_sem=chip_send.at[slot, other],
            recv_sem=chip_recv.at[g, other], device_id=(2 * other + core, z), device_id_type=MESH,
        )

    def product(i):
        d, k = arrival(z, i, planes, per)
        g, slot = d * per + k, lax.rem(i, 2)
        own = pltpu.make_async_copy(expr.at[:, pl.ds(pl.multiple_of(k * GK, 128), GK)], stage, st_sem)
        pull = pltpu.make_async_copy(gath.at[g], stage, st_sem)

        @pl.when(d == z)
        def _():
            own.start()

        @pl.when(d != z)
        def _():
            z_copy(gath.at[g], g, down, down_send).wait_recv()

        @pl.when((d < z) & (z < planes - 1))
        def _():
            z_copy(gath.at[g], g, up, up_send).start()

        @pl.when((d > z) & (z > 0))
        def _():
            z_copy(gath.at[g], g, down, down_send).start()

        @pl.when(d != z)
        def _():
            pull.start()

        pull.wait()
        columns = pl.ds(pl.multiple_of(g * GK, 128), GK)

        @pl.when(i >= 1)
        def _():
            pltpu.make_async_copy(xparts, x_out.at[:, :, columns], put_sem).wait()

        def keep_parts(t, _):
            high, low = split(stage[pl.ds(pl.multiple_of(t * part, 16), part), :])
            xparts[t, pl.ds(0, part), :] = high
            xparts[t, pl.ds(part, part), :] = low
            return 0

        lax.fori_loop(0, parts, keep_parts, 0)
        pltpu.make_async_copy(xparts, x_out.at[:, :, columns], put_sem).start()

        @pl.when(i >= 2)
        def _():
            core_copy(g, slot).wait_send()

        def turn(t, _):
            place = pl.ds(pl.multiple_of(t * 128, 128), 128)
            high, low = split(stage[place, :].T)
            amat[:GK, place] = high
            amat[GK:, place] = low
            return 0

        lax.fori_loop(0, C // 128, turn, 0)

        def multiply(t, _):
            place = pl.ds(pl.multiple_of(t * tile, tile), tile)
            both = dot(amat[...], ehi[:, place])
            total = both[:GK] + both[GK:] + dot(amat[:GK, :], elo[:, place])
            partial[slot, :, :, :, place] = total.reshape(chips, 2, r, tile)
            return 0

        lax.fori_loop(0, S // tile, multiply, 0)
        core_copy(g, slot).start()

    def to_chips(i):
        d, k = arrival(z, i, planes, per)
        g, slot = d * per + k, lax.rem(i, 2)
        core_copy(g, slot).wait_recv()

        @pl.when(i >= 2)
        def _():
            def drain(step, _):
                chip_copy(g, slot, lax.rem(chip + step, chips)).wait_send()
                return 0

            lax.fori_loop(1, chips, drain, 0)

        def add(other, _):
            half[slot, other] = partial[slot, other, core] + corer[g, other]

            @pl.when(other != chip)
            def _():
                chip_copy(g, slot, other).start()

            return 0

        lax.fori_loop(0, chips, add, 0)

    def finish(i):
        d, k = arrival(z, i, planes, per)
        g, slot = d * per + k, lax.rem(i, 2)
        pltpu.make_async_copy(spat.at[g], spat.at[g], spat_recv.at[g]).wait()

        def add(step, total):
            other = lax.rem(chip + step, chips)
            chip_wait(g, slot, other).wait_recv()
            return total + chipr[g, other]

        p = lax.fori_loop(1, chips, add, half[slot, chip]) * vec[0:1, :]
        s = spat[g]
        pred[g] = p
        ps, pp, ss = p * s, p * p, s * s
        acc[0] += ps
        acc[1] += pp
        acc[2] += ss
        lane = lax.broadcasted_iota(jnp.int32, (r, 128), 1)
        cols = jnp.zeros((r, 128), F32)
        for n, v in enumerate((ps, pp, ss)):
            for m in range(2):
                one = jnp.sum(v * vec[4 + m : 5 + m, :], axis=1, keepdims=True)
                cols = jnp.where(lane == 2 * n + m, one, cols)
        gcol[pl.ds(pl.multiple_of(g * r, 8), r), :] = cols

    def step(i, _):
        @pl.when((i >= per) & (i < per + pieces) & at_end & helped)
        def _():
            far_copy(i - per).start()

        @pl.when(i < chunks)
        def _():
            product(i)

        @pl.when(i == 1)
        def _():
            total = collect(tots, totr, tot_send, tot_recv, c, cells, in_plane)
            vec[0:1, :] = 1.0 / total[0:1, :]
            vec[1:2, :] = total[1:2, :] / total[0:1, :]

        @pl.when((i >= 1) & (i <= chunks))
        def _():
            to_chips(i - 1)

        @pl.when(i >= 2)
        def _():
            finish(i - 2)

        return 0

    lax.fori_loop(0, chunks + 2, step, 0)

    spots[...] = jnp.zeros_like(spots)
    for n in range(3):
        spots[n : n + 1, :] = jnp.sum(acc[n], axis=0, keepdims=True)
    share(spots, spotr, spot_send, spot_recv, c, cells, in_plane)
    gst[...] = jnp.zeros_like(gst)
    gst[0:8, :] = gcol[...].T[0:8, :]
    density = vec[1:2, :]
    target = dens[...]
    lane = lax.broadcasted_iota(jnp.int32, (1, gst.shape[1]), 1)
    logs = target * jnp.log(target), target * jnp.log(density)
    for n, v in enumerate((jnp.ones_like(target), target, density, *logs)):
        line = jnp.zeros((1, gst.shape[1]), F32)
        for m in range(2):
            one = jnp.sum(v * vec[4 + m : 5 + m, :], axis=1, keepdims=True)
            line = jnp.where(lane == m, one, line)
        gst[8 + n : 9 + n, :] = line
    share(gst, gstr, gst_send, gst_recv, z, planes, in_column)

    genes = collect(gst, gstr, gst_send, gst_recv, z, planes, in_column)
    dot_g, aa_g, bb_g = ([genes[2 * n + m : 2 * n + m + 1, :] for m in range(2)] for n in range(3))
    slides = [[genes[8 + n : 9 + n, m : m + 1] for m in range(2)] for n in range(5)]
    lines, cos_sums, own_losses = [], [], []
    for m in range(2):
        norm = jnp.sqrt((aa_g[m] + epsilon) * (bb_g[m] + epsilon))
        cos = dot_g[m] / norm
        lines += [-1.0 / (norm * G), cos / ((aa_g[m] + epsilon) * G)]
        cos_sums.append(jnp.sum(cos, axis=1, keepdims=True))
    lines.append(jnp.zeros((124, gst.shape[1]), F32))
    gcol[...] = jnp.concatenate(lines, axis=0).T
    live = [jnp.maximum(v, 1.0) for v in slides[0]]
    mass_target, mass_pred = slides[1], slides[2]
    divergence = [
        (slides[3][m] - slides[4][m]) / mass_target[m] - jnp.log(mass_target[m]) + jnp.log(mass_pred[m])
        for m in range(2)
    ]
    mask0, mask1 = vec[4:5, :], vec[5:6, :]
    grad_density = (
        mask0 / mass_pred[0] + mask1 / mass_pred[1]
        - dens[...] * (mask0 / mass_target[0] + mask1 / mass_target[1]) / vec[1:2, :]
    )
    spot_weight = mask0 / live[0] + mask1 / live[1]

    spot = collect(spots, spotr, spot_send, spot_recv, c, cells, in_plane)
    norm = jnp.sqrt((spot[1:2, :] + epsilon) * (spot[2:3, :] + epsilon))
    spot_cos = spot[0:1, :] / norm
    inverse = vec[0:1, :]
    vec[2:3, :] = -spot_weight / norm
    vec[3:4, :] = spot_weight * spot_cos / (spot[1:2, :] + epsilon)
    vec[6:7, :] = grad_density * inverse
    vec[7:8, :] = vec[1:2, :] * grad_density * inverse
    acc[0] = jnp.zeros((r, S), F32)

    def gradient(g, _):
        columns = gcol[pl.ds(pl.multiple_of(g * r, 8), r), :]
        by_spatial = vec[4:5, :] * columns[:, 0:1] + vec[5:6, :] * columns[:, 2:3] + vec[2:3, :]
        by_pred = vec[4:5, :] * columns[:, 1:2] + vec[5:6, :] * columns[:, 3:4] + vec[3:4, :]
        p = pred[g]
        value = (spat[g] * by_spatial + p * by_pred) * vec[0:1, :]
        acc[0] += p * value
        pred[g] = value
        return 0

    lax.fori_loop(0, chunks, gradient, 0)
    copy = pltpu.make_async_copy(pred, gp_out.at[:, chip, core], out_sem.at[2])
    copy.start()
    vec_out[...] = jnp.zeros_like(vec_out)
    vec_out[0:1, :] = jnp.sum(acc[0], axis=0, keepdims=True)
    vec_out[8:9, :] = vec[6:7, :]
    vec_out[9:10, :] = vec[7:8, :]
    lane = lax.broadcasted_iota(jnp.int32, (1, 128), 1)
    vec_out[1:2, 0:128] = jnp.where(lane == 0, cos_sums[0], jnp.where(lane == 1, cos_sums[1], 0.0))
    spot_sums = [jnp.sum(vec[4 + m : 5 + m, :] * spot_cos, axis=1, keepdims=True) for m in range(2)]
    loss_out[...] = jnp.zeros_like(loss_out)
    for n, v in enumerate((spot_sums, live, divergence)):
        loss_out[n : n + 1, :] = jnp.where(lane == 0, v[0], jnp.where(lane == 1, v[1], 0.0))

    copy.wait()
    for copy in keep:
        copy.wait()
    pltpu.make_async_copy(xparts, x_out.at[:, :, pl.ds(0, GK)], put_sem).wait()

    def drain_far(n, _):
        @pl.when(at_end & helped)
        def _():
            far_copy(n).wait_send()

        @pl.when(helper)
        def _():
            far_copy(n).wait_recv()

        return 0

    lax.fori_loop(0, pieces, drain_far, 0)

    def drain_z(g, _):
        d = lax.div(g, per)

        @pl.when((d <= z) & (z < planes - 1))
        def _():
            z_copy(gath.at[g], g, up, up_send).wait_send()

        @pl.when((d >= z) & (z > 0))
        def _():
            z_copy(gath.at[g], g, down, down_send).wait_send()

        return 0

    lax.fori_loop(0, chunks, drain_z, 0)

    def drain_spat(b, _):
        owner, remote, _ = spat_copy(b)

        @pl.when(owner != c)
        def _():
            remote.wait_send()

        return 0

    lax.fori_loop(0, blocks, drain_spat, 0)
    for slot in range(2):
        core_copy(0, slot).wait_send()

        def drain(step, _):
            chip_copy(0, slot, lax.rem(chip + step, chips)).wait_send()
            return 0

        lax.fori_loop(1, chips, drain, 0)


ANY = pl.BlockSpec(memory_space=pl.ANY)
VMEM = pl.BlockSpec(memory_space=pltpu.VMEM)


def forward(cfg, logits, expression, spatial, counts, dens, slide, pad):
    cells, planes, C, S, G, GK, r = (cfg[k] for k in ("cells", "planes", "C", "S", "G", "GK", "r"))
    chips, per, chunks = cells // 2, G // planes // GK, G // GK
    rows = cfg["rows"]
    wide = max(G // cells, 128)
    blocks = G // cells // r
    sem = pltpu.SemaphoreType.DMA
    scratch = [
        pltpu.VMEM((C, S), BF16), pltpu.VMEM((C, S), BF16), pltpu.VMEM((2, rows, S), F32),
        pltpu.VMEM((C, GK), F32), pltpu.VMEM((cfg["parts"], 2 * C // cfg["parts"], GK), BF16), pltpu.VMEM((2 * GK, C), BF16),
        pltpu.VMEM((2, chips, 2, r, S), F32), pltpu.VMEM((chunks, chips, r, S), F32),
        pltpu.VMEM((2, chips, r, S), F32), pltpu.VMEM((chunks, chips, r, S), F32),
        pltpu.VMEM((chunks, r, S), F32), pltpu.VMEM((chunks, r, S), F32),
        pltpu.VMEM((8, S), F32), pltpu.VMEM((cells, 8, S), F32), pltpu.VMEM((3, r, S), F32),
        pltpu.VMEM((8, S), F32), pltpu.VMEM((cells, 8, S), F32), pltpu.VMEM((wide, 128), F32),
        pltpu.VMEM((16, wide), F32), pltpu.VMEM((planes, 16, wide), F32), pltpu.VMEM((8, S), F32),
        sem((chunks,)), sem((chunks,)), sem((chunks,)), sem((2,)), sem, sem,
        sem((2,)), sem((chunks,)), sem((2, chips)), sem((chunks, chips)),
        sem((cfg["pieces"],)), sem((cfg["pieces"],)),
        sem((blocks,)), sem((chunks,)), sem((cells,)), sem((cells,)), sem((cells,)), sem((cells,)),
        sem((planes,)), sem((planes,)), sem((3,)),
    ]
    flops = 6 * C * S * G
    return pl.pallas_call(
        functools.partial(forward_kernel, cfg),
        out_shape=(
            jax.ShapeDtypeStruct((chunks, C, GK), F32),
            jax.ShapeDtypeStruct((C, S), BF16),
            jax.ShapeDtypeStruct((C, S), BF16),
            jax.ShapeDtypeStruct((cfg["parts"], 2 * C // cfg["parts"], G), BF16),
            jax.ShapeDtypeStruct((C // 2, S), F32),
            jax.ShapeDtypeStruct((chunks, chips, 2, r, S), F32),
            jax.ShapeDtypeStruct((16, S), F32),
            jax.ShapeDtypeStruct((8, 128), F32),
        ),
        in_specs=[ANY, ANY, ANY, VMEM, VMEM, VMEM, VMEM],
        out_specs=(ANY, ANY, ANY, ANY, ANY, ANY, VMEM, VMEM),
        scratch_shapes=scratch,
        compiler_params=pltpu.CompilerParams(
            collective_id=0, has_side_effects=True, vmem_limit_bytes=56 * 2**20
        ),
        cost_estimate=pl.CostEstimate(flops=flops, bytes_accessed=8 * C * S, transcendentals=C * S),
        name="forward",
    )(logits, expression, spatial, counts, dens, slide, pad)


def backward_kernel(
    cfg, ehi, elo, xparts, far_logits, vec, loss, counts, _gp, _gath,
    grad_logits, grad_expr, losses, land, far_land, zland, zlast,
    e2, x2, e3, gph, gpl, far_g, gstage, fstage, lbuf, zst, zsend, outst, inst, cols, vecr, lossr, weight,
    e_sem, x_sem, l_sem, g_recv, g_pair, g_sent, f_recv, f_pair, f_sent, row_recv, row_sent, gs_sem, fs_sem,
    z_recv, zs_sem, zst_sem, out_sem, in_sem, vec_send, vec_recv, loss_send, loss_recv,
):
    cells, planes, C, S, G, GK, r = (cfg[k] for k in ("cells", "planes", "C", "S", "G", "GK", "r"))
    chips, per, chunks = cells // 2, G // planes // GK, G // GK
    parts, tile, slots, group, zslots = (cfg[k] for k in ("parts", "tile", "slots", "group", "zslots"))
    ahead = cfg["ahead"]
    handed = cfg["handed"]
    count, groups = parts * (S // tile), chunks // group
    cuts = (0, chunks // 2, chunks)
    last = len(cuts) - 2
    helped, across = cfg["helped"], cfg["across"]
    rows, tiles, halves = C // parts, S // tile, parts // 2
    piece = cfg["piece"]
    pieces = C // 2 // piece
    down_chips = chips // across
    c, z = lax.axis_index("cell"), lax.axis_index("spot")
    chip, core = lax.div(c, 2), lax.rem(c, 2)
    chip_row, chip_col = lax.div(chip, across), lax.rem(chip, across)
    sibling = c + 1 - 2 * core
    in_plane = lambda other: (other, z)
    in_column = lambda other: (c, other)
    at_end = ((z == 0) | (z == planes - 1)) & helped
    helper = ((z == 1) | (z == planes - 2)) & helped
    beside = jnp.where(z == 0, 1, jnp.where(z == planes - 1, planes - 2, jnp.where(z == 1, 0, planes - 1)))

    def order(i):
        d, k = arrival(z, chunks - 1 - i, planes, per)
        return d, k, d * per + k

    greet(c, z, cells, planes)

    def spread(land, recv, pair, sent, buffer, ready):
        def copy(ref, source, g, other):
            return pltpu.make_async_remote_copy(
                src_ref=ref, dst_ref=ref, send_sem=sent.at[g, 0], recv_sem=recv.at[g, source],
                device_id=(2 * other + core, z), device_id_type=MESH,
            )

        def along_row(n):
            return chip_row * across + lax.rem(chip_col + n, across)

        def along_col(n):
            return lax.rem(chip_row + n, down_chips) * across + chip_col

        def each(count, body):
            def one(n, _):
                body(n)
                return 0

            lax.fori_loop(1, count, one, 0)

        def send(g):
            own = land.at[g, chip, core]
            each(across, lambda n: copy(own, chip, g, along_row(n)).start())
            each(down_chips, lambda n: copy(own, chip, g, along_col(n)).start())

        def landed(g, source):
            ref = land.at[g, source, core]
            pltpu.make_async_copy(ref, ref, recv.at[g, source]).wait()

        def first_hop(g):
            def from_row(n):
                source = along_row(n)
                landed(g, source)
                half = land.at[g, source, core, :, pl.ds(0, S // 2)]
                each(down_chips, lambda m: copy(half, source, g, along_col(m)).start())

            def from_col(n):
                source = along_col(n)
                landed(g, source)
                half = land.at[g, source, core, :, pl.ds(S // 2, S // 2)]
                each(across, lambda m: copy(half, source, g, along_row(m)).start())

            each(across, from_row)
            each(down_chips, from_col)

        def to_sibling(g):
            ref = land.at[g, :, core]
            return pltpu.make_async_remote_copy(
                src_ref=ref, dst_ref=ref, send_sem=sent.at[g, 1], recv_sem=pair.at[g],
                device_id=(sibling, z), device_id_type=MESH,
            )

        def second_hop(g):
            def from_rest(n):
                other = lax.rem(chip_row + 1 + lax.div(n - 1, across - 1), down_chips) * across
                landed(g, other + lax.rem(chip_col + 1 + lax.rem(n - 1, across - 1), across))

            each((across - 1) * (down_chips - 1) + 1, from_rest)
            to_sibling(g).start()

        def stage(g, slot):
            ref = land.at[g, :, 1 - core]
            pltpu.make_async_copy(ref, ref, pair.at[g]).wait()
            pltpu.make_async_copy(land.at[g], buffer.at[slot], ready.at[slot]).start()

        def take(slot, high_ref, low_ref, first):
            pltpu.make_async_copy(buffer.at[slot], buffer.at[slot], ready.at[slot]).wait()

            def split_tile(t, _):
                place = pl.ds(pl.multiple_of(t * 128, 128), 128)
                high, low = split(buffer[slot, :, :, :, place].reshape(GK, 128))
                lines = pl.ds(pl.multiple_of(first, 128), GK)
                high_ref[lines, place] = high
                low_ref[lines, place] = low
                return 0

            lax.fori_loop(0, S // 128, split_tile, 0)

        def drain(g):
            direct = land.at[g, pl.ds(0, chips - 1), 0]
            pltpu.make_async_copy(direct, direct, sent.at[g, 0]).wait()
            to_sibling(g).wait_send()

        return send, first_hop, second_hop, stage, take, drain

    send_own, first_own, second_own, stage_own, take_own, drain_own = spread(
        land, g_recv, g_pair, g_sent, gstage, gs_sem
    )
    send_far, first_far, second_far, stage_far, take_far, drain_far = spread(
        far_land, f_recv, f_pair, f_sent, fstage, fs_sem
    )

    def rank(d, k):
        end = jnp.where(at_end, z, beside)
        return (planes - 1 - jnp.abs(d - end)) * per + per - 1 - k

    def row_copy(n, g):
        return pltpu.make_async_remote_copy(
            src_ref=land.at[g, chip, core], dst_ref=far_land.at[n, chip, core],
            send_sem=row_sent.at[n], recv_sem=row_recv.at[n],
            device_id=(c, beside), device_id_type=MESH,
        )

    def announce(i):
        _, _, g = order(i)
        send_own(g)

        @pl.when(at_end & (i < handed))
        def _():
            row_copy(i, g).start()

    announce(0)
    announce(1)

    def e_copy(t):
        place = pl.ds(pl.multiple_of(t * rows, 16), rows)
        return (
            pltpu.make_async_copy(ehi.at[place], e2.at[t, pl.ds(0, rows)], e_sem.at[0, t]),
            pltpu.make_async_copy(elo.at[place], e2.at[t, pl.ds(rows, rows)], e_sem.at[1, t]),
        )

    for t in range(parts):
        for copy in e_copy(t):
            copy.start()
    def load_x(i, _):
        from_place = pl.ds(pl.multiple_of(order(i)[2] * GK, 128), GK)
        to_place = pl.ds(pl.multiple_of(i * GK, 128), GK)
        pltpu.make_async_copy(xparts.at[:, :, from_place], x2.at[:, :, to_place], x_sem).start()
        return 0

    mine = vec.at[pl.ds(0, 8)]
    share(mine, vecr, vec_send, vec_recv, c, cells, in_plane)
    share(loss, lossr, loss_send, loss_recv, z, planes, in_column)

    def far_exponentials():
        def load(n):
            return pltpu.make_async_copy(
                far_logits.at[pl.ds(pl.multiple_of(n * piece, 8), piece)], lbuf.at[lax.rem(n, 2)], l_sem.at[lax.rem(n, 2)]
            )

        for n in range(2):
            load(n).start()

        def exps(n, _):
            load(n).wait()
            high, low = split(jnp.exp(lbuf[lax.rem(n, 2)]))
            t, place = lax.div(n * piece, rows), lax.rem(n * piece, rows)
            e3[t, pl.ds(pl.multiple_of(place, 16), piece), :] = high
            e3[t, pl.ds(pl.multiple_of(rows + place, 16), piece), :] = low

            @pl.when(n + 2 < pieces)
            def _():
                load(n + 2).start()

            return 0

        lax.fori_loop(0, pieces, exps, 0)

    def far_step(n, what):
        @pl.when(helper & (n < handed))
        def _():
            what(n)

    def ask_far(n):
        row_copy(n, 0).wait_recv()
        send_far(n)

    def z_copy(land, index, number, slot, n, h, to):
        place = pl.ds(h * (C // 2), C // 2)
        return pltpu.make_async_remote_copy(
            src_ref=zsend.at[slot, n, h], dst_ref=land.at[index, place], send_sem=zs_sem.at[slot, n, h],
            recv_sem=z_recv.at[number, h], device_id=(c, to), device_id_type=MESH,
        )

    def sent(slot, n, h):
        pltpu.make_async_copy(zsend.at[slot, n, h], zsend.at[slot, n, h], zs_sem.at[slot, n, h]).wait()

    def had(p, h):
        return True if h == 0 else jnp.logical_not(at_end) | (p * group >= handed)

    def multiply_group(p):
        slot = lax.rem(p, zslots)
        lines = pl.ds(pl.multiple_of(p * group * GK, 128), group * GK)

        def half(h):
            @pl.when((p >= zslots) & had(p - zslots, h))
            def _():
                for n in range(group):
                    sent(slot, n, h)

            def multiply(t, _):
                both = dot(e2[h * halves + t], gph[lines, :], NT)
                total = both[:rows] + both[rows:] + dot(e2[h * halves + t, pl.ds(0, rows)], gpl[lines, :], NT)
                for n in range(group):
                    zsend[slot, n, h, pl.ds(pl.multiple_of(t * rows, 16), rows), :] = total[:, n * GK : (n + 1) * GK]
                return 0

            lax.fori_loop(0, halves, multiply, 0)

        half(0)

        @pl.when(had(p, 1))
        def _():
            half(1)

    def finish_group(p):
        slot = lax.rem(p, zslots)
        members = [order(p * group + n) for n in range(group)]

        def first(h):
            for n, (d, k, g) in enumerate(members):
                fetch_half(n, h, d, k, g)

        def second(h):
            for n, (d, k, g) in enumerate(members):
                finish_half(slot, n, h, d, k, g)

        first(0)

        @pl.when(had(p, 1))
        def _():
            first(1)

        second(0)

        @pl.when(had(p, 1))
        def _():
            for n, (d, k, g) in enumerate(members):

                @pl.when(helper & (rank(d, k) < handed))
                def _():
                    take_far(n, far_g.at[0], far_g.at[1], 0)

                    def more(t, _):
                        right = jnp.concatenate([far_g[0], far_g[1]], axis=0)
                        both = dot(e3[t, pl.ds(0, rows)], right, NT)
                        total = both[:, :GK] + both[:, GK:] + dot(e3[t, pl.ds(rows, rows)], far_g[0], NT)
                        zsend[slot, n, 1, pl.ds(pl.multiple_of(t * rows, 16), rows), :] += total
                        return 0

                    lax.fori_loop(0, halves, more, 0)

            second(1)

    def fetch(land, index, number, n, h):
        place = land.at[index, pl.ds(h * (C // 2), C // 2)]
        pltpu.make_async_copy(place, place, z_recv.at[number, h]).wait()
        copy = pltpu.make_async_copy(place, zst.at[n, h], zst_sem.at[n, h])
        copy.start()
        return copy

    def from_behind(h, d, k):
        comes = ((d >= z) & (z > 0)) | ((d < z) & (z < planes - 1))
        if h == 0:
            return comes
        from_end = ((z == 1) & (d >= z)) | ((z == planes - 2) & (d < z))
        return comes & jnp.logical_not(helper & from_end & (rank(d, k) < handed))

    def from_front(h, d, k):
        comes = (d == z) & (z < planes - 1)
        if h == 0:
            return comes
        return comes & jnp.logical_not(helper & (z == planes - 2) & (rank(d, k) < handed))

    def fetch_half(n, h, d, k, g):
        @pl.when(from_behind(h, d, k))
        def _():
            fetch(zland, g, g, n, h)

    def finish_half(slot, n, h, d, k, g):
        def add():
            pltpu.make_async_copy(zst.at[n, h], zst.at[n, h], zst_sem.at[n, h]).wait()

            def one(t, _):
                place = pl.ds(pl.multiple_of(t * rows, 16), rows)
                zsend[slot, n, h, place, :] += zst[n, h, place, :]
                return 0

            lax.fori_loop(0, halves, one, 0)

        @pl.when(from_behind(h, d, k))
        def _():
            add()

        @pl.when(from_front(h, d, k))
        def _():
            fetch(zlast, k, chunks + k, n, h)
            add()

        @pl.when(d > z)
        def _():
            z_copy(zland, g, g, slot, n, h, jnp.minimum(z + 1, planes - 1)).start()

        @pl.when(d < z - 1)
        def _():
            z_copy(zland, g, g, slot, n, h, jnp.maximum(z - 1, 0)).start()

        @pl.when(d == z - 1)
        def _():
            z_copy(zlast, k, chunks + k, slot, n, h, jnp.maximum(z - 1, 0)).start()

        @pl.when(d == z)
        def _():
            place = pl.ds(h * (C // 2), C // 2), pl.ds(pl.multiple_of(k * GK, 128), GK)
            pltpu.make_async_copy(zsend.at[slot, n, h], grad_expr.at[place], zs_sem.at[slot, n, h]).start()

    def tile_of(j):
        t, n = lax.div(j, tiles), lax.rem(j, tiles)
        return grad_logits.at[pl.ds(pl.multiple_of(t * rows, 8), rows), pl.ds(pl.multiple_of(n * tile, 128), tile)]

    def out_copy(j):
        return pltpu.make_async_copy(outst.at[lax.rem(j, 2)], tile_of(j), out_sem.at[lax.rem(j, 2)])

    def in_copy(j):
        return pltpu.make_async_copy(tile_of(j), inst.at[lax.rem(j, 2)], in_sem.at[lax.rem(j, 2)])

    def map_part(j, first, last):
        t, place = lax.div(j, tiles), pl.ds(pl.multiple_of(lax.rem(j, tiles) * tile, 128), tile)
        genes = pl.ds(first * GK, (last - first) * GK)
        both = dot(x2[t, :, genes], gph[genes, place])
        return both[:rows] + both[rows:] + dot(x2[t, pl.ds(0, rows), genes], gpl[genes, place])

    def stored_part(j, stage):
        slot = lax.rem(j, 2)

        @pl.when(j >= 2)
        def _():
            out_copy(j - 2).wait()

        if stage > 0:

            @pl.when(j + 1 < count)
            def _():
                in_copy(j + 1).start()

        total = map_part(j, cuts[stage], cuts[stage + 1])
        if stage == last:
            t, place = lax.div(j, tiles), pl.ds(pl.multiple_of(lax.rem(j, tiles) * tile, 128), tile)
            scale = weight[pl.ds(pl.multiple_of(t * rows, 8), rows), 0:1]
            total = total + (scale * cols[0:1, place] - cols[1:2, place])
        if stage > 0:
            in_copy(j).wait()
            total = total + inst[slot]
        if stage == last:
            exponent = e2[t, pl.ds(0, rows), place].astype(F32) + e2[t, pl.ds(rows, rows), place].astype(F32)
            total = exponent * total
        outst[slot] = total
        out_copy(j).start()

    ends = [0] + [group - 1 + 2 * group * p for p in range(1, groups)]
    finishes = [4 + group + 2 * group * p for p in range(groups)]
    if group == 2 and groups == 8:
        finishes = [6, 10, 13, 16, 18, 20, 26, 32]
    makes = [max((p + 1) * group - 1, finishes[p - zslots] + 5 if p >= zslots else 0) for p in range(groups)]
    makes = finishes

    def at(t, of_ends, of_others):
        p = jnp.int32(-1)
        for n in range(groups):
            p = jnp.where(t == jnp.where(at_end, of_ends[n], of_others[n]), n, p)
        return p

    def step(t, _):
        def hops(firsts, seconds):
            for i in firsts:
                first_own(order(i)[2])
            for i in seconds:
                second_own(order(i)[2])

        @pl.when(t == 0)
        def _():
            hops((0, 1), ())
            for i in range(2, ahead + 1):
                announce(i)
            hops((), (0, 1))
            stage_own(order(0)[2], 0)
            stage_own(order(1)[2], 1)

        @pl.when(t == 1)
        def _():
            hops((2, 3), (2,))

        @pl.when(t == 2)
        def _():
            hops((4, 5), (3, 4))

        @pl.when((t >= 3) & (t + 3 < chunks))
        def _():
            first_own(order(t + 3)[2])

        @pl.when((t >= 3) & (t + 2 < chunks))
        def _():
            second_own(order(t + 2)[2])

        @pl.when((t >= 1) & (t + 1 < chunks))
        def _():
            stage_own(order(t + 1)[2], lax.rem(t + 1, 2))

        @pl.when((t >= 1) & (t + ahead < chunks))
        def _():
            announce(t + ahead)

        @pl.when(lax.rem(t, 2) == 0)
        def _():
            far_step(lax.div(t, 2), ask_far)

            @pl.when(t >= 2)
            def _():
                far_step(lax.div(t - 2, 2), first_far)

        @pl.when((t >= 3) & (lax.rem(t, 2) == 1))
        def _():
            far_step(lax.div(t - 3, 2), second_far)

        soon = at(t + 1, [-1] * groups, finishes)

        @pl.when(helper & (soon >= 0))
        def _():
            for n in range(group):
                d, k, _ = order(soon * group + n)
                far_step(rank(d, k), lambda m, n=n: stage_far(m, n))

        @pl.when((t < chunks) & (t != 1))
        def _():
            take_own(lax.rem(t, 2), gph, gpl, t * GK)

        @pl.when(t == 0)
        def _():
            take_own(1, gph, gpl, GK)
            for n in range(parts):
                for copy in e_copy(n):
                    copy.wait()
            lax.fori_loop(0, chunks, load_x, 0)

        p = at(t, ends, makes)

        @pl.when(p >= 0)
        def _():
            multiply_group(p)

        q = at(t, ends, finishes)

        @pl.when(q >= 0)
        def _():
            finish_group(q)

        @pl.when((t == 2) & helper)
        def _():
            far_exponentials()

        @pl.when(t == cuts[1])
        def _():
            pltpu.make_async_copy(xparts, x2, x_sem).wait()
            total = collect(mine, vecr, vec_send, vec_recv, c, cells, in_plane)
            spot_sum = collect(loss, lossr, loss_send, loss_recv, z, planes, in_column)
            weight[...] = jnp.broadcast_to(counts[...].astype(F32)[None, :], (128, C)).T
            cols[0:1, :] = vec[8:9, :]
            cols[1:2, :] = total[0:1, :] + vec[9:10, :]
            losses[...] = jnp.zeros_like(losses)
            losses[0:1, :] = loss[2:3, :] - total[1:2, 0:128] / G - spot_sum[0:1, :] / loss[1:2, :]

        for stage in range(last + 1):
            begin = cuts[stage + 1]
            steps = cuts[stage + 2] - begin if stage < last else count
            each = -(-count // steps)

            @pl.when((t >= begin) & (t < begin + steps))
            def _():
                if stage > 0:

                    @pl.when(t == begin)
                    def _():
                        for j in range(count - 2, count):
                            out_copy(j).wait()
                        in_copy(0).start()

                def one(j, _):
                    stored_part(j, stage)
                    return 0

                lax.fori_loop(
                    jnp.minimum((t - begin) * each, count), jnp.minimum((t - begin + 1) * each, count), one, 0
                )

        return 0

    lax.fori_loop(0, slots, step, 0)

    for p in range(groups - zslots, groups):
        for h in range(2):

            @pl.when(had(p, h))
            def _():
                for n in range(group):
                    sent(p % zslots, n, h)

    for j in range(count - 2, count):
        out_copy(j).wait()

    def drain(g, _):
        n = rank(lax.div(g, per), lax.rem(g, per))
        drain_own(g)

        @pl.when(helper & (n < handed))
        def _():
            drain_far(n)

        @pl.when(at_end & (n < handed))
        def _():
            row_copy(n, g).wait_send()

        return 0

    lax.fori_loop(0, chunks, drain, 0)


def backward(cfg, ehi, elo, xparts, far_logits, vec, loss, counts, gp, spent):
    cells, planes, C, S, G, GK, r = (cfg[k] for k in ("cells", "planes", "C", "S", "G", "GK", "r"))
    chips, per, chunks = cells // 2, G // planes // GK, G // GK
    parts, tile, group, zslots = cfg["parts"], cfg["tile"], cfg["group"], cfg["zslots"]
    rows, handed = C // parts, cfg["handed"]
    sem = pltpu.SemaphoreType.DMA
    scratch = [
        pltpu.VMEM((parts, 2 * rows, S), BF16), pltpu.VMEM((parts, 2 * rows, G), BF16),
        pltpu.VMEM((parts // 2, 2 * rows, S), BF16),
        pltpu.VMEM((G, S), BF16), pltpu.VMEM((G, S), BF16), pltpu.VMEM((2, GK, S), BF16),
        pltpu.VMEM((2, chips, 2, r, S), F32), pltpu.VMEM((group, chips, 2, r, S), F32),
        pltpu.VMEM((2, cfg["piece"], S), F32), pltpu.VMEM((group, 2, C // 2, GK), F32),
        pltpu.VMEM((zslots, group, 2, C // 2, GK), F32), pltpu.VMEM((2, rows, tile), F32), pltpu.VMEM((2, rows, tile), F32),
        pltpu.VMEM((8, S), F32), pltpu.VMEM((cells, 8, S), F32), pltpu.VMEM((planes, 8, 128), F32), pltpu.VMEM((C, 128), F32),
        sem((2, parts)), sem, sem((2,)), sem((chunks, chips)), sem((chunks,)), sem((chunks, 2)),
        sem((handed, chips)), sem((handed,)), sem((handed, 2)),
        sem((handed,)), sem((handed,)), sem((2,)), sem((group,)),
        sem((chunks + per, 2)), sem((zslots, group, 2)), sem((group, 2)), sem((2,)), sem((2,)),
        sem((cells,)), sem((cells,)), sem((planes,)), sem((planes,)),
    ]
    return pl.pallas_call(
        functools.partial(backward_kernel, cfg),
        out_shape=(
            jax.ShapeDtypeStruct((C, S), F32),
            jax.ShapeDtypeStruct((C, G // planes), F32),
            jax.ShapeDtypeStruct((8, 128), F32),
            jax.ShapeDtypeStruct((chunks, chips, 2, r, S), F32),
            jax.ShapeDtypeStruct((cfg["handed"], chips, 2, r, S), F32),
            jax.ShapeDtypeStruct((chunks, C, GK), F32),
            jax.ShapeDtypeStruct((per, C, GK), F32),
        ),
        in_specs=[ANY, ANY, ANY, ANY, VMEM, VMEM, VMEM, ANY, ANY],
        out_specs=(ANY, ANY, VMEM, ANY, ANY, ANY, ANY),
        input_output_aliases={7: 3, 8: 5},
        scratch_shapes=scratch,
        compiler_params=pltpu.CompilerParams(
            collective_id=1, has_side_effects=True, vmem_limit_bytes=61 * 2**20
        ),
        cost_estimate=pl.CostEstimate(flops=12 * C * S * G, bytes_accessed=16 * C * S, transcendentals=0),
        name="backward",
    )(ehi, elo, xparts, far_logits, vec, loss, counts, gp, spent)


def passing_kernel(pieces, losses, first, second, out_losses, out_first, out_second, *rest):
    buffers, (read, write) = rest[:2], rest[2:]
    moves = []
    for n, (source, target) in enumerate(((first, out_first), (second, out_second))):
        rows = source.shape[0] // pieces[n]
        for i in range(pieces[n]):
            place = pl.ds(i * rows, rows)
            slot = len(moves)
            moves.append(
                (
                    pltpu.make_async_copy(source.at[place], buffers[n].at[place], read.at[slot]),
                    pltpu.make_async_copy(buffers[n].at[place], target.at[place], write.at[slot]),
                )
            )
    for load, _ in moves:
        load.start()
    for n in range(2):
        out_losses[n] = losses[0, n]
    for load, store in moves:
        load.wait()
        store.start()
    for _, store in moves:
        store.wait()


def passing(losses, first, second):
    pieces = [8, 2]
    smem = pl.BlockSpec(memory_space=pltpu.SMEM)
    return pl.pallas_call(
        functools.partial(passing_kernel, pieces),
        out_shape=(
            jax.ShapeDtypeStruct((2,), F32),
            jax.ShapeDtypeStruct(first.shape, first.dtype),
            jax.ShapeDtypeStruct(second.shape, second.dtype),
        ),
        in_specs=[smem, ANY, ANY],
        out_specs=(smem, ANY, ANY),
        scratch_shapes=[
            pltpu.VMEM(first.shape, first.dtype), pltpu.VMEM(second.shape, second.dtype),
            pltpu.SemaphoreType.DMA((sum(pieces),)), pltpu.SemaphoreType.DMA((sum(pieces),)),
        ],
        compiler_params=pltpu.CompilerParams(vmem_limit_bytes=60 * 2**20),
        name="passing",
    )(losses, first, second)


def local(cells, planes, logits, expression, spatial, cell_counts, spot_density, slide_id, padding):
    C, S = logits.shape
    G = expression.shape[1] * planes
    GK = max(128, 8 * cells)
    chunks, parts, group = G // GK, 4, 256 // GK
    tile = 256 * group
    across = 1
    while across * across < cells // 2:
        across *= 2
    cfg = dict(
        cells=cells, planes=planes, C=C, S=S, G=G, GK=GK, r=GK // cells, rows=128, tile=tile, parts=parts,
        group=group, zslots=1 + group, slots=max(chunks + parts * (S // tile), 5 + group + 2 * (chunks - group)), pieces=8, ahead=5, handed=chunks // 4,
        across=across, helped=planes >= 4, piece=max(n for n in range(16, 65, 16) if C // parts % n == 0),
    )
    counts = cell_counts
    gath, ehi, elo, xparts, far_logits, gp, vec, loss = forward(
        cfg, logits, expression, spatial, counts, spot_density[None, :],
        slide_id[None, :], padding[None, :],
    )
    grad_logits, grad_expression, losses, *_ = backward(
        cfg, ehi, elo, xparts, far_logits, vec, loss, counts, gp, gath
    )
    return passing(losses, grad_logits, grad_expression)


def solution(mesh):
    cells, planes = mesh.shape["cell"], mesh.shape["spot"]
    in_specs = (
        P("cell", "spot"), P("cell", "spot"), P("cell", "spot"), P("cell"), P("spot"), P("spot"), P("spot"),
    )
    out_specs = (P(), P("cell", "spot"), P("cell", "spot"))
    return jax.shard_map(
        functools.partial(local, cells, planes), mesh=mesh, in_specs=in_specs, out_specs=out_specs, check_vma=False
    )
```

```python
import functools

import jax
import jax.numpy as jnp
from jax import lax
from jax.experimental import pallas as pl
from jax.experimental.pallas import tpu as pltpu
from jax.sharding import PartitionSpec as P

epsilon = 1e-06
MESH = pl.DeviceIdType.MESH
F32, BF16 = jnp.float32, jnp.bfloat16
TN = (((0,), (0,)), ((), ()))
NN = (((1,), (0,)), ((), ()))
NT = (((1,), (1,)), ((), ()))


def dot(left, right, dims=NN):
    return lax.dot_general(left, right, dims, preferred_element_type=F32)


def split(v):
    high = v.astype(BF16)
    return high, (v - high.astype(F32)).astype(BF16)


def arrival(z, i, planes, per):
    near = jnp.minimum(z, planes - 1 - z)
    j = jnp.maximum(i - per, 0)
    pair = lax.rem(j, 2 * per)
    t = 1 + lax.div(j, 2 * per)
    both = jnp.where(lax.rem(pair, 2) == 0, z - t, z + t)
    late = jnp.maximum(j - 2 * near * per, 0)
    t = near + 1 + lax.div(late, per)
    one = jnp.where(z < planes - 1 - z, z + t, z - t)
    in_pairs = j < 2 * near * per
    shard = jnp.where(i < per, z, jnp.where(in_pairs, both, one))
    chunk = jnp.where(i < per, i, jnp.where(in_pairs, lax.div(pair, 2), lax.rem(late, per)))
    return shard, chunk


def greet(c, z, cells, planes):
    barrier = pltpu.get_barrier_semaphore()

    def in_plane(step, _):
        pl.semaphore_signal(barrier, inc=1, device_id=(lax.rem(c + step, cells), z), device_id_type=MESH)
        return 0

    def in_column(step, _):
        pl.semaphore_signal(barrier, inc=1, device_id=(c, lax.rem(z + step, planes)), device_id_type=MESH)
        return 0

    lax.fori_loop(1, cells, in_plane, 0)
    lax.fori_loop(1, planes, in_column, 0)
    pl.semaphore_wait(barrier, cells + planes - 2)


def share(src, dst, send, recv, me, count, device):
    def start(step, _):
        other = lax.rem(me + step, count)
        pltpu.make_async_remote_copy(
            src_ref=src, dst_ref=dst.at[me], send_sem=send.at[other], recv_sem=recv.at[me],
            device_id=device(other), device_id_type=MESH,
        ).start()
        return 0

    lax.fori_loop(1, count, start, 0)


def collect(src, dst, send, recv, me, count, device):
    def wait(step, total):
        other = lax.rem(me + step, count)
        copy = pltpu.make_async_remote_copy(
            src_ref=src, dst_ref=dst.at[other], send_sem=send.at[other], recv_sem=recv.at[other],
            device_id=device(other), device_id_type=MESH,
        )
        copy.wait_send()
        copy.wait_recv()
        return total + dst[other]

    return lax.fori_loop(1, count, wait, src[...])


def forward_kernel(
    cfg, logits, expr, spatial, counts, dens, slide, pad,
    gath, ehi_out, elo_out, x_out, far_logits, gp_out, vec_out, loss_out,
    ehi, elo, lbuf, stage, xparts, amat, partial, corer, half, chipr, pred, spat,
    tots, totr, acc, spots, spotr, gcol, gst, gstr, vec,
    g_recv, up_send, down_send, l_sem, st_sem, put_sem, core_send, core_recv, chip_send, chip_recv,
    far_send, far_recv, spat_send, spat_recv, tot_send, tot_recv, spot_send, spot_recv, gst_send, gst_recv, out_sem,
):
    cells, planes, C, S, G, GK, r = (cfg[k] for k in ("cells", "planes", "C", "S", "G", "GK", "r"))
    chips, per, chunks = cells // 2, G // planes // GK, G // GK
    rows, tile, parts, helped = cfg["rows"], cfg["tile"], cfg["parts"], cfg["helped"]
    part, pieces = C // parts, cfg["pieces"]
    own_genes = G // cells
    c, z = lax.axis_index("cell"), lax.axis_index("spot")
    chip, core = lax.div(c, 2), lax.rem(c, 2)
    sibling = c + 1 - 2 * core
    in_plane = lambda other: (other, z)
    in_column = lambda other: (c, other)

    greet(c, z, cells, planes)

    def z_copy(src, g, to, send):
        return pltpu.make_async_remote_copy(
            src_ref=src, dst_ref=gath.at[g], send_sem=send.at[g], recv_sem=g_recv.at[g],
            device_id=(c, to), device_id_type=MESH,
        )

    up, down = jnp.minimum(z + 1, planes - 1), jnp.maximum(z - 1, 0)

    def send_own(k, _):
        g = z * per + k
        src = expr.at[:, pl.ds(pl.multiple_of(k * GK, 128), GK)]

        @pl.when(z < planes - 1)
        def _():
            z_copy(src, g, up, up_send).start()

        @pl.when(z > 0)
        def _():
            z_copy(src, g, down, down_send).start()

        return 0

    lax.fori_loop(0, per, send_own, 0)

    at_end = (z == 0) | (z == planes - 1)
    helper = ((z == 1) | (z == planes - 2)) & helped
    beside = jnp.where(z == 0, 1, jnp.where(z == planes - 1, planes - 2, jnp.where(z == 1, 0, planes - 1)))
    piece = C // 2 // pieces

    def far_copy(n):
        return pltpu.make_async_remote_copy(
            src_ref=logits.at[pl.ds(pl.multiple_of(C // 2 + n * piece, 8), piece)],
            dst_ref=far_logits.at[pl.ds(pl.multiple_of(n * piece, 8), piece)],
            send_sem=far_send.at[n], recv_sem=far_recv.at[n], device_id=(c, beside), device_id_type=MESH,
        )

    blocks = own_genes // r

    def spat_copy(b):
        place = c * blocks + b
        g, owner = lax.div(place, cells), lax.rem(place, cells)
        src = spatial.at[pl.ds(pl.multiple_of(b * r, 8), r)]
        remote = pltpu.make_async_remote_copy(
            src_ref=src, dst_ref=spat.at[g], send_sem=spat_send.at[b], recv_sem=spat_recv.at[g],
            device_id=(owner, z), device_id_type=MESH,
        )
        local = pltpu.make_async_copy(src, spat.at[g], spat_recv.at[g])
        return owner, remote, local

    def send_spat(b, _):
        owner, remote, local = spat_copy(b)

        @pl.when(owner != c)
        def _():
            remote.start()

        @pl.when(owner == c)
        def _():
            local.start()

        return 0

    lax.fori_loop(0, blocks, send_spat, 0)

    def load(t):
        return pltpu.make_async_copy(
            logits.at[pl.ds(pl.multiple_of(t * rows, rows), rows)], lbuf.at[lax.rem(t, 2)], l_sem.at[lax.rem(t, 2)]
        )

    load(0).start()

    def exps(t, _):
        @pl.when(t + 1 < C // rows)
        def _():
            load(t + 1).start()

        load(t).wait()
        high, low = split(jnp.exp(lbuf[lax.rem(t, 2)]))
        place = pl.ds(pl.multiple_of(t * rows, rows), rows)
        ehi[place, :] = high
        elo[place, :] = low
        return 0

    lax.fori_loop(0, C // rows, exps, 0)
    keep = [pltpu.make_async_copy(ehi, ehi_out, out_sem.at[0]), pltpu.make_async_copy(elo, elo_out, out_sem.at[1])]
    for copy in keep:
        copy.start()

    row = lax.broadcasted_iota(jnp.int32, (16, C), 0)
    weight = jnp.broadcast_to(counts[...].astype(F32)[None, :], (16, C))
    lhs = jnp.where(row == 0, 1.0, jnp.where(row == 1, weight, 0.0)).astype(BF16)

    def sums(t, _):
        place = pl.ds(pl.multiple_of(t * tile, tile), tile)
        both = dot(lhs, ehi[:, place]) + dot(lhs, elo[:, place])
        tots[:, place] = both[:8]
        return 0

    lax.fori_loop(0, S // tile, sums, 0)
    share(tots, totr, tot_send, tot_recv, c, cells, in_plane)

    valid = (1 - pad[...]).astype(F32)
    mask0 = valid * (slide[...] == 0).astype(F32)
    mask1 = valid * (slide[...] == 1).astype(F32)
    vec[4:5, :] = mask0
    vec[5:6, :] = mask1
    acc[...] = jnp.zeros_like(acc)
    gcol[...] = jnp.zeros_like(gcol)

    def core_copy(g, slot):
        return pltpu.make_async_remote_copy(
            src_ref=partial.at[slot, :, 1 - core], dst_ref=corer.at[g], send_sem=core_send.at[slot],
            recv_sem=core_recv.at[g], device_id=(sibling, z), device_id_type=MESH,
        )

    def chip_copy(g, slot, other):
        return pltpu.make_async_remote_copy(
            src_ref=half.at[slot, other], dst_ref=chipr.at[g, chip], send_sem=chip_send.at[slot, other],
            recv_sem=chip_recv.at[g, chip], device_id=(2 * other + core, z), device_id_type=MESH,
        )

    def chip_wait(g, slot, other):
        return pltpu.make_async_remote_copy(
            src_ref=half.at[slot, chip], dst_ref=chipr.at[g, other], send_sem=chip_send.at[slot, other],
            recv_sem=chip_recv.at[g, other], device_id=(2 * other + core, z), device_id_type=MESH,
        )

    def product(i):
        d, k = arrival(z, i, planes, per)
        g, slot = d * per + k, lax.rem(i, 2)
        own = pltpu.make_async_copy(expr.at[:, pl.ds(pl.multiple_of(k * GK, 128), GK)], stage, st_sem)
        pull = pltpu.make_async_copy(gath.at[g], stage, st_sem)

        @pl.when(d == z)
        def _():
            own.start()

        @pl.when(d != z)
        def _():
            z_copy(gath.at[g], g, down, down_send).wait_recv()

        @pl.when((d < z) & (z < planes - 1))
        def _():
            z_copy(gath.at[g], g, up, up_send).start()

        @pl.when((d > z) & (z > 0))
        def _():
            z_copy(gath.at[g], g, down, down_send).start()

        @pl.when(d != z)
        def _():
            pull.start()

        pull.wait()
        @pl.when(i >= 2)
        def _():
            core_copy(g, slot).wait_send()

        def turn(t, _):
            place = pl.ds(pl.multiple_of(t * 128, 128), 128)
            high, low = split(stage[place, :].T)
            amat[:GK, place] = high
            amat[GK:, place] = low
            return 0

        lax.fori_loop(0, C // 128, turn, 0)

        def multiply(t, _):
            place = pl.ds(pl.multiple_of(t * tile, tile), tile)
            both = dot(amat[...], ehi[:, place])
            total = both[:GK] + both[GK:] + dot(amat[:GK, :], elo[:, place])
            partial[slot, :, :, :, place] = total.reshape(chips, 2, r, tile)
            return 0

        lax.fori_loop(0, S // tile, multiply, 0)
        core_copy(g, slot).start()
        columns = pl.ds(pl.multiple_of(g * GK, 128), GK)

        @pl.when(i >= 1)
        def _():
            pltpu.make_async_copy(xparts, x_out.at[:, :, columns], put_sem).wait()

        def keep_parts(t, _):
            high, low = split(stage[pl.ds(pl.multiple_of(t * part, 16), part), :])
            xparts[t, pl.ds(0, part), :] = high
            xparts[t, pl.ds(part, part), :] = low
            return 0

        lax.fori_loop(0, parts, keep_parts, 0)
        pltpu.make_async_copy(xparts, x_out.at[:, :, columns], put_sem).start()

    def to_chips(i):
        d, k = arrival(z, i, planes, per)
        g, slot = d * per + k, lax.rem(i, 2)
        core_copy(g, slot).wait_recv()

        @pl.when(i >= 2)
        def _():
            def drain(step, _):
                chip_copy(g, slot, lax.rem(chip + step, chips)).wait_send()
                return 0

            lax.fori_loop(1, chips, drain, 0)

        def add(other, _):
            half[slot, other] = partial[slot, other, core] + corer[g, other]

            @pl.when(other != chip)
            def _():
                chip_copy(g, slot, other).start()

            return 0

        lax.fori_loop(0, chips, add, 0)

    def finish(i):
        d, k = arrival(z, i, planes, per)
        g, slot = d * per + k, lax.rem(i, 2)
        pltpu.make_async_copy(spat.at[g], spat.at[g], spat_recv.at[g]).wait()

        def add(step, total):
            other = lax.rem(chip + step, chips)
            chip_wait(g, slot, other).wait_recv()
            return total + chipr[g, other]

        p = lax.fori_loop(1, chips, add, half[slot, chip]) * vec[0:1, :]
        s = spat[g]
        pred[g] = p
        ps, pp, ss = p * s, p * p, s * s
        acc[0] += ps
        acc[1] += pp
        acc[2] += ss
        lane = lax.broadcasted_iota(jnp.int32, (r, 128), 1)
        cols = jnp.zeros((r, 128), F32)
        for n, v in enumerate((ps, pp, ss)):
            for m in range(2):
                one = jnp.sum(v * vec[4 + m : 5 + m, :], axis=1, keepdims=True)
                cols = jnp.where(lane == 2 * n + m, one, cols)
        gcol[pl.ds(pl.multiple_of(g * r, 8), r), :] = cols

    def step(i, _):
        @pl.when((i >= per) & (i < per + pieces) & at_end & helped)
        def _():
            far_copy(i - per).start()

        @pl.when(i < chunks)
        def _():
            product(i)

        @pl.when(i == 1)
        def _():
            total = collect(tots, totr, tot_send, tot_recv, c, cells, in_plane)
            vec[0:1, :] = 1.0 / total[0:1, :]
            vec[1:2, :] = total[1:2, :] / total[0:1, :]
            gst[...] = jnp.zeros_like(gst)
            density = vec[1:2, :]
            target = dens[...]
            lane = lax.broadcasted_iota(jnp.int32, (1, gst.shape[1]), 1)
            logs = target * jnp.log(target), target * jnp.log(density)
            for n, v in enumerate((jnp.ones_like(target), target, density, *logs)):
                line = jnp.zeros((1, gst.shape[1]), F32)
                for m in range(2):
                    one = jnp.sum(v * vec[4 + m : 5 + m, :], axis=1, keepdims=True)
                    line = jnp.where(lane == m, one, line)
                gst[8 + n : 9 + n, :] = line

        @pl.when((i >= 1) & (i <= chunks))
        def _():
            to_chips(i - 1)

        @pl.when(i >= 2)
        def _():
            finish(i - 2)

        return 0

    lax.fori_loop(0, chunks + 2, step, 0)

    spots[...] = jnp.zeros_like(spots)
    for n in range(3):
        spots[n : n + 1, :] = jnp.sum(acc[n], axis=0, keepdims=True)
    share(spots, spotr, spot_send, spot_recv, c, cells, in_plane)
    gst[0:8, :] = gcol[...].T[0:8, :]
    share(gst, gstr, gst_send, gst_recv, z, planes, in_column)

    genes = collect(gst, gstr, gst_send, gst_recv, z, planes, in_column)
    dot_g, aa_g, bb_g = ([genes[2 * n + m : 2 * n + m + 1, :] for m in range(2)] for n in range(3))
    slides = [[genes[8 + n : 9 + n, m : m + 1] for m in range(2)] for n in range(5)]
    lines, cos_sums, own_losses = [], [], []
    for m in range(2):
        norm = jnp.sqrt((aa_g[m] + epsilon) * (bb_g[m] + epsilon))
        cos = dot_g[m] / norm
        lines += [-1.0 / (norm * G), cos / ((aa_g[m] + epsilon) * G)]
        cos_sums.append(jnp.sum(cos, axis=1, keepdims=True))
    lines.append(jnp.zeros((124, gst.shape[1]), F32))
    gcol[...] = jnp.concatenate(lines, axis=0).T
    live = [jnp.maximum(v, 1.0) for v in slides[0]]
    mass_target, mass_pred = slides[1], slides[2]
    divergence = [
        (slides[3][m] - slides[4][m]) / mass_target[m] - jnp.log(mass_target[m]) + jnp.log(mass_pred[m])
        for m in range(2)
    ]
    mask0, mask1 = vec[4:5, :], vec[5:6, :]
    grad_density = (
        mask0 / mass_pred[0] + mask1 / mass_pred[1]
        - dens[...] * (mask0 / mass_target[0] + mask1 / mass_target[1]) / vec[1:2, :]
    )
    spot_weight = mask0 / live[0] + mask1 / live[1]

    spot = collect(spots, spotr, spot_send, spot_recv, c, cells, in_plane)
    norm = jnp.sqrt((spot[1:2, :] + epsilon) * (spot[2:3, :] + epsilon))
    spot_cos = spot[0:1, :] / norm
    inverse = vec[0:1, :]
    vec[2:3, :] = -spot_weight / norm
    vec[3:4, :] = spot_weight * spot_cos / (spot[1:2, :] + epsilon)
    vec[6:7, :] = grad_density * inverse
    vec[7:8, :] = vec[1:2, :] * grad_density * inverse
    acc[0] = jnp.zeros((r, S), F32)

    def gradient(g, _):
        columns = gcol[pl.ds(pl.multiple_of(g * r, 8), r), :]
        by_spatial = vec[4:5, :] * columns[:, 0:1] + vec[5:6, :] * columns[:, 2:3] + vec[2:3, :]
        by_pred = vec[4:5, :] * columns[:, 1:2] + vec[5:6, :] * columns[:, 3:4] + vec[3:4, :]
        p = pred[g]
        value = (spat[g] * by_spatial + p * by_pred) * vec[0:1, :]
        acc[0] += p * value
        pred[g] = value
        pltpu.make_async_copy(pred.at[g], gp_out.at[g, chip, core], out_sem.at[2]).start()
        return 0

    lax.fori_loop(0, chunks, gradient, 0)
    copy = pltpu.make_async_copy(pred, gp_out.at[:, chip, core], out_sem.at[2])
    vec_out[...] = jnp.zeros_like(vec_out)
    vec_out[0:1, :] = jnp.sum(acc[0], axis=0, keepdims=True)
    vec_out[8:9, :] = vec[6:7, :]
    vec_out[9:10, :] = vec[7:8, :]
    lane = lax.broadcasted_iota(jnp.int32, (1, 128), 1)
    vec_out[1:2, 0:128] = jnp.where(lane == 0, cos_sums[0], jnp.where(lane == 1, cos_sums[1], 0.0))
    spot_sums = [jnp.sum(vec[4 + m : 5 + m, :] * spot_cos, axis=1, keepdims=True) for m in range(2)]
    loss_out[...] = jnp.zeros_like(loss_out)
    for n, v in enumerate((spot_sums, live, divergence)):
        loss_out[n : n + 1, :] = jnp.where(lane == 0, v[0], jnp.where(lane == 1, v[1], 0.0))

    copy.wait()
    for copy in keep:
        copy.wait()
    pltpu.make_async_copy(xparts, x_out.at[:, :, pl.ds(0, GK)], put_sem).wait()

    def drain_far(n, _):
        @pl.when(at_end & helped)
        def _():
            far_copy(n).wait_send()

        @pl.when(helper)
        def _():
            far_copy(n).wait_recv()

        return 0

    lax.fori_loop(0, pieces, drain_far, 0)

    def drain_z(g, _):
        d = lax.div(g, per)

        @pl.when((d <= z) & (z < planes - 1))
        def _():
            z_copy(gath.at[g], g, up, up_send).wait_send()

        @pl.when((d >= z) & (z > 0))
        def _():
            z_copy(gath.at[g], g, down, down_send).wait_send()

        return 0

    lax.fori_loop(0, chunks, drain_z, 0)

    def drain_spat(b, _):
        owner, remote, _ = spat_copy(b)

        @pl.when(owner != c)
        def _():
            remote.wait_send()

        return 0

    lax.fori_loop(0, blocks, drain_spat, 0)
    for slot in range(2):
        core_copy(0, slot).wait_send()

        def drain(step, _):
            chip_copy(0, slot, lax.rem(chip + step, chips)).wait_send()
            return 0

        lax.fori_loop(1, chips, drain, 0)


ANY = pl.BlockSpec(memory_space=pl.ANY)
VMEM = pl.BlockSpec(memory_space=pltpu.VMEM)


def forward(cfg, logits, expression, spatial, counts, dens, slide, pad):
    cells, planes, C, S, G, GK, r = (cfg[k] for k in ("cells", "planes", "C", "S", "G", "GK", "r"))
    chips, per, chunks = cells // 2, G // planes // GK, G // GK
    rows = cfg["rows"]
    wide = max(G // cells, 128)
    blocks = G // cells // r
    sem = pltpu.SemaphoreType.DMA
    scratch = [
        pltpu.VMEM((C, S), BF16), pltpu.VMEM((C, S), BF16), pltpu.VMEM((2, rows, S), F32),
        pltpu.VMEM((C, GK), F32), pltpu.VMEM((cfg["parts"], 2 * C // cfg["parts"], GK), BF16), pltpu.VMEM((2 * GK, C), BF16),
        pltpu.VMEM((2, chips, 2, r, S), F32), pltpu.VMEM((chunks, chips, r, S), F32),
        pltpu.VMEM((2, chips, r, S), F32), pltpu.VMEM((chunks, chips, r, S), F32),
        pltpu.VMEM((chunks, r, S), F32), pltpu.VMEM((chunks, r, S), F32),
        pltpu.VMEM((8, S), F32), pltpu.VMEM((cells, 8, S), F32), pltpu.VMEM((3, r, S), F32),
        pltpu.VMEM((8, S), F32), pltpu.VMEM((cells, 8, S), F32), pltpu.VMEM((wide, 128), F32),
        pltpu.VMEM((16, wide), F32), pltpu.VMEM((planes, 16, wide), F32), pltpu.VMEM((8, S), F32),
        sem((chunks,)), sem((chunks,)), sem((chunks,)), sem((2,)), sem, sem,
        sem((2,)), sem((chunks,)), sem((2, chips)), sem((chunks, chips)),
        sem((cfg["pieces"],)), sem((cfg["pieces"],)),
        sem((blocks,)), sem((chunks,)), sem((cells,)), sem((cells,)), sem((cells,)), sem((cells,)),
        sem((planes,)), sem((planes,)), sem((3,)),
    ]
    flops = 6 * C * S * G
    return pl.pallas_call(
        functools.partial(forward_kernel, cfg),
        out_shape=(
            jax.ShapeDtypeStruct((chunks, C, GK), F32),
            jax.ShapeDtypeStruct((C, S), BF16),
            jax.ShapeDtypeStruct((C, S), BF16),
            jax.ShapeDtypeStruct((cfg["parts"], 2 * C // cfg["parts"], G), BF16),
            jax.ShapeDtypeStruct((C // 2, S), F32),
            jax.ShapeDtypeStruct((chunks, chips, 2, r, S), F32),
            jax.ShapeDtypeStruct((16, S), F32),
            jax.ShapeDtypeStruct((8, 128), F32),
        ),
        in_specs=[ANY, ANY, ANY, VMEM, VMEM, VMEM, VMEM],
        out_specs=(ANY, ANY, ANY, ANY, ANY, ANY, VMEM, VMEM),
        scratch_shapes=scratch,
        compiler_params=pltpu.CompilerParams(
            collective_id=0, has_side_effects=True, vmem_limit_bytes=56 * 2**20
        ),
        cost_estimate=pl.CostEstimate(flops=flops, bytes_accessed=8 * C * S, transcendentals=C * S),
        name="forward",
    )(logits, expression, spatial, counts, dens, slide, pad)


def backward_kernel(
    cfg, ehi, elo, xparts, far_logits, vec, loss, counts, _gp, _gath,
    grad_logits, grad_expr, losses, land, far_land, zland, zlast,
    e2, x2, e3, gph, gpl, far_g, gstage, fstage, lbuf, zst, zsend, outst, inst, cols, vecr, lossr, weight,
    e_sem, x_sem, l_sem, g_recv, g_pair, g_sent, f_recv, f_pair, f_sent, row_recv, row_sent, gs_sem, fs_sem,
    z_recv, zs_sem, zst_sem, out_sem, in_sem, vec_send, vec_recv, loss_send, loss_recv,
):
    cells, planes, C, S, G, GK, r = (cfg[k] for k in ("cells", "planes", "C", "S", "G", "GK", "r"))
    chips, per, chunks = cells // 2, G // planes // GK, G // GK
    parts, tile, slots, group, zslots = (cfg[k] for k in ("parts", "tile", "slots", "group", "zslots"))
    ahead = cfg["ahead"]
    handed = cfg["handed"]
    count, groups = parts * (S // tile), chunks // group
    cuts = (0, chunks // 2, chunks)
    last = len(cuts) - 2
    helped, across = cfg["helped"], cfg["across"]
    rows, tiles, halves = C // parts, S // tile, parts // 2
    piece = cfg["piece"]
    pieces = C // 2 // piece
    down_chips = chips // across
    c, z = lax.axis_index("cell"), lax.axis_index("spot")
    chip, core = lax.div(c, 2), lax.rem(c, 2)
    chip_row, chip_col = lax.div(chip, across), lax.rem(chip, across)
    sibling = c + 1 - 2 * core
    in_plane = lambda other: (other, z)
    in_column = lambda other: (c, other)
    at_end = ((z == 0) | (z == planes - 1)) & helped
    helper = ((z == 1) | (z == planes - 2)) & helped
    beside = jnp.where(z == 0, 1, jnp.where(z == planes - 1, planes - 2, jnp.where(z == 1, 0, planes - 1)))

    def order(i):
        d, k = arrival(z, chunks - 1 - i, planes, per)
        return d, k, d * per + k

    greet(c, z, cells, planes)

    def spread(land, recv, pair, sent, buffer, ready):
        def copy(ref, source, g, other):
            return pltpu.make_async_remote_copy(
                src_ref=ref, dst_ref=ref, send_sem=sent.at[g, 0], recv_sem=recv.at[g, source],
                device_id=(2 * other + core, z), device_id_type=MESH,
            )

        def along_row(n):
            return chip_row * across + lax.rem(chip_col + n, across)

        def along_col(n):
            return lax.rem(chip_row + n, down_chips) * across + chip_col

        def each(count, body):
            def one(n, _):
                body(n)
                return 0

            lax.fori_loop(1, count, one, 0)

        def send(g):
            own = land.at[g, chip, core]
            each(across, lambda n: copy(own, chip, g, along_row(n)).start())
            each(down_chips, lambda n: copy(own, chip, g, along_col(n)).start())

        def landed(g, source):
            ref = land.at[g, source, core]
            pltpu.make_async_copy(ref, ref, recv.at[g, source]).wait()

        def first_hop(g):
            def from_row(n):
                source = along_row(n)
                landed(g, source)
                half = land.at[g, source, core, :, pl.ds(0, S // 2)]
                each(down_chips, lambda m: copy(half, source, g, along_col(m)).start())

            def from_col(n):
                source = along_col(n)
                landed(g, source)
                half = land.at[g, source, core, :, pl.ds(S // 2, S // 2)]
                each(across, lambda m: copy(half, source, g, along_row(m)).start())

            each(across, from_row)
            each(down_chips, from_col)

        def to_sibling(g):
            ref = land.at[g, :, core]
            return pltpu.make_async_remote_copy(
                src_ref=ref, dst_ref=ref, send_sem=sent.at[g, 1], recv_sem=pair.at[g],
                device_id=(sibling, z), device_id_type=MESH,
            )

        def second_hop(g):
            def from_rest(n):
                other = lax.rem(chip_row + 1 + lax.div(n - 1, across - 1), down_chips) * across
                landed(g, other + lax.rem(chip_col + 1 + lax.rem(n - 1, across - 1), across))

            each((across - 1) * (down_chips - 1) + 1, from_rest)
            to_sibling(g).start()

        def stage(g, slot):
            ref = land.at[g, :, 1 - core]
            pltpu.make_async_copy(ref, ref, pair.at[g]).wait()
            pltpu.make_async_copy(land.at[g], buffer.at[slot], ready.at[slot]).start()

        def take(slot, high_ref, low_ref, first):
            pltpu.make_async_copy(buffer.at[slot], buffer.at[slot], ready.at[slot]).wait()

            def split_tile(t, _):
                place = pl.ds(pl.multiple_of(t * 128, 128), 128)
                high, low = split(buffer[slot, :, :, :, place].reshape(GK, 128))
                lines = pl.ds(pl.multiple_of(first, 128), GK)
                high_ref[lines, place] = high
                low_ref[lines, place] = low
                return 0

            lax.fori_loop(0, S // 128, split_tile, 0)

        def drain(g):
            direct = land.at[g, pl.ds(0, chips - 1), 0]
            pltpu.make_async_copy(direct, direct, sent.at[g, 0]).wait()
            to_sibling(g).wait_send()

        return send, first_hop, second_hop, stage, take, drain

    send_own, first_own, second_own, stage_own, take_own, drain_own = spread(
        land, g_recv, g_pair, g_sent, gstage, gs_sem
    )
    send_far, first_far, second_far, stage_far, take_far, drain_far = spread(
        far_land, f_recv, f_pair, f_sent, fstage, fs_sem
    )

    def rank(d, k):
        end = jnp.where(at_end, z, beside)
        return (planes - 1 - jnp.abs(d - end)) * per + per - 1 - k

    def row_copy(n, g):
        return pltpu.make_async_remote_copy(
            src_ref=land.at[g, chip, core], dst_ref=far_land.at[n, chip, core],
            send_sem=row_sent.at[n], recv_sem=row_recv.at[n],
            device_id=(c, beside), device_id_type=MESH,
        )

    def announce(i):
        _, _, g = order(i)
        send_own(g)

        @pl.when(at_end & (i < handed))
        def _():
            row_copy(i, g).start()

    announce(0)
    announce(1)

    def e_copy(t):
        place = pl.ds(pl.multiple_of(t * rows, 16), rows)
        return (
            pltpu.make_async_copy(ehi.at[place], e2.at[t, pl.ds(0, rows)], e_sem.at[0, t]),
            pltpu.make_async_copy(elo.at[place], e2.at[t, pl.ds(rows, rows)], e_sem.at[1, t]),
        )

    for t in range(parts):
        for copy in e_copy(t):
            copy.start()
    def load_x(i, _):
        from_place = pl.ds(pl.multiple_of(order(i)[2] * GK, 128), GK)
        to_place = pl.ds(pl.multiple_of(i * GK, 128), GK)
        pltpu.make_async_copy(xparts.at[:, :, from_place], x2.at[:, :, to_place], x_sem).start()
        return 0

    mine = vec.at[pl.ds(0, 8)]
    share(mine, vecr, vec_send, vec_recv, c, cells, in_plane)
    share(loss, lossr, loss_send, loss_recv, z, planes, in_column)

    def far_exponentials():
        def load(n):
            return pltpu.make_async_copy(
                far_logits.at[pl.ds(pl.multiple_of(n * piece, 8), piece)], lbuf.at[lax.rem(n, 2)], l_sem.at[lax.rem(n, 2)]
            )

        for n in range(2):
            load(n).start()

        def exps(n, _):
            load(n).wait()
            high, low = split(jnp.exp(lbuf[lax.rem(n, 2)]))
            t, place = lax.div(n * piece, rows), lax.rem(n * piece, rows)
            e3[t, pl.ds(pl.multiple_of(place, 16), piece), :] = high
            e3[t, pl.ds(pl.multiple_of(rows + place, 16), piece), :] = low

            @pl.when(n + 2 < pieces)
            def _():
                load(n + 2).start()

            return 0

        lax.fori_loop(0, pieces, exps, 0)

    def far_step(n, what):
        @pl.when(helper & (n < handed))
        def _():
            what(n)

    def ask_far(n):
        row_copy(n, 0).wait_recv()
        send_far(n)

    def z_copy(land, index, number, slot, n, h, to):
        place = pl.ds(h * (C // 2), C // 2)
        return pltpu.make_async_remote_copy(
            src_ref=zsend.at[slot, n, h], dst_ref=land.at[index, place], send_sem=zs_sem.at[slot, n, h],
            recv_sem=z_recv.at[number, h], device_id=(c, to), device_id_type=MESH,
        )

    def sent(slot, n, h):
        pltpu.make_async_copy(zsend.at[slot, n, h], zsend.at[slot, n, h], zs_sem.at[slot, n, h]).wait()

    def had(p, h):
        return True if h == 0 else jnp.logical_not(at_end) | (p * group >= handed)

    def multiply_group(p):
        slot = lax.rem(p, zslots)
        lines = pl.ds(pl.multiple_of(p * group * GK, 128), group * GK)

        def half(h):
            @pl.when((p >= zslots) & had(p - zslots, h))
            def _():
                for n in range(group):
                    sent(slot, n, h)

            def multiply(t, _):
                both = dot(e2[h * halves + t], gph[lines, :], NT)
                total = both[:rows] + both[rows:] + dot(e2[h * halves + t, pl.ds(0, rows)], gpl[lines, :], NT)
                for n in range(group):
                    zsend[slot, n, h, pl.ds(pl.multiple_of(t * rows, 16), rows), :] = total[:, n * GK : (n + 1) * GK]
                return 0

            lax.fori_loop(0, halves, multiply, 0)

        half(0)

        @pl.when(had(p, 1))
        def _():
            half(1)

    def finish_group(p):
        slot = lax.rem(p, zslots)
        members = [order(p * group + n) for n in range(group)]

        def first(h):
            for n, (d, k, g) in enumerate(members):
                fetch_half(n, h, d, k, g)

        def second(h):
            for n, (d, k, g) in enumerate(members):
                finish_half(slot, n, h, d, k, g)

        first(0)

        @pl.when(had(p, 1))
        def _():
            first(1)

        second(0)

        @pl.when(had(p, 1))
        def _():
            for n, (d, k, g) in enumerate(members):

                @pl.when(helper & (rank(d, k) < handed))
                def _():
                    take_far(n, far_g.at[0], far_g.at[1], 0)

                    def more(t, _):
                        right = jnp.concatenate([far_g[0], far_g[1]], axis=0)
                        both = dot(e3[t, pl.ds(0, rows)], right, NT)
                        total = both[:, :GK] + both[:, GK:] + dot(e3[t, pl.ds(rows, rows)], far_g[0], NT)
                        zsend[slot, n, 1, pl.ds(pl.multiple_of(t * rows, 16), rows), :] += total
                        return 0

                    lax.fori_loop(0, halves, more, 0)

            second(1)

    def fetch(land, index, number, n, h):
        place = land.at[index, pl.ds(h * (C // 2), C // 2)]
        pltpu.make_async_copy(place, place, z_recv.at[number, h]).wait()
        copy = pltpu.make_async_copy(place, zst.at[n, h], zst_sem.at[n, h])
        copy.start()
        return copy

    def from_behind(h, d, k):
        comes = ((d >= z) & (z > 0)) | ((d < z) & (z < planes - 1))
        if h == 0:
            return comes
        from_end = ((z == 1) & (d >= z)) | ((z == planes - 2) & (d < z))
        return comes & jnp.logical_not(helper & from_end & (rank(d, k) < handed))

    def from_front(h, d, k):
        comes = (d == z) & (z < planes - 1)
        if h == 0:
            return comes
        return comes & jnp.logical_not(helper & (z == planes - 2) & (rank(d, k) < handed))

    def fetch_half(n, h, d, k, g):
        @pl.when(from_behind(h, d, k))
        def _():
            fetch(zland, g, g, n, h)

    def finish_half(slot, n, h, d, k, g):
        def add():
            pltpu.make_async_copy(zst.at[n, h], zst.at[n, h], zst_sem.at[n, h]).wait()

            def one(t, _):
                place = pl.ds(pl.multiple_of(t * rows, 16), rows)
                zsend[slot, n, h, place, :] += zst[n, h, place, :]
                return 0

            lax.fori_loop(0, halves, one, 0)

        @pl.when(from_behind(h, d, k))
        def _():
            add()

        @pl.when(from_front(h, d, k))
        def _():
            fetch(zlast, k, chunks + k, n, h)
            add()

        @pl.when(d > z)
        def _():
            z_copy(zland, g, g, slot, n, h, jnp.minimum(z + 1, planes - 1)).start()

        @pl.when(d < z - 1)
        def _():
            z_copy(zland, g, g, slot, n, h, jnp.maximum(z - 1, 0)).start()

        @pl.when(d == z - 1)
        def _():
            z_copy(zlast, k, chunks + k, slot, n, h, jnp.maximum(z - 1, 0)).start()

        @pl.when(d == z)
        def _():
            place = pl.ds(h * (C // 2), C // 2), pl.ds(pl.multiple_of(k * GK, 128), GK)
            pltpu.make_async_copy(zsend.at[slot, n, h], grad_expr.at[place], zs_sem.at[slot, n, h]).start()

    def tile_of(j):
        t, n = lax.div(j, tiles), lax.rem(j, tiles)
        return grad_logits.at[pl.ds(pl.multiple_of(t * rows, 8), rows), pl.ds(pl.multiple_of(n * tile, 128), tile)]

    def out_copy(j):
        return pltpu.make_async_copy(outst.at[lax.rem(j, 2)], tile_of(j), out_sem.at[lax.rem(j, 2)])

    def in_copy(j):
        return pltpu.make_async_copy(tile_of(j), inst.at[lax.rem(j, 2)], in_sem.at[lax.rem(j, 2)])

    def map_part(j, first, last):
        t, place = lax.div(j, tiles), pl.ds(pl.multiple_of(lax.rem(j, tiles) * tile, 128), tile)
        genes = pl.ds(first * GK, (last - first) * GK)
        both = dot(x2[t, :, genes], gph[genes, place])
        return both[:rows] + both[rows:] + dot(x2[t, pl.ds(0, rows), genes], gpl[genes, place])

    def stored_part(j, stage):
        slot = lax.rem(j, 2)

        @pl.when(j >= 2)
        def _():
            out_copy(j - 2).wait()

        if stage > 0:

            @pl.when(j + 1 < count)
            def _():
                in_copy(j + 1).start()

        total = map_part(j, cuts[stage], cuts[stage + 1])
        if stage == last:
            t, place = lax.div(j, tiles), pl.ds(pl.multiple_of(lax.rem(j, tiles) * tile, 128), tile)
            scale = weight[pl.ds(pl.multiple_of(t * rows, 8), rows), 0:1]
            total = total + (scale * cols[0:1, place] - cols[1:2, place])
        if stage > 0:
            in_copy(j).wait()
            total = total + inst[slot]
        if stage == last:
            exponent = e2[t, pl.ds(0, rows), place].astype(F32) + e2[t, pl.ds(rows, rows), place].astype(F32)
            total = exponent * total
        outst[slot] = total
        out_copy(j).start()

    ends = [0] + [group - 1 + 2 * group * p for p in range(1, groups)]
    finishes = [4 + group + 2 * group * p for p in range(groups)]
    if group == 2 and groups == 8:
        finishes = [6, 10, 13, 16, 18, 20, 26, 32]
    makes = [max((p + 1) * group - 1, finishes[p - zslots] + 5 if p >= zslots else 0) for p in range(groups)]
    makes = finishes

    def at(t, of_ends, of_others):
        p = jnp.int32(-1)
        for n in range(groups):
            p = jnp.where(t == jnp.where(at_end, of_ends[n], of_others[n]), n, p)
        return p

    def step(t, _):
        def hops(firsts, seconds):
            for i in firsts:
                first_own(order(i)[2])
            for i in seconds:
                second_own(order(i)[2])

        @pl.when(t == 0)
        def _():
            hops((0, 1), ())
            for i in range(2, ahead + 1):
                announce(i)
            hops((), (0, 1))
            stage_own(order(0)[2], 0)
            stage_own(order(1)[2], 1)

        @pl.when(t == 1)
        def _():
            hops((2, 3), (2,))

        @pl.when(t == 2)
        def _():
            hops((4, 5), (3, 4))

        @pl.when((t >= 3) & (t + 3 < chunks))
        def _():
            first_own(order(t + 3)[2])

        @pl.when((t >= 3) & (t + 2 < chunks))
        def _():
            second_own(order(t + 2)[2])

        @pl.when((t >= 1) & (t + 1 < chunks))
        def _():
            stage_own(order(t + 1)[2], lax.rem(t + 1, 2))

        @pl.when((t >= 1) & (t + ahead < chunks))
        def _():
            announce(t + ahead)

        @pl.when(lax.rem(t, 2) == 0)
        def _():
            far_step(lax.div(t, 2), ask_far)

            @pl.when(t >= 2)
            def _():
                far_step(lax.div(t - 2, 2), first_far)

        @pl.when((t >= 3) & (lax.rem(t, 2) == 1))
        def _():
            far_step(lax.div(t - 3, 2), second_far)

        soon = at(t + 1, [-1] * groups, finishes)

        @pl.when(helper & (soon >= 0))
        def _():
            for n in range(group):
                d, k, _ = order(soon * group + n)
                far_step(rank(d, k), lambda m, n=n: stage_far(m, n))

        @pl.when((t < chunks) & (t != 1))
        def _():
            take_own(lax.rem(t, 2), gph, gpl, t * GK)

        @pl.when(t == 0)
        def _():
            take_own(1, gph, gpl, GK)
            for n in range(parts):
                for copy in e_copy(n):
                    copy.wait()
            lax.fori_loop(0, chunks, load_x, 0)

        p = at(t, ends, makes)

        @pl.when(p >= 0)
        def _():
            multiply_group(p)

        q = at(t, ends, finishes)

        @pl.when(q >= 0)
        def _():
            finish_group(q)

        @pl.when((t == 2) & helper)
        def _():
            far_exponentials()

        @pl.when(t == cuts[1])
        def _():
            pltpu.make_async_copy(xparts, x2, x_sem).wait()
            total = collect(mine, vecr, vec_send, vec_recv, c, cells, in_plane)
            spot_sum = collect(loss, lossr, loss_send, loss_recv, z, planes, in_column)
            weight[...] = jnp.broadcast_to(counts[...].astype(F32)[None, :], (128, C)).T
            cols[0:1, :] = vec[8:9, :]
            cols[1:2, :] = total[0:1, :] + vec[9:10, :]
            losses[...] = jnp.zeros_like(losses)
            losses[0:1, :] = loss[2:3, :] - total[1:2, 0:128] / G - spot_sum[0:1, :] / loss[1:2, :]

        for stage in range(last + 1):
            begin = cuts[stage + 1]
            steps = cuts[stage + 2] - begin if stage < last else count
            each = -(-count // steps)

            @pl.when((t >= begin) & (t < begin + steps))
            def _():
                if stage > 0:

                    @pl.when(t == begin)
                    def _():
                        for j in range(count - 2, count):
                            out_copy(j).wait()
                        in_copy(0).start()

                def one(j, _):
                    stored_part(j, stage)
                    return 0

                lax.fori_loop(
                    jnp.minimum((t - begin) * each, count), jnp.minimum((t - begin + 1) * each, count), one, 0
                )

        return 0

    lax.fori_loop(0, slots, step, 0)

    for p in range(groups - zslots, groups):
        for h in range(2):

            @pl.when(had(p, h))
            def _():
                for n in range(group):
                    sent(p % zslots, n, h)

    for j in range(count - 2, count):
        out_copy(j).wait()

    def drain(g, _):
        n = rank(lax.div(g, per), lax.rem(g, per))
        drain_own(g)

        @pl.when(helper & (n < handed))
        def _():
            drain_far(n)

        @pl.when(at_end & (n < handed))
        def _():
            row_copy(n, g).wait_send()

        return 0

    lax.fori_loop(0, chunks, drain, 0)


def backward(cfg, ehi, elo, xparts, far_logits, vec, loss, counts, gp, spent):
    cells, planes, C, S, G, GK, r = (cfg[k] for k in ("cells", "planes", "C", "S", "G", "GK", "r"))
    chips, per, chunks = cells // 2, G // planes // GK, G // GK
    parts, tile, group, zslots = cfg["parts"], cfg["tile"], cfg["group"], cfg["zslots"]
    rows, handed = C // parts, cfg["handed"]
    sem = pltpu.SemaphoreType.DMA
    scratch = [
        pltpu.VMEM((parts, 2 * rows, S), BF16), pltpu.VMEM((parts, 2 * rows, G), BF16),
        pltpu.VMEM((parts // 2, 2 * rows, S), BF16),
        pltpu.VMEM((G, S), BF16), pltpu.VMEM((G, S), BF16), pltpu.VMEM((2, GK, S), BF16),
        pltpu.VMEM((2, chips, 2, r, S), F32), pltpu.VMEM((group, chips, 2, r, S), F32),
        pltpu.VMEM((2, cfg["piece"], S), F32), pltpu.VMEM((group, 2, C // 2, GK), F32),
        pltpu.VMEM((zslots, group, 2, C // 2, GK), F32), pltpu.VMEM((2, rows, tile), F32), pltpu.VMEM((2, rows, tile), F32),
        pltpu.VMEM((8, S), F32), pltpu.VMEM((cells, 8, S), F32), pltpu.VMEM((planes, 8, 128), F32), pltpu.VMEM((C, 128), F32),
        sem((2, parts)), sem, sem((2,)), sem((chunks, chips)), sem((chunks,)), sem((chunks, 2)),
        sem((handed, chips)), sem((handed,)), sem((handed, 2)),
        sem((handed,)), sem((handed,)), sem((2,)), sem((group,)),
        sem((chunks + per, 2)), sem((zslots, group, 2)), sem((group, 2)), sem((2,)), sem((2,)),
        sem((cells,)), sem((cells,)), sem((planes,)), sem((planes,)),
    ]
    return pl.pallas_call(
        functools.partial(backward_kernel, cfg),
        out_shape=(
            jax.ShapeDtypeStruct((C, S), F32),
            jax.ShapeDtypeStruct((C, G // planes), F32),
            jax.ShapeDtypeStruct((8, 128), F32),
            jax.ShapeDtypeStruct((chunks, chips, 2, r, S), F32),
            jax.ShapeDtypeStruct((cfg["handed"], chips, 2, r, S), F32),
            jax.ShapeDtypeStruct((chunks, C, GK), F32),
            jax.ShapeDtypeStruct((per, C, GK), F32),
        ),
        in_specs=[ANY, ANY, ANY, ANY, VMEM, VMEM, VMEM, ANY, ANY],
        out_specs=(ANY, ANY, VMEM, ANY, ANY, ANY, ANY),
        input_output_aliases={7: 3, 8: 5},
        scratch_shapes=scratch,
        compiler_params=pltpu.CompilerParams(
            collective_id=1, has_side_effects=True, vmem_limit_bytes=61 * 2**20
        ),
        cost_estimate=pl.CostEstimate(flops=12 * C * S * G, bytes_accessed=16 * C * S, transcendentals=0),
        name="backward",
    )(ehi, elo, xparts, far_logits, vec, loss, counts, gp, spent)


def passing_kernel(pieces, losses, first, second, out_losses, out_first, out_second, *rest):
    buffers, (read, write) = rest[:2], rest[2:]
    moves = []
    for n, (source, target) in enumerate(((first, out_first), (second, out_second))):
        rows = source.shape[0] // pieces[n]
        for i in range(pieces[n]):
            place = pl.ds(i * rows, rows)
            slot = len(moves)
            moves.append(
                (
                    pltpu.make_async_copy(source.at[place], buffers[n].at[place], read.at[slot]),
                    pltpu.make_async_copy(buffers[n].at[place], target.at[place], write.at[slot]),
                )
            )
    for load, _ in moves:
        load.start()
    for n in range(2):
        out_losses[n] = losses[0, n]
    for load, store in moves:
        load.wait()
        store.start()
    for _, store in moves:
        store.wait()


def passing(losses, first, second):
    pieces = [8, 2]
    smem = pl.BlockSpec(memory_space=pltpu.SMEM)
    return pl.pallas_call(
        functools.partial(passing_kernel, pieces),
        out_shape=(
            jax.ShapeDtypeStruct((2,), F32),
            jax.ShapeDtypeStruct(first.shape, first.dtype),
            jax.ShapeDtypeStruct(second.shape, second.dtype),
        ),
        in_specs=[smem, ANY, ANY],
        out_specs=(smem, ANY, ANY),
        scratch_shapes=[
            pltpu.VMEM(first.shape, first.dtype), pltpu.VMEM(second.shape, second.dtype),
            pltpu.SemaphoreType.DMA((sum(pieces),)), pltpu.SemaphoreType.DMA((sum(pieces),)),
        ],
        compiler_params=pltpu.CompilerParams(vmem_limit_bytes=60 * 2**20),
        name="passing",
    )(losses, first, second)


def local(cells, planes, logits, expression, spatial, cell_counts, spot_density, slide_id, padding):
    C, S = logits.shape
    G = expression.shape[1] * planes
    GK = max(128, 8 * cells)
    chunks, parts, group = G // GK, 4, 256 // GK
    tile = 256 * group
    across = 1
    while across * across < cells // 2:
        across *= 2
    cfg = dict(
        cells=cells, planes=planes, C=C, S=S, G=G, GK=GK, r=GK // cells, rows=128, tile=tile, parts=parts,
        group=group, zslots=1 + group, slots=max(chunks + parts * (S // tile), 5 + group + 2 * (chunks - group)), pieces=8, ahead=5, handed=chunks // 4,
        across=across, helped=planes >= 4, piece=max(n for n in range(16, 65, 16) if C // parts % n == 0),
    )
    counts = cell_counts
    gath, ehi, elo, xparts, far_logits, gp, vec, loss = forward(
        cfg, logits, expression, spatial, counts, spot_density[None, :],
        slide_id[None, :], padding[None, :],
    )
    grad_logits, grad_expression, losses, *_ = backward(
        cfg, ehi, elo, xparts, far_logits, vec, loss, counts, gp, gath
    )
    return passing(losses, grad_logits, grad_expression)


def solution(mesh):
    cells, planes = mesh.shape["cell"], mesh.shape["spot"]
    in_specs = (
        P("cell", "spot"), P("cell", "spot"), P("cell", "spot"), P("cell"), P("spot"), P("spot"), P("spot"),
    )
    out_specs = (P(), P("cell", "spot"), P("cell", "spot"))
    return jax.shard_map(
        functools.partial(local, cells, planes), mesh=mesh, in_specs=in_specs, out_specs=out_specs, check_vma=False
    )
```

```python
import functools

import jax
import jax.numpy as jnp
from jax import lax
from jax.experimental import pallas as pl
from jax.experimental.pallas import tpu as pltpu
from jax.sharding import PartitionSpec as P

epsilon = 1e-06
MESH = pl.DeviceIdType.MESH
F32, BF16 = jnp.float32, jnp.bfloat16
TN = (((0,), (0,)), ((), ()))
NN = (((1,), (0,)), ((), ()))
NT = (((1,), (1,)), ((), ()))


def dot(left, right, dims=NN):
    return lax.dot_general(left, right, dims, preferred_element_type=F32)


def split(v):
    high = v.astype(BF16)
    return high, (v - high.astype(F32)).astype(BF16)


def arrival(z, i, planes, per):
    near = jnp.minimum(z, planes - 1 - z)
    j = jnp.maximum(i - per, 0)
    pair = lax.rem(j, 2 * per)
    t = 1 + lax.div(j, 2 * per)
    both = jnp.where(lax.rem(pair, 2) == 0, z - t, z + t)
    late = jnp.maximum(j - 2 * near * per, 0)
    t = near + 1 + lax.div(late, per)
    one = jnp.where(z < planes - 1 - z, z + t, z - t)
    in_pairs = j < 2 * near * per
    shard = jnp.where(i < per, z, jnp.where(in_pairs, both, one))
    chunk = jnp.where(i < per, i, jnp.where(in_pairs, lax.div(pair, 2), lax.rem(late, per)))
    return shard, chunk


def greet(c, z, cells, planes):
    barrier = pltpu.get_barrier_semaphore()

    def in_plane(step, _):
        pl.semaphore_signal(barrier, inc=1, device_id=(lax.rem(c + step, cells), z), device_id_type=MESH)
        return 0

    def in_column(step, _):
        pl.semaphore_signal(barrier, inc=1, device_id=(c, lax.rem(z + step, planes)), device_id_type=MESH)
        return 0

    lax.fori_loop(1, cells, in_plane, 0)
    lax.fori_loop(1, planes, in_column, 0)
    pl.semaphore_wait(barrier, cells + planes - 2)


def share(src, dst, send, recv, me, count, device):
    def start(step, _):
        other = lax.rem(me + step, count)
        pltpu.make_async_remote_copy(
            src_ref=src, dst_ref=dst.at[me], send_sem=send.at[other], recv_sem=recv.at[me],
            device_id=device(other), device_id_type=MESH,
        ).start()
        return 0

    lax.fori_loop(1, count, start, 0)


def collect(src, dst, send, recv, me, count, device):
    def wait(step, total):
        other = lax.rem(me + step, count)
        copy = pltpu.make_async_remote_copy(
            src_ref=src, dst_ref=dst.at[other], send_sem=send.at[other], recv_sem=recv.at[other],
            device_id=device(other), device_id_type=MESH,
        )
        copy.wait_send()
        copy.wait_recv()
        return total + dst[other]

    return lax.fori_loop(1, count, wait, src[...])


def forward_kernel(
    cfg, logits, expr, spatial, counts, dens, slide, pad,
    gath, ehi_out, elo_out, x_out, far_logits, gp_out, vec_out, loss_out,
    ehi, elo, lbuf, stage, xparts, amat, partial, corer, half, chipr, pred, spat,
    tots, totr, acc, spots, spotr, gcol, gst, gstr, vec,
    g_recv, up_send, down_send, l_sem, st_sem, put_sem, core_send, core_recv, chip_send, chip_recv,
    far_send, far_recv, spat_send, spat_recv, tot_send, tot_recv, spot_send, spot_recv, gst_send, gst_recv, out_sem,
):
    cells, planes, C, S, G, GK, r = (cfg[k] for k in ("cells", "planes", "C", "S", "G", "GK", "r"))
    chips, per, chunks = cells // 2, G // planes // GK, G // GK
    rows, tile, parts, helped = cfg["rows"], cfg["tile"], cfg["parts"], cfg["helped"]
    part, pieces = C // parts, cfg["pieces"]
    own_genes = G // cells
    c, z = lax.axis_index("cell"), lax.axis_index("spot")
    chip, core = lax.div(c, 2), lax.rem(c, 2)
    sibling = c + 1 - 2 * core
    in_plane = lambda other: (other, z)
    in_column = lambda other: (c, other)

    greet(c, z, cells, planes)

    def z_copy(src, g, to, send):
        return pltpu.make_async_remote_copy(
            src_ref=src, dst_ref=gath.at[g], send_sem=send.at[g], recv_sem=g_recv.at[g],
            device_id=(c, to), device_id_type=MESH,
        )

    up, down = jnp.minimum(z + 1, planes - 1), jnp.maximum(z - 1, 0)

    def send_own(k, _):
        g = z * per + k
        src = expr.at[:, pl.ds(pl.multiple_of(k * GK, 128), GK)]

        @pl.when(z < planes - 1)
        def _():
            z_copy(src, g, up, up_send).start()

        @pl.when(z > 0)
        def _():
            z_copy(src, g, down, down_send).start()

        return 0

    lax.fori_loop(0, per, send_own, 0)

    at_end = (z == 0) | (z == planes - 1)
    helper = ((z == 1) | (z == planes - 2)) & helped
    beside = jnp.where(z == 0, 1, jnp.where(z == planes - 1, planes - 2, jnp.where(z == 1, 0, planes - 1)))
    piece = C // 2 // pieces

    def far_copy(n):
        return pltpu.make_async_remote_copy(
            src_ref=logits.at[pl.ds(pl.multiple_of(C // 2 + n * piece, 8), piece)],
            dst_ref=far_logits.at[pl.ds(pl.multiple_of(n * piece, 8), piece)],
            send_sem=far_send.at[n], recv_sem=far_recv.at[n], device_id=(c, beside), device_id_type=MESH,
        )

    blocks = own_genes // r

    def spat_copy(b):
        place = c * blocks + b
        g, owner = lax.div(place, cells), lax.rem(place, cells)
        src = spatial.at[pl.ds(pl.multiple_of(b * r, 8), r)]
        remote = pltpu.make_async_remote_copy(
            src_ref=src, dst_ref=spat.at[g], send_sem=spat_send.at[b], recv_sem=spat_recv.at[g],
            device_id=(owner, z), device_id_type=MESH,
        )
        local = pltpu.make_async_copy(src, spat.at[g], spat_recv.at[g])
        return owner, remote, local

    def send_spat(b, _):
        owner, remote, local = spat_copy(b)

        @pl.when(owner != c)
        def _():
            remote.start()

        @pl.when(owner == c)
        def _():
            local.start()

        return 0

    lax.fori_loop(0, blocks, send_spat, 0)

    def load(t):
        return pltpu.make_async_copy(
            logits.at[pl.ds(pl.multiple_of(t * rows, rows), rows)], lbuf.at[lax.rem(t, 2)], l_sem.at[lax.rem(t, 2)]
        )

    load(0).start()

    def exps(t, _):
        @pl.when(t + 1 < C // rows)
        def _():
            load(t + 1).start()

        load(t).wait()
        high, low = split(jnp.exp(lbuf[lax.rem(t, 2)]))
        place = pl.ds(pl.multiple_of(t * rows, rows), rows)
        ehi[place, :] = high
        elo[place, :] = low
        return 0

    lax.fori_loop(0, C // rows, exps, 0)
    keep = [pltpu.make_async_copy(ehi, ehi_out, out_sem.at[0]), pltpu.make_async_copy(elo, elo_out, out_sem.at[1])]
    for copy in keep:
        copy.start()

    row = lax.broadcasted_iota(jnp.int32, (16, C), 0)
    weight = jnp.broadcast_to(counts[...].astype(F32)[None, :], (16, C))
    lhs = jnp.where(row == 0, 1.0, jnp.where(row == 1, weight, 0.0)).astype(BF16)

    def sums(t, _):
        place = pl.ds(pl.multiple_of(t * tile, tile), tile)
        both = dot(lhs, ehi[:, place]) + dot(lhs, elo[:, place])
        tots[:, place] = both[:8]
        return 0

    lax.fori_loop(0, S // tile, sums, 0)
    share(tots, totr, tot_send, tot_recv, c, cells, in_plane)

    valid = (1 - pad[...]).astype(F32)
    mask0 = valid * (slide[...] == 0).astype(F32)
    mask1 = valid * (slide[...] == 1).astype(F32)
    vec[4:5, :] = mask0
    vec[5:6, :] = mask1
    acc[...] = jnp.zeros_like(acc)
    gcol[...] = jnp.zeros_like(gcol)

    def core_copy(g, slot):
        return pltpu.make_async_remote_copy(
            src_ref=partial.at[slot, :, 1 - core], dst_ref=corer.at[g], send_sem=core_send.at[slot],
            recv_sem=core_recv.at[g], device_id=(sibling, z), device_id_type=MESH,
        )

    def chip_copy(g, slot, other):
        return pltpu.make_async_remote_copy(
            src_ref=half.at[slot, other], dst_ref=chipr.at[g, chip], send_sem=chip_send.at[slot, other],
            recv_sem=chip_recv.at[g, chip], device_id=(2 * other + core, z), device_id_type=MESH,
        )

    def chip_wait(g, slot, other):
        return pltpu.make_async_remote_copy(
            src_ref=half.at[slot, chip], dst_ref=chipr.at[g, other], send_sem=chip_send.at[slot, other],
            recv_sem=chip_recv.at[g, other], device_id=(2 * other + core, z), device_id_type=MESH,
        )

    def product(i):
        d, k = arrival(z, i, planes, per)
        g, slot = d * per + k, lax.rem(i, 2)
        own = pltpu.make_async_copy(expr.at[:, pl.ds(pl.multiple_of(k * GK, 128), GK)], stage, st_sem)
        pull = pltpu.make_async_copy(gath.at[g], stage, st_sem)

        @pl.when(d == z)
        def _():
            own.start()

        @pl.when(d != z)
        def _():
            z_copy(gath.at[g], g, down, down_send).wait_recv()

        @pl.when((d < z) & (z < planes - 1))
        def _():
            z_copy(gath.at[g], g, up, up_send).start()

        @pl.when((d > z) & (z > 0))
        def _():
            z_copy(gath.at[g], g, down, down_send).start()

        @pl.when(d != z)
        def _():
            pull.start()

        pull.wait()
        @pl.when(i >= 2)
        def _():
            core_copy(g, slot).wait_send()

        def turn(t, _):
            place = pl.ds(pl.multiple_of(t * 128, 128), 128)
            high, low = split(stage[place, :].T)
            amat[:GK, place] = high
            amat[GK:, place] = low
            return 0

        lax.fori_loop(0, C // 128, turn, 0)

        def multiply(t, _):
            place = pl.ds(pl.multiple_of(t * tile, tile), tile)
            both = dot(amat[...], ehi[:, place])
            total = both[:GK] + both[GK:] + dot(amat[:GK, :], elo[:, place])
            partial[slot, :, :, :, place] = total.reshape(chips, 2, r, tile)
            return 0

        lax.fori_loop(0, S // tile, multiply, 0)
        core_copy(g, slot).start()
        columns = pl.ds(pl.multiple_of(g * GK, 128), GK)

        @pl.when(i >= 1)
        def _():
            pltpu.make_async_copy(xparts, x_out.at[:, :, columns], put_sem).wait()

        def keep_parts(t, _):
            high, low = split(stage[pl.ds(pl.multiple_of(t * part, 16), part), :])
            xparts[t, pl.ds(0, part), :] = high
            xparts[t, pl.ds(part, part), :] = low
            return 0

        lax.fori_loop(0, parts, keep_parts, 0)
        pltpu.make_async_copy(xparts, x_out.at[:, :, columns], put_sem).start()

    def to_chips(i):
        d, k = arrival(z, i, planes, per)
        g, slot = d * per + k, lax.rem(i, 2)
        core_copy(g, slot).wait_recv()

        @pl.when(i >= 2)
        def _():
            def drain(step, _):
                chip_copy(g, slot, lax.rem(chip + step, chips)).wait_send()
                return 0

            lax.fori_loop(1, chips, drain, 0)

        def add(other, _):
            half[slot, other] = partial[slot, other, core] + corer[g, other]

            @pl.when(other != chip)
            def _():
                chip_copy(g, slot, other).start()

            return 0

        lax.fori_loop(0, chips, add, 0)

    def finish(i):
        d, k = arrival(z, i, planes, per)
        g, slot = d * per + k, lax.rem(i, 2)
        pltpu.make_async_copy(spat.at[g], spat.at[g], spat_recv.at[g]).wait()

        def add(step, total):
            other = lax.rem(chip + step, chips)
            chip_wait(g, slot, other).wait_recv()
            return total + chipr[g, other]

        p = lax.fori_loop(1, chips, add, half[slot, chip]) * vec[0:1, :]
        s = spat[g]
        pred[g] = p
        ps, pp, ss = p * s, p * p, s * s
        acc[0] += ps
        acc[1] += pp
        acc[2] += ss
        lane = lax.broadcasted_iota(jnp.int32, (r, 128), 1)
        cols = jnp.zeros((r, 128), F32)
        for n, v in enumerate((ps, pp, ss)):
            for m in range(2):
                one = jnp.sum(v * vec[4 + m : 5 + m, :], axis=1, keepdims=True)
                cols = jnp.where(lane == 2 * n + m, one, cols)
        gcol[pl.ds(pl.multiple_of(g * r, 8), r), :] = cols

    def step(i, _):
        @pl.when((i >= per) & (i < per + pieces) & at_end & helped)
        def _():
            far_copy(i - per).start()

        @pl.when(i < chunks)
        def _():
            product(i)

        @pl.when(i == 1)
        def _():
            total = collect(tots, totr, tot_send, tot_recv, c, cells, in_plane)
            vec[0:1, :] = 1.0 / total[0:1, :]
            vec[1:2, :] = total[1:2, :] / total[0:1, :]
            gst[...] = jnp.zeros_like(gst)
            density = vec[1:2, :]
            target = dens[...]
            lane = lax.broadcasted_iota(jnp.int32, (1, gst.shape[1]), 1)
            logs = target * jnp.log(target), target * jnp.log(density)
            for n, v in enumerate((jnp.ones_like(target), target, density, *logs)):
                line = jnp.zeros((1, gst.shape[1]), F32)
                for m in range(2):
                    one = jnp.sum(v * vec[4 + m : 5 + m, :], axis=1, keepdims=True)
                    line = jnp.where(lane == m, one, line)
                gst[8 + n : 9 + n, :] = line

        @pl.when((i >= 1) & (i <= chunks))
        def _():
            to_chips(i - 1)

        @pl.when(i >= 2)
        def _():
            finish(i - 2)

        return 0

    lax.fori_loop(0, chunks + 2, step, 0)

    spots[...] = jnp.zeros_like(spots)
    for n in range(3):
        spots[n : n + 1, :] = jnp.sum(acc[n], axis=0, keepdims=True)
    share(spots, spotr, spot_send, spot_recv, c, cells, in_plane)
    gst[0:8, :] = gcol[...].T[0:8, :]
    share(gst, gstr, gst_send, gst_recv, z, planes, in_column)

    genes = collect(gst, gstr, gst_send, gst_recv, z, planes, in_column)
    dot_g, aa_g, bb_g = ([genes[2 * n + m : 2 * n + m + 1, :] for m in range(2)] for n in range(3))
    slides = [[genes[8 + n : 9 + n, m : m + 1] for m in range(2)] for n in range(5)]
    lines, cos_sums, own_losses = [], [], []
    for m in range(2):
        norm = jnp.sqrt((aa_g[m] + epsilon) * (bb_g[m] + epsilon))
        cos = dot_g[m] / norm
        lines += [-1.0 / (norm * G), cos / ((aa_g[m] + epsilon) * G)]
        cos_sums.append(jnp.sum(cos, axis=1, keepdims=True))
    lines.append(jnp.zeros((124, gst.shape[1]), F32))
    gcol[...] = jnp.concatenate(lines, axis=0).T
    live = [jnp.maximum(v, 1.0) for v in slides[0]]
    mass_target, mass_pred = slides[1], slides[2]
    divergence = [
        (slides[3][m] - slides[4][m]) / mass_target[m] - jnp.log(mass_target[m]) + jnp.log(mass_pred[m])
        for m in range(2)
    ]
    mask0, mask1 = vec[4:5, :], vec[5:6, :]
    grad_density = (
        mask0 / mass_pred[0] + mask1 / mass_pred[1]
        - dens[...] * (mask0 / mass_target[0] + mask1 / mass_target[1]) / vec[1:2, :]
    )
    spot_weight = mask0 / live[0] + mask1 / live[1]

    spot = collect(spots, spotr, spot_send, spot_recv, c, cells, in_plane)
    norm = jnp.sqrt((spot[1:2, :] + epsilon) * (spot[2:3, :] + epsilon))
    spot_cos = spot[0:1, :] / norm
    inverse = vec[0:1, :]
    vec[2:3, :] = -spot_weight / norm
    vec[3:4, :] = spot_weight * spot_cos / (spot[1:2, :] + epsilon)
    vec[6:7, :] = grad_density * inverse
    vec[7:8, :] = vec[1:2, :] * grad_density * inverse
    acc[0] = jnp.zeros((r, S), F32)

    def gradient(g, _):
        columns = gcol[pl.ds(pl.multiple_of(g * r, 8), r), :]
        by_spatial = vec[4:5, :] * columns[:, 0:1] + vec[5:6, :] * columns[:, 2:3] + vec[2:3, :]
        by_pred = vec[4:5, :] * columns[:, 1:2] + vec[5:6, :] * columns[:, 3:4] + vec[3:4, :]
        p = pred[g]
        value = (spat[g] * by_spatial + p * by_pred) * vec[0:1, :]
        acc[0] += p * value
        pred[g] = value
        pltpu.make_async_copy(pred.at[g], gp_out.at[g, chip, core], out_sem.at[2]).start()
        return 0

    lax.fori_loop(0, chunks, gradient, 0)
    copy = pltpu.make_async_copy(pred, gp_out.at[:, chip, core], out_sem.at[2])
    vec_out[...] = jnp.zeros_like(vec_out)
    vec_out[0:1, :] = jnp.sum(acc[0], axis=0, keepdims=True)
    vec_out[8:9, :] = vec[6:7, :]
    vec_out[9:10, :] = vec[7:8, :]
    lane = lax.broadcasted_iota(jnp.int32, (1, 128), 1)
    vec_out[1:2, 0:128] = jnp.where(lane == 0, cos_sums[0], jnp.where(lane == 1, cos_sums[1], 0.0))
    spot_sums = [jnp.sum(vec[4 + m : 5 + m, :] * spot_cos, axis=1, keepdims=True) for m in range(2)]
    loss_out[...] = jnp.zeros_like(loss_out)
    for n, v in enumerate((spot_sums, live, divergence)):
        loss_out[n : n + 1, :] = jnp.where(lane == 0, v[0], jnp.where(lane == 1, v[1], 0.0))

    copy.wait()
    for copy in keep:
        copy.wait()
    pltpu.make_async_copy(xparts, x_out.at[:, :, pl.ds(0, GK)], put_sem).wait()

    def drain_far(n, _):
        @pl.when(at_end & helped)
        def _():
            far_copy(n).wait_send()

        @pl.when(helper)
        def _():
            far_copy(n).wait_recv()

        return 0

    lax.fori_loop(0, pieces, drain_far, 0)

    def drain_z(g, _):
        d = lax.div(g, per)

        @pl.when((d <= z) & (z < planes - 1))
        def _():
            z_copy(gath.at[g], g, up, up_send).wait_send()

        @pl.when((d >= z) & (z > 0))
        def _():
            z_copy(gath.at[g], g, down, down_send).wait_send()

        return 0

    lax.fori_loop(0, chunks, drain_z, 0)

    def drain_spat(b, _):
        owner, remote, _ = spat_copy(b)

        @pl.when(owner != c)
        def _():
            remote.wait_send()

        return 0

    lax.fori_loop(0, blocks, drain_spat, 0)
    for slot in range(2):
        core_copy(0, slot).wait_send()

        def drain(step, _):
            chip_copy(0, slot, lax.rem(chip + step, chips)).wait_send()
            return 0

        lax.fori_loop(1, chips, drain, 0)


ANY = pl.BlockSpec(memory_space=pl.ANY)
VMEM = pl.BlockSpec(memory_space=pltpu.VMEM)


def forward(cfg, logits, expression, spatial, counts, dens, slide, pad):
    cells, planes, C, S, G, GK, r = (cfg[k] for k in ("cells", "planes", "C", "S", "G", "GK", "r"))
    chips, per, chunks = cells // 2, G // planes // GK, G // GK
    rows = cfg["rows"]
    wide = max(G // cells, 128)
    blocks = G // cells // r
    sem = pltpu.SemaphoreType.DMA
    scratch = [
        pltpu.VMEM((C, S), BF16), pltpu.VMEM((C, S), BF16), pltpu.VMEM((2, rows, S), F32),
        pltpu.VMEM((C, GK), F32), pltpu.VMEM((cfg["parts"], 2 * C // cfg["parts"], GK), BF16), pltpu.VMEM((2 * GK, C), BF16),
        pltpu.VMEM((2, chips, 2, r, S), F32), pltpu.VMEM((chunks, chips, r, S), F32),
        pltpu.VMEM((2, chips, r, S), F32), pltpu.VMEM((chunks, chips, r, S), F32),
        pltpu.VMEM((chunks, r, S), F32), pltpu.VMEM((chunks, r, S), F32),
        pltpu.VMEM((8, S), F32), pltpu.VMEM((cells, 8, S), F32), pltpu.VMEM((3, r, S), F32),
        pltpu.VMEM((8, S), F32), pltpu.VMEM((cells, 8, S), F32), pltpu.VMEM((wide, 128), F32),
        pltpu.VMEM((16, wide), F32), pltpu.VMEM((planes, 16, wide), F32), pltpu.VMEM((8, S), F32),
        sem((chunks,)), sem((chunks,)), sem((chunks,)), sem((2,)), sem, sem,
        sem((2,)), sem((chunks,)), sem((2, chips)), sem((chunks, chips)),
        sem((cfg["pieces"],)), sem((cfg["pieces"],)),
        sem((blocks,)), sem((chunks,)), sem((cells,)), sem((cells,)), sem((cells,)), sem((cells,)),
        sem((planes,)), sem((planes,)), sem((3,)),
    ]
    flops = 6 * C * S * G
    return pl.pallas_call(
        functools.partial(forward_kernel, cfg),
        out_shape=(
            jax.ShapeDtypeStruct((chunks, C, GK), F32),
            jax.ShapeDtypeStruct((C, S), BF16),
            jax.ShapeDtypeStruct((C, S), BF16),
            jax.ShapeDtypeStruct((cfg["parts"], 2 * C // cfg["parts"], G), BF16),
            jax.ShapeDtypeStruct((C // 2, S), F32),
            jax.ShapeDtypeStruct((chunks, chips, 2, r, S), F32),
            jax.ShapeDtypeStruct((16, S), F32),
            jax.ShapeDtypeStruct((8, 128), F32),
        ),
        in_specs=[ANY, ANY, ANY, VMEM, VMEM, VMEM, VMEM],
        out_specs=(ANY, ANY, ANY, ANY, ANY, ANY, VMEM, VMEM),
        scratch_shapes=scratch,
        compiler_params=pltpu.CompilerParams(
            collective_id=0, has_side_effects=True, vmem_limit_bytes=56 * 2**20
        ),
        cost_estimate=pl.CostEstimate(flops=flops, bytes_accessed=8 * C * S, transcendentals=C * S),
        name="forward",
    )(logits, expression, spatial, counts, dens, slide, pad)


def backward_kernel(
    cfg, ehi, elo, xparts, far_logits, vec, loss, counts, _gp, _gath,
    grad_logits, grad_expr, losses, land, far_land, zland, zlast,
    e2, x2, e3, gph, gpl, far_g, gstage, fstage, lbuf, zst, zsend, outst, inst, cols, vecr, lossr, weight,
    e_sem, x_sem, l_sem, g_recv, g_pair, g_sent, f_recv, f_pair, f_sent, row_recv, row_sent, gs_sem, fs_sem,
    z_recv, zs_sem, zst_sem, out_sem, in_sem, vec_send, vec_recv, loss_send, loss_recv,
):
    cells, planes, C, S, G, GK, r = (cfg[k] for k in ("cells", "planes", "C", "S", "G", "GK", "r"))
    chips, per, chunks = cells // 2, G // planes // GK, G // GK
    parts, tile, slots, group, zslots = (cfg[k] for k in ("parts", "tile", "slots", "group", "zslots"))
    ahead = cfg["ahead"]
    handed = cfg["handed"]
    count, groups = parts * (S // tile), chunks // group
    cuts = (0, chunks // 2, chunks)
    last = len(cuts) - 2
    helped, across = cfg["helped"], cfg["across"]
    rows, tiles, halves = C // parts, S // tile, parts // 2
    piece = cfg["piece"]
    pieces = C // 2 // piece
    down_chips = chips // across
    c, z = lax.axis_index("cell"), lax.axis_index("spot")
    chip, core = lax.div(c, 2), lax.rem(c, 2)
    chip_row, chip_col = lax.div(chip, across), lax.rem(chip, across)
    sibling = c + 1 - 2 * core
    in_plane = lambda other: (other, z)
    in_column = lambda other: (c, other)
    at_end = ((z == 0) | (z == planes - 1)) & helped
    helper = ((z == 1) | (z == planes - 2)) & helped
    beside = jnp.where(z == 0, 1, jnp.where(z == planes - 1, planes - 2, jnp.where(z == 1, 0, planes - 1)))

    def order(i):
        d, k = arrival(z, chunks - 1 - i, planes, per)
        return d, k, d * per + k

    greet(c, z, cells, planes)

    def spread(land, recv, pair, sent, buffer, ready):
        def copy(ref, source, g, other):
            return pltpu.make_async_remote_copy(
                src_ref=ref, dst_ref=ref, send_sem=sent.at[g, 0], recv_sem=recv.at[g, source],
                device_id=(2 * other + core, z), device_id_type=MESH,
            )

        def along_row(n):
            return chip_row * across + lax.rem(chip_col + n, across)

        def along_col(n):
            return lax.rem(chip_row + n, down_chips) * across + chip_col

        def each(count, body):
            def one(n, _):
                body(n)
                return 0

            lax.fori_loop(1, count, one, 0)

        def send(g):
            own = land.at[g, chip, core]
            each(across, lambda n: copy(own, chip, g, along_row(n)).start())
            each(down_chips, lambda n: copy(own, chip, g, along_col(n)).start())

        def landed(g, source):
            ref = land.at[g, source, core]
            pltpu.make_async_copy(ref, ref, recv.at[g, source]).wait()

        def first_hop(g):
            def from_row(n):
                source = along_row(n)
                landed(g, source)
                half = land.at[g, source, core, :, pl.ds(0, S // 2)]
                each(down_chips, lambda m: copy(half, source, g, along_col(m)).start())

            def from_col(n):
                source = along_col(n)
                landed(g, source)
                half = land.at[g, source, core, :, pl.ds(S // 2, S // 2)]
                each(across, lambda m: copy(half, source, g, along_row(m)).start())

            each(across, from_row)
            each(down_chips, from_col)

        def to_sibling(g):
            ref = land.at[g, :, core]
            return pltpu.make_async_remote_copy(
                src_ref=ref, dst_ref=ref, send_sem=sent.at[g, 1], recv_sem=pair.at[g],
                device_id=(sibling, z), device_id_type=MESH,
            )

        def second_hop(g):
            def from_rest(n):
                other = lax.rem(chip_row + 1 + lax.div(n - 1, across - 1), down_chips) * across
                landed(g, other + lax.rem(chip_col + 1 + lax.rem(n - 1, across - 1), across))

            each((across - 1) * (down_chips - 1) + 1, from_rest)
            to_sibling(g).start()

        def stage(g, slot):
            ref = land.at[g, :, 1 - core]
            pltpu.make_async_copy(ref, ref, pair.at[g]).wait()
            pltpu.make_async_copy(land.at[g], buffer.at[slot], ready.at[slot]).start()

        def take(slot, high_ref, low_ref, first):
            pltpu.make_async_copy(buffer.at[slot], buffer.at[slot], ready.at[slot]).wait()

            def split_tile(t, _):
                place = pl.ds(pl.multiple_of(t * 128, 128), 128)
                high, low = split(buffer[slot, :, :, :, place].reshape(GK, 128))
                lines = pl.ds(pl.multiple_of(first, 128), GK)
                high_ref[lines, place] = high
                low_ref[lines, place] = low
                return 0

            lax.fori_loop(0, S // 128, split_tile, 0)

        def drain(g):
            direct = land.at[g, pl.ds(0, chips - 1), 0]
            pltpu.make_async_copy(direct, direct, sent.at[g, 0]).wait()
            to_sibling(g).wait_send()

        return send, first_hop, second_hop, stage, take, drain

    send_own, first_own, second_own, stage_own, take_own, drain_own = spread(
        land, g_recv, g_pair, g_sent, gstage, gs_sem
    )
    send_far, first_far, second_far, stage_far, take_far, drain_far = spread(
        far_land, f_recv, f_pair, f_sent, fstage, fs_sem
    )

    def rank(d, k):
        end = jnp.where(at_end, z, beside)
        return (planes - 1 - jnp.abs(d - end)) * per + per - 1 - k

    def row_copy(n, g):
        return pltpu.make_async_remote_copy(
            src_ref=land.at[g, chip, core], dst_ref=far_land.at[n, chip, core],
            send_sem=row_sent.at[n], recv_sem=row_recv.at[n],
            device_id=(c, beside), device_id_type=MESH,
        )

    def announce(i):
        _, _, g = order(i)
        send_own(g)

        @pl.when(at_end & (i < handed))
        def _():
            row_copy(i, g).start()

    announce(0)
    announce(1)

    def e_copy(t):
        place = pl.ds(pl.multiple_of(t * rows, 16), rows)
        return (
            pltpu.make_async_copy(ehi.at[place], e2.at[t, pl.ds(0, rows)], e_sem.at[0, t]),
            pltpu.make_async_copy(elo.at[place], e2.at[t, pl.ds(rows, rows)], e_sem.at[1, t]),
        )

    for t in range(parts):
        for copy in e_copy(t):
            copy.start()
    def load_x(i, _):
        from_place = pl.ds(pl.multiple_of(order(i)[2] * GK, 128), GK)
        to_place = pl.ds(pl.multiple_of(i * GK, 128), GK)
        pltpu.make_async_copy(xparts.at[:, :, from_place], x2.at[:, :, to_place], x_sem).start()
        return 0

    mine = vec.at[pl.ds(0, 8)]
    share(mine, vecr, vec_send, vec_recv, c, cells, in_plane)
    share(loss, lossr, loss_send, loss_recv, z, planes, in_column)

    def far_exponentials():
        def load(n):
            return pltpu.make_async_copy(
                far_logits.at[pl.ds(pl.multiple_of(n * piece, 8), piece)], lbuf.at[lax.rem(n, 2)], l_sem.at[lax.rem(n, 2)]
            )

        for n in range(2):
            load(n).start()

        def exps(n, _):
            load(n).wait()
            high, low = split(jnp.exp(lbuf[lax.rem(n, 2)]))
            t, place = lax.div(n * piece, rows), lax.rem(n * piece, rows)
            e3[t, pl.ds(pl.multiple_of(place, 16), piece), :] = high
            e3[t, pl.ds(pl.multiple_of(rows + place, 16), piece), :] = low

            @pl.when(n + 2 < pieces)
            def _():
                load(n + 2).start()

            return 0

        lax.fori_loop(0, pieces, exps, 0)

    def far_step(n, what):
        @pl.when(helper & (n < handed))
        def _():
            what(n)

    def ask_far(n):
        row_copy(n, 0).wait_recv()
        send_far(n)

    def z_copy(land, index, number, slot, n, h, to):
        place = pl.ds(h * (C // 2), C // 2)
        return pltpu.make_async_remote_copy(
            src_ref=zsend.at[slot, n, h], dst_ref=land.at[index, place], send_sem=zs_sem.at[slot, n, h],
            recv_sem=z_recv.at[number, h], device_id=(c, to), device_id_type=MESH,
        )

    def sent(slot, n, h):
        pltpu.make_async_copy(zsend.at[slot, n, h], zsend.at[slot, n, h], zs_sem.at[slot, n, h]).wait()

    def had(p, h):
        return True if h == 0 else jnp.logical_not(at_end) | (p * group >= handed)

    def multiply_group(p):
        slot = lax.rem(p, zslots)
        lines = pl.ds(pl.multiple_of(p * group * GK, 128), group * GK)

        def half(h):
            @pl.when((p >= zslots) & had(p - zslots, h))
            def _():
                for n in range(group):
                    sent(slot, n, h)

            def multiply(t, _):
                both = dot(e2[h * halves + t], gph[lines, :], NT)
                total = both[:rows] + both[rows:] + dot(e2[h * halves + t, pl.ds(0, rows)], gpl[lines, :], NT)
                for n in range(group):
                    zsend[slot, n, h, pl.ds(pl.multiple_of(t * rows, 16), rows), :] = total[:, n * GK : (n + 1) * GK]
                return 0

            lax.fori_loop(0, halves, multiply, 0)

        half(0)

        @pl.when(had(p, 1))
        def _():
            half(1)

    def finish_group(p):
        slot = lax.rem(p, zslots)
        members = [order(p * group + n) for n in range(group)]

        def first(h):
            for n, (d, k, g) in enumerate(members):
                fetch_half(n, h, d, k, g)

        def second(h):
            for n, (d, k, g) in enumerate(members):
                finish_half(slot, n, h, d, k, g)

        first(0)

        @pl.when(had(p, 1))
        def _():
            first(1)

        second(0)

        @pl.when(had(p, 1))
        def _():
            for n, (d, k, g) in enumerate(members):

                @pl.when(helper & (rank(d, k) < handed))
                def _():
                    take_far(n, far_g.at[0], far_g.at[1], 0)

                    def more(t, _):
                        right = jnp.concatenate([far_g[0], far_g[1]], axis=0)
                        both = dot(e3[t, pl.ds(0, rows)], right, NT)
                        total = both[:, :GK] + both[:, GK:] + dot(e3[t, pl.ds(rows, rows)], far_g[0], NT)
                        zsend[slot, n, 1, pl.ds(pl.multiple_of(t * rows, 16), rows), :] += total
                        return 0

                    lax.fori_loop(0, halves, more, 0)

            second(1)

    def fetch(land, index, number, n, h):
        place = land.at[index, pl.ds(h * (C // 2), C // 2)]
        pltpu.make_async_copy(place, place, z_recv.at[number, h]).wait()
        copy = pltpu.make_async_copy(place, zst.at[n, h], zst_sem.at[n, h])
        copy.start()
        return copy

    def from_behind(h, d, k):
        comes = ((d >= z) & (z > 0)) | ((d < z) & (z < planes - 1))
        if h == 0:
            return comes
        from_end = ((z == 1) & (d >= z)) | ((z == planes - 2) & (d < z))
        return comes & jnp.logical_not(helper & from_end & (rank(d, k) < handed))

    def from_front(h, d, k):
        comes = (d == z) & (z < planes - 1)
        if h == 0:
            return comes
        return comes & jnp.logical_not(helper & (z == planes - 2) & (rank(d, k) < handed))

    def fetch_half(n, h, d, k, g):
        @pl.when(from_behind(h, d, k))
        def _():
            fetch(zland, g, g, n, h)

    def finish_half(slot, n, h, d, k, g):
        def add():
            pltpu.make_async_copy(zst.at[n, h], zst.at[n, h], zst_sem.at[n, h]).wait()

            def one(t, _):
                place = pl.ds(pl.multiple_of(t * rows, 16), rows)
                zsend[slot, n, h, place, :] += zst[n, h, place, :]
                return 0

            lax.fori_loop(0, halves, one, 0)

        @pl.when(from_behind(h, d, k))
        def _():
            add()

        @pl.when(from_front(h, d, k))
        def _():
            fetch(zlast, k, chunks + k, n, h)
            add()

        @pl.when(d > z)
        def _():
            z_copy(zland, g, g, slot, n, h, jnp.minimum(z + 1, planes - 1)).start()

        @pl.when(d < z - 1)
        def _():
            z_copy(zland, g, g, slot, n, h, jnp.maximum(z - 1, 0)).start()

        @pl.when(d == z - 1)
        def _():
            z_copy(zlast, k, chunks + k, slot, n, h, jnp.maximum(z - 1, 0)).start()

        @pl.when(d == z)
        def _():
            place = pl.ds(h * (C // 2), C // 2), pl.ds(pl.multiple_of(k * GK, 128), GK)
            pltpu.make_async_copy(zsend.at[slot, n, h], grad_expr.at[place], zs_sem.at[slot, n, h]).start()

    def tile_of(j):
        t, n = lax.div(j, tiles), lax.rem(j, tiles)
        return grad_logits.at[pl.ds(pl.multiple_of(t * rows, 8), rows), pl.ds(pl.multiple_of(n * tile, 128), tile)]

    def out_copy(j):
        return pltpu.make_async_copy(outst.at[lax.rem(j, 2)], tile_of(j), out_sem.at[lax.rem(j, 2)])

    def in_copy(j):
        return pltpu.make_async_copy(tile_of(j), inst.at[lax.rem(j, 2)], in_sem.at[lax.rem(j, 2)])

    def map_part(j, first, last):
        t, place = lax.div(j, tiles), pl.ds(pl.multiple_of(lax.rem(j, tiles) * tile, 128), tile)
        genes = pl.ds(first * GK, (last - first) * GK)
        both = dot(x2[t, :, genes], gph[genes, place])
        return both[:rows] + both[rows:] + dot(x2[t, pl.ds(0, rows), genes], gpl[genes, place])

    def stored_part(j, stage):
        slot = lax.rem(j, 2)

        @pl.when(j >= 2)
        def _():
            out_copy(j - 2).wait()

        if stage > 0:

            @pl.when(j + 1 < count)
            def _():
                in_copy(j + 1).start()

        total = map_part(j, cuts[stage], cuts[stage + 1])
        if stage == last:
            t, place = lax.div(j, tiles), pl.ds(pl.multiple_of(lax.rem(j, tiles) * tile, 128), tile)
            scale = weight[pl.ds(pl.multiple_of(t * rows, 8), rows), 0:1]
            total = total + (scale * cols[0:1, place] - cols[1:2, place])
        if stage > 0:
            in_copy(j).wait()
            total = total + inst[slot]
        if stage == last:
            exponent = e2[t, pl.ds(0, rows), place].astype(F32) + e2[t, pl.ds(rows, rows), place].astype(F32)
            total = exponent * total
        outst[slot] = total
        out_copy(j).start()

    ends = [0] + [group - 1 + 2 * group * p for p in range(1, groups)]
    finishes = [4 + group + 2 * group * p for p in range(groups)]
    if group == 2 and groups == 8:
        finishes = [6, 10, 13, 16, 18, 20, 26, 32]
    makes = [max((p + 1) * group - 1, finishes[p - zslots] + 5 if p >= zslots else 0) for p in range(groups)]
    makes = finishes

    def at(t, of_ends, of_others):
        p = jnp.int32(-1)
        for n in range(groups):
            p = jnp.where(t == jnp.where(at_end, of_ends[n], of_others[n]), n, p)
        return p

    def step(t, _):
        def hops(firsts, seconds):
            for i in firsts:
                first_own(order(i)[2])
            for i in seconds:
                second_own(order(i)[2])

        @pl.when(t == 0)
        def _():
            hops((0, 1), ())
            for i in range(2, ahead + 1):
                announce(i)
            hops((), (0, 1))
            stage_own(order(0)[2], 0)
            stage_own(order(1)[2], 1)

        @pl.when(t == 1)
        def _():
            hops((2, 3), (2,))

        @pl.when(t == 2)
        def _():
            hops((4, 5), (3, 4))

        @pl.when((t >= 3) & (t + 3 < chunks))
        def _():
            first_own(order(t + 3)[2])

        @pl.when((t >= 3) & (t + 2 < chunks))
        def _():
            second_own(order(t + 2)[2])

        @pl.when((t >= 1) & (t + 1 < chunks))
        def _():
            stage_own(order(t + 1)[2], lax.rem(t + 1, 2))

        @pl.when((t >= 1) & (t + ahead < chunks))
        def _():
            announce(t + ahead)

        @pl.when(lax.rem(t, 2) == 0)
        def _():
            far_step(lax.div(t, 2), ask_far)

            @pl.when(t >= 2)
            def _():
                far_step(lax.div(t - 2, 2), first_far)

        @pl.when((t >= 3) & (lax.rem(t, 2) == 1))
        def _():
            far_step(lax.div(t - 3, 2), second_far)

        soon = at(t + 1, [-1] * groups, finishes)

        @pl.when(helper & (soon >= 0))
        def _():
            for n in range(group):
                d, k, _ = order(soon * group + n)
                far_step(rank(d, k), lambda m, n=n: stage_far(m, n))

        @pl.when((t < chunks) & (t != 1))
        def _():
            take_own(lax.rem(t, 2), gph, gpl, t * GK)

        @pl.when(t == 0)
        def _():
            take_own(1, gph, gpl, GK)
            for n in range(parts):
                for copy in e_copy(n):
                    copy.wait()
            lax.fori_loop(0, chunks, load_x, 0)

        p = at(t, ends, makes)

        @pl.when(p >= 0)
        def _():
            multiply_group(p)

        q = at(t, ends, finishes)

        @pl.when(q >= 0)
        def _():
            finish_group(q)

        @pl.when((t == 2) & helper)
        def _():
            far_exponentials()

        @pl.when(t == cuts[1])
        def _():
            pltpu.make_async_copy(xparts, x2, x_sem).wait()
            total = collect(mine, vecr, vec_send, vec_recv, c, cells, in_plane)
            spot_sum = collect(loss, lossr, loss_send, loss_recv, z, planes, in_column)
            weight[...] = jnp.broadcast_to(counts[...].astype(F32)[None, :], (128, C)).T
            cols[0:1, :] = vec[8:9, :]
            cols[1:2, :] = total[0:1, :] + vec[9:10, :]
            losses[...] = jnp.zeros_like(losses)
            losses[0:1, :] = loss[2:3, :] - total[1:2, 0:128] / G - spot_sum[0:1, :] / loss[1:2, :]

        for stage in range(last + 1):
            begin = cuts[stage + 1]
            steps = cuts[stage + 2] - begin if stage < last else count
            each = -(-count // steps)

            @pl.when((t >= begin) & (t < begin + steps))
            def _():
                if stage > 0:

                    @pl.when(t == begin)
                    def _():
                        for j in range(count - 2, count):
                            out_copy(j).wait()
                        in_copy(0).start()

                def one(j, _):
                    stored_part(j, stage)
                    return 0

                lax.fori_loop(
                    jnp.minimum((t - begin) * each, count), jnp.minimum((t - begin + 1) * each, count), one, 0
                )

        return 0

    lax.fori_loop(0, slots, step, 0)

    for p in range(groups - zslots, groups):
        for h in range(2):

            @pl.when(had(p, h))
            def _():
                for n in range(group):
                    sent(p % zslots, n, h)

    for j in range(count - 2, count):
        out_copy(j).wait()

    def drain(g, _):
        n = rank(lax.div(g, per), lax.rem(g, per))
        drain_own(g)

        @pl.when(helper & (n < handed))
        def _():
            drain_far(n)

        @pl.when(at_end & (n < handed))
        def _():
            row_copy(n, g).wait_send()

        return 0

    lax.fori_loop(0, chunks, drain, 0)


def backward(cfg, ehi, elo, xparts, far_logits, vec, loss, counts, gp, spent):
    cells, planes, C, S, G, GK, r = (cfg[k] for k in ("cells", "planes", "C", "S", "G", "GK", "r"))
    chips, per, chunks = cells // 2, G // planes // GK, G // GK
    parts, tile, group, zslots = cfg["parts"], cfg["tile"], cfg["group"], cfg["zslots"]
    rows, handed = C // parts, cfg["handed"]
    sem = pltpu.SemaphoreType.DMA
    scratch = [
        pltpu.VMEM((parts, 2 * rows, S), BF16), pltpu.VMEM((parts, 2 * rows, G), BF16),
        pltpu.VMEM((parts // 2, 2 * rows, S), BF16),
        pltpu.VMEM((G, S), BF16), pltpu.VMEM((G, S), BF16), pltpu.VMEM((2, GK, S), BF16),
        pltpu.VMEM((2, chips, 2, r, S), F32), pltpu.VMEM((group, chips, 2, r, S), F32),
        pltpu.VMEM((2, cfg["piece"], S), F32), pltpu.VMEM((group, 2, C // 2, GK), F32),
        pltpu.VMEM((zslots, group, 2, C // 2, GK), F32), pltpu.VMEM((2, rows, tile), F32), pltpu.VMEM((2, rows, tile), F32),
        pltpu.VMEM((8, S), F32), pltpu.VMEM((cells, 8, S), F32), pltpu.VMEM((planes, 8, 128), F32), pltpu.VMEM((C, 128), F32),
        sem((2, parts)), sem, sem((2,)), sem((chunks, chips)), sem((chunks,)), sem((chunks, 2)),
        sem((handed, chips)), sem((handed,)), sem((handed, 2)),
        sem((handed,)), sem((handed,)), sem((2,)), sem((group,)),
        sem((chunks + per, 2)), sem((zslots, group, 2)), sem((group, 2)), sem((2,)), sem((2,)),
        sem((cells,)), sem((cells,)), sem((planes,)), sem((planes,)),
    ]
    return pl.pallas_call(
        functools.partial(backward_kernel, cfg),
        out_shape=(
            jax.ShapeDtypeStruct((C, S), F32),
            jax.ShapeDtypeStruct((C, G // planes), F32),
            jax.ShapeDtypeStruct((8, 128), F32),
            jax.ShapeDtypeStruct((chunks, chips, 2, r, S), F32),
            jax.ShapeDtypeStruct((cfg["handed"], chips, 2, r, S), F32),
            jax.ShapeDtypeStruct((chunks, C, GK), F32),
            jax.ShapeDtypeStruct((per, C, GK), F32),
        ),
        in_specs=[ANY, ANY, ANY, ANY, VMEM, VMEM, VMEM, ANY, ANY],
        out_specs=(ANY, ANY, VMEM, ANY, ANY, ANY, ANY),
        input_output_aliases={7: 3, 8: 5},
        scratch_shapes=scratch,
        compiler_params=pltpu.CompilerParams(
            collective_id=1, has_side_effects=True, vmem_limit_bytes=61 * 2**20
        ),
        cost_estimate=pl.CostEstimate(flops=12 * C * S * G, bytes_accessed=16 * C * S, transcendentals=0),
        name="backward",
    )(ehi, elo, xparts, far_logits, vec, loss, counts, gp, spent)


def passing_kernel(pieces, losses, first, second, out_losses, out_first, out_second, *rest):
    buffers, (read, write) = rest[:2], rest[2:]
    moves = []
    for n, (source, target) in enumerate(((first, out_first), (second, out_second))):
        rows = source.shape[0] // pieces[n]
        for i in range(pieces[n]):
            place = pl.ds(i * rows, rows)
            slot = len(moves)
            moves.append(
                (
                    pltpu.make_async_copy(source.at[place], buffers[n].at[place], read.at[slot]),
                    pltpu.make_async_copy(buffers[n].at[place], target.at[place], write.at[slot]),
                )
            )
    for load, _ in moves:
        load.start()
    for n in range(2):
        out_losses[n] = losses[0, n]
    for load, store in moves:
        load.wait()
        store.start()
    for _, store in moves:
        store.wait()


def passing(losses, first, second):
    pieces = [8, 2]
    smem = pl.BlockSpec(memory_space=pltpu.SMEM)
    return pl.pallas_call(
        functools.partial(passing_kernel, pieces),
        out_shape=(
            jax.ShapeDtypeStruct((2,), F32),
            jax.ShapeDtypeStruct(first.shape, first.dtype),
            jax.ShapeDtypeStruct(second.shape, second.dtype),
        ),
        in_specs=[smem, ANY, ANY],
        out_specs=(smem, ANY, ANY),
        scratch_shapes=[
            pltpu.VMEM(first.shape, first.dtype), pltpu.VMEM(second.shape, second.dtype),
            pltpu.SemaphoreType.DMA((sum(pieces),)), pltpu.SemaphoreType.DMA((sum(pieces),)),
        ],
        compiler_params=pltpu.CompilerParams(vmem_limit_bytes=60 * 2**20),
        name="passing",
    )(losses, first, second)


def local(cells, planes, logits, expression, spatial, cell_counts, spot_density, slide_id, padding):
    C, S = logits.shape
    G = expression.shape[1] * planes
    GK = max(128, 8 * cells)
    chunks, parts, group = G // GK, 2, 256 // GK
    tile = 128 * group
    across = 1
    while across * across < cells // 2:
        across *= 2
    cfg = dict(
        cells=cells, planes=planes, C=C, S=S, G=G, GK=GK, r=GK // cells, rows=128, tile=tile, parts=parts,
        group=group, zslots=1 + group, slots=max(chunks + parts * (S // tile), 5 + group + 2 * (chunks - group)), pieces=8, ahead=5, handed=chunks // 4,
        across=across, helped=planes >= 4, piece=max(n for n in range(16, 33, 16) if C // parts % n == 0),
    )
    counts = cell_counts
    gath, ehi, elo, xparts, far_logits, gp, vec, loss = forward(
        cfg, logits, expression, spatial, counts, spot_density[None, :],
        slide_id[None, :], padding[None, :],
    )
    grad_logits, grad_expression, losses, *_ = backward(
        cfg, ehi, elo, xparts, far_logits, vec, loss, counts, gp, gath
    )
    return passing(losses, grad_logits, grad_expression)


def solution(mesh):
    cells, planes = mesh.shape["cell"], mesh.shape["spot"]
    in_specs = (
        P("cell", "spot"), P("cell", "spot"), P("cell", "spot"), P("cell"), P("spot"), P("spot"), P("spot"),
    )
    out_specs = (P(), P("cell", "spot"), P("cell", "spot"))
    return jax.shard_map(
        functools.partial(local, cells, planes), mesh=mesh, in_specs=in_specs, out_specs=out_specs, check_vma=False
    )
```
